256 devices in a mesh: section: 4 (over y_hi, core), dp: 64 (over x, y_lo, z).
Axes of the slice: x: 4, y: 4 (y_hi: 2, y_lo: 2; y = y_hi * 2 + y_lo), z: 8, core: 2. Of those that a mesh axis runs over, the one named last changes fastest.
Arguments:
- hidden_in: bfloat16 [2, 4096, 3584], P(None, 'dp'), may hold values from -60 to 60
- head_grad: bfloat16 [2, 4096, 3584], P(None, 'dp'), may hold values from -0.4375 to 0.4375
- down_w: bfloat16 [4, 1, 3584, 256], P('section'), may hold values from -0.09375 to 0.09375
- up_w: bfloat16 [4, 1, 3584, 256], P('section'), may hold values from -0.375 to 0.375
- norm_gain: float32 [4, 1, 3584], P('section'), may hold values from 0.1 to 1.9
- codec: bfloat16 [3584, 512], P('dp'), may hold values from -0.0625 to 0.0625
Outputs:
- grad_down: float32 [4, 1, 3584, 256], P('section', None, 'dp')
- grad_up: float32 [4, 1, 3584, 256], P('section', None, 'dp')
- grad_gain: float32 [4, 1, 3584], P('section', None, 'dp')
The draws below stay inside these ranges and needn't reach their ends.
All inputs are finite; a program needn't handle non-finite values.
Results may differ from the reference program's by a relative error of at most 0.018.
Values may be sent and summed in bfloat16 or wider, within the bound.
A program may use at most 128 MiB of HBM per device.

```python
import math
import jax
import jax.numpy as jnp
from jax import lax

D = 3584
C = 512
K = 256
LAYERS = 1
MB = 2
SECTIONS = 4
ROWS = 4096


def draw_hidden_in(key, part):
    key = jax.random.fold_in(key, 11)
    sub_keys = jax.random.split(key, 3)
    col_scale = jnp.exp(jax.random.uniform(sub_keys[2], (1, 1, D), jnp.float32) * math.log(10.0))
    base_values = jnp.clip(jax.random.normal(sub_keys[0], (MB, ROWS, D), jnp.float32), -6.0, 6.0)
    row_scale = jnp.exp(jax.random.uniform(sub_keys[1], (MB, ROWS, 1), jnp.float32) * math.log(10.0))
    return (base_values * row_scale * col_scale * 0.1).astype(jnp.bfloat16)


def strengthened(result, own_key, source, target, blocks, factor):
    def block_of(axis_at):
        return (jnp.arange(result.shape[axis_at]) // (result.shape[axis_at] // blocks)).reshape((-1,) + (1,) * (result.ndim - 1 - axis_at))

    one_side = jax.random.permutation(own_key, blocks)[block_of(target)]
    second = (block_of(target) + blocks // 2) % blocks
    return jnp.where((block_of(source) == one_side) | (block_of(source) == second), factor * result, result)


def level_of(key, extent, cuts, smallest, high):
    def one(axis_at, parts):
        draws = jax.random.uniform(jax.random.fold_in(jax.random.fold_in(key, 6), axis_at), (parts,), jnp.float32, smallest / len(cuts), high / len(cuts))
        return jnp.repeat(jnp.exp(draws), extent[axis_at] // parts).reshape((-1,) + (1,) * (len(extent) - axis_at - 1))

    loudness = one(*cuts[0])
    for cut in cuts[1:]:
        loudness = loudness * one(*cut)
    return loudness


def bell_draw(rng, shape, width, most, cuts=(), held_as=jnp.bfloat16):
    gain = level_of(rng, shape, cuts, -0.22, 0.18) if cuts else 1.0
    drawn = jax.random.normal(rng, shape, jnp.float32) * width * gain
    return jnp.minimum(jnp.maximum(drawn, -most), most).astype(held_as)


def heavy_noise(own_key, dims, width, limit, cuts, heavy, kind=jnp.bfloat16):
    result = width * jax.random.normal(own_key, dims, jnp.float32)
    if cuts:
        result = result * level_of(own_key, dims, cuts, -0.22, 0.18)
    return jnp.clip(strengthened(result, jax.random.fold_in(own_key, 3), *heavy), -limit, limit).astype(kind)


def setup_inputs(seed: int = 0) -> dict:
    arg_keys = jax.random.split(jax.random.key(seed), 7)
    return {
        "hidden_in": draw_hidden_in(jax.random.fold_in(arg_keys[6], 71), 0),
        "head_grad": heavy_noise(arg_keys[1], (MB, ROWS, D), (1.0 / (MB * ROWS) ** 0.5), 0.4375, ((1, 64),), (1, 2, 64, 4.0)),
        "down_w": bell_draw(arg_keys[2], (SECTIONS, LAYERS, D, K), D ** -0.5, 0.09375, ((0, 4),)),
        "up_w": bell_draw(arg_keys[3], (SECTIONS, LAYERS, D, K), K ** -0.5, 0.375, ((0, 4),)),
        "norm_gain": jnp.clip(1.0 + 0.18 * jax.random.normal(arg_keys[4], (SECTIONS, LAYERS, D), jnp.float32), 0.1, 1.9),
        "codec": bell_draw(arg_keys[5], (D, C), (D * (D / C) ** 0.5) ** -0.5, 0.0625, ((0, 64),)),
    }


epsilon = 1e-06

def right_dot(left_side, right_side):
    return lax.dot_general(left_side, right_side, (((1,), (1,)), ((), ())), preferred_element_type=jnp.float32)

def layer_forward(stream, gains, down_rows, up_rows):
    inverse_rms = lax.rsqrt(lax.optimization_barrier(jnp.mean(stream * stream, axis=-1, keepdims=True)) + epsilon)
    normed = (stream * inverse_rms * gains).astype(jnp.bfloat16)
    latent = jnp.dot(normed, down_rows, preferred_element_type=jnp.float32)
    active = jax.nn.silu(latent).astype(jnp.bfloat16)
    return (stream + right_dot(active, up_rows), inverse_rms, normed, latent, active)

def reference(hidden_in, head_grad, down_w, up_w, norm_gain, codec):
    code_ratio = D / C
    sum_down = [[jnp.zeros((D, K), jnp.float32) for layer_index in range(LAYERS)] for section_index in range(SECTIONS)]
    sum_up = [[jnp.zeros((D, K), jnp.float32) for layer_index in range(LAYERS)] for section_index in range(SECTIONS)]
    sum_gain = [[jnp.zeros((D,), jnp.float32) for layer_index in range(LAYERS)] for section_index in range(SECTIONS)]
    for batch_index in range(MB):
        entries = []
        stream = hidden_in[batch_index].astype(jnp.float32)
        code_rows = None
        for section_index in range(SECTIONS):
            if section_index > 0:
                stream = code_ratio * right_dot(code_rows, codec)
            section_entries = []
            for layer_index in range(LAYERS):
                section_entries.append(stream)
                stream = layer_forward(stream, norm_gain[section_index, layer_index], down_w[section_index, layer_index], up_w[section_index, layer_index])[0]
            entries.append(section_entries)
            if section_index < SECTIONS - 1:
                section_out = stream.astype(jnp.bfloat16)
                code_rows = jnp.dot(section_out, codec, preferred_element_type=jnp.float32).astype(jnp.bfloat16)
        gradient = head_grad[batch_index].astype(jnp.float32)
        back_code = None
        for section_index in reversed(range(SECTIONS)):
            if section_index < SECTIONS - 1:
                gradient = right_dot(back_code, codec)
            for layer_index in reversed(range(LAYERS)):
                gains = norm_gain[section_index, layer_index]
                down_rows = down_w[section_index, layer_index]
                up_rows = up_w[section_index, layer_index]
                stream = entries[section_index][layer_index]
                unused_out, inverse_rms, normed, latent, active = layer_forward(stream, gains, down_rows, up_rows)
                grad_rows = gradient.astype(jnp.bfloat16)
                d_active = jnp.dot(grad_rows, up_rows, preferred_element_type=jnp.float32)
                sigmoid_value = jax.nn.sigmoid(latent)
                d_latent = (d_active * sigmoid_value * (1.0 + latent * (1.0 - sigmoid_value))).astype(jnp.bfloat16)
                d_normed = right_dot(d_latent, down_rows)
                weighted = d_normed * gains
                cube = inverse_rms * inverse_rms * inverse_rms
                gradient = gradient + inverse_rms * weighted - stream * cube * lax.optimization_barrier(jnp.mean(weighted * stream, axis=-1, keepdims=True))
                sum_down[section_index][layer_index] = sum_down[section_index][layer_index] + jnp.dot(normed.T, d_latent, preferred_element_type=jnp.float32)
                sum_up[section_index][layer_index] = sum_up[section_index][layer_index] + jnp.dot(grad_rows.T, active, preferred_element_type=jnp.float32)
                sum_gain[section_index][layer_index] = sum_gain[section_index][layer_index] + lax.optimization_barrier(jnp.sum(d_normed * stream * inverse_rms, axis=0))
            if section_index > 0:
                grad_entry = gradient.astype(jnp.bfloat16)
                back_code = (code_ratio * jnp.dot(grad_entry, codec, preferred_element_type=jnp.float32)).astype(jnp.bfloat16)
    grad_down = jnp.stack([jnp.stack(sum_down[section_index]) for section_index in range(SECTIONS)])
    grad_up = jnp.stack([jnp.stack(sum_up[section_index]) for section_index in range(SECTIONS)])
    grad_gain = jnp.stack([jnp.stack(sum_gain[section_index]) for section_index in range(SECTIONS)])
    return (grad_down, grad_up, grad_gain)
```

```python
import functools

import jax
import jax.numpy as jnp
from jax import lax
from jax.experimental import pallas as pl
from jax.experimental.pallas import tpu as pltpu
from jax.sharding import PartitionSpec as P

epsilon = 1e-06
y_size, z_size = 2, 8
f32, bf16 = jnp.float32, jnp.bfloat16
mesh_ids = pl.DeviceIdType.MESH


def plain_dot(left, right):
    return lax.dot_general(left, right, (((1,), (0,)), ((), ())), preferred_element_type=f32)


def right_dot(left, right):
    return lax.dot_general(left, right, (((1,), (1,)), ((), ())), preferred_element_type=f32)


def left_dot(left, right):
    return lax.dot_general(left, right, (((0,), (0,)), ((), ())), preferred_element_type=f32)


def sigmoid(value):
    return 1.0 / (1.0 + jnp.exp(-value))


def silu_slope(latent):
    gate = sigmoid(latent)
    return gate * (1.0 + latent * (1.0 - gate))


def kernel(
    sizes,
    hidden,
    head,
    down_hbm,
    up_hbm,
    gain,
    codec,
    out_down,
    out_up,
    out_gain,
    tok,
    down,
    up,
    down32,
    gain_col,
    gdown,
    planes,
    flat,
    acc,
    weights,
    tok_code,
    latent_ref,
    active_ref,
    inv_ref,
    slope_ref,
    code_grid,
    code_in,
    code_out,
    back_in,
    back_out,
    wide_in,
    factor,
    factor_in,
    big,
    y_send,
    y_in,
    z_send,
    z_in,
    part,
    sum_a_send,
    sum_a_in,
    sum_z_send,
    sum_z_in,
    sum_g,
    local_sem,
    send_sem,
    recv_sem,
):
    X, Y, Z = sizes
    micro, rows, D = hidden.shape
    R = micro * rows
    C, K = codec.shape[1], down.shape[1]
    own = codec.shape[0]
    lanes = C // 4
    chunk = D // X
    ratio = D / C
    sec = lax.axis_index("section")
    dp = lax.axis_index("dp")
    core = lax.rem(sec, 2)
    x = dp // (Y * Z)
    y = lax.rem(dp // Z, Y)
    z = lax.rem(dp, Z)
    xy = dp // Z
    other_y = 1 - y
    far_sec = lax.rem(sec + 2, 4)
    sibling = sec + 1 - 2 * core
    ends = jnp.logical_or(sec == 0, sec == 3)
    middle = jnp.logical_not(ends)

    def place(px, py, pz):
        return (px * Y + py) * Z + pz

    def ring(mine, count):
        return [lax.rem(mine + off, count) for off in range(1, count)]

    names = [
        ("x0", X), ("z0", Z), ("y0", 2), ("z1", Z), ("y1", 2), ("x1", X), ("d0", 2), ("d1", X),
        ("code", 1), ("back", 1), ("wide", X), ("factor", X), ("big_y", 1), ("big_z", Z),
        ("sum_a", X * Y), ("sum_z", Z), ("sum_g", X * Y),
    ]
    base, total = {}, 0
    for name, count in names:
        base[name] = total
        total += count
    sent = [0]

    def start(src, dst, name, index, section, place_at, slot=None):
        if slot is None:
            slot = sent[0]
            sent[0] += 1
        copy = pltpu.make_async_remote_copy(
            src_ref=src, dst_ref=dst, send_sem=send_sem.at[slot],
            recv_sem=recv_sem.at[base[name] + index],
            device_id=(section, place_at), device_id_type=mesh_ids,
        )
        copy.start()
        return copy

    def left(src, slot):
        pltpu.make_async_remote_copy(
            src_ref=src, dst_ref=src, send_sem=send_sem.at[slot], recv_sem=recv_sem.at[0],
            device_id=(sec, dp), device_id_type=mesh_ids,
        ).wait_send()

    def arrive(dst, name, index):
        pltpu.make_async_remote_copy(
            src_ref=dst, dst_ref=dst, send_sem=send_sem.at[0],
            recv_sem=recv_sem.at[base[name] + index],
            device_id=(sec, dp), device_id_type=mesh_ids,
        ).wait_recv()

    load_down = pltpu.make_async_copy(down_hbm, down, local_sem.at[0])
    load_up = pltpu.make_async_copy(up_hbm, up, local_sem.at[1])
    load_hidden = pltpu.make_async_copy(hidden, tok, local_sem.at[2])
    load_head = pltpu.make_async_copy(head, tok, local_sem.at[2])
    load_down.start()
    load_up.start()
    pl.when(sec == 0)(load_hidden.start)
    pl.when(sec == 3)(load_head.start)

    color0, color1 = 2 * core, 2 * core + 1

    @pl.when(core == 0)
    def _():
        planes[0, x, y, z] = codec[:, 0:lanes]
        planes[1, x, y, z] = codec[:, lanes : 2 * lanes]

    @pl.when(core == 1)
    def _():
        planes[2, x, y, z] = codec[:, 2 * lanes : 3 * lanes]
        planes[3, x, y, z] = codec[:, 3 * lanes :]

    barrier = pltpu.get_barrier_semaphore()
    peers = [(sec, place(x, y, pz)) for pz in ring(z, Z)]
    xy_ring = ring(xy, X * Y)
    peers += [(sec, pxy * Z + z) for pxy in xy_ring]
    peers += [(sibling, dp), (far_sec, place(x, other_y, z)), (3 - sec, dp)]
    for peer in peers:
        pl.semaphore_signal(barrier, inc=1, device_id=peer, device_id_type=mesh_ids)
    pl.semaphore_wait(barrier, len(peers))

    half_x, half_z = X // 2, Z // 2
    copies = []
    mine = planes.at[color0, x, y, z]
    for px in ring(x, X):
        copies.append(start(mine, mine, "x0", x, sec, place(px, y, z)))
    mine = planes.at[color1, x, y, z]
    for pz in ring(z, Z):
        copies.append(start(mine, mine, "z1", z, sec, place(x, y, pz)))

    load_down.wait()
    step = 128

    def scale_rows(index, carry):
        at = pl.ds(pl.multiple_of(index * step, step), step)
        column = jnp.broadcast_to(gain[:, at], (step, step)).T
        gain_col[at, :] = column
        wide = down[at, :].astype(f32)
        down32[at, :] = wide
        parts = [wide[:, k : k + step] * column[:, : min(step, K)] for k in range(0, K, step)]
        gdown[at, :] = jnp.concatenate(parts, axis=1).astype(bf16)
        return carry

    for px in ring(x, X):
        arrive(planes.at[color0, px, y, z], "x0", px)
    line = planes.at[color0, :, y, z]
    for pz in ring(z, Z):
        copies.append(start(line, line, "z0", z, sec, place(x, y, pz)))

    lax.fori_loop(0, D // step, scale_rows, 0)

    for pz in ring(z, Z):
        arrive(planes.at[color1, x, y, pz], "z1", pz)
    near, far = planes.at[color1, x, y, 0:half_z], planes.at[color1, x, y, half_z:Z]
    copies.append(start(near, near, "y1", 0, sec, place(x, other_y, z)))
    copies.append(start(far, far, "y1", 1, far_sec, place(x, other_y, z)))

    load_up.wait()

    @pl.when(sec == 0)
    def _():
        load_hidden.wait()

        def squares(index, carry):
            at = pl.ds(pl.multiple_of(index * chunk, chunk), chunk)
            value = tok[:, :, at].reshape(R, chunk).astype(f32)
            return carry + jnp.sum(value * value, axis=-1, keepdims=True)

        square = lax.fori_loop(0, X, squares, jnp.zeros((R, 1), f32))
        inverse = lax.rsqrt(square / D + epsilon)
        inv_ref[...] = inverse

        def project(index, carry):
            at = pl.ds(pl.multiple_of(index * chunk, chunk), chunk)
            value = tok[:, :, at].reshape(R, chunk).astype(f32)
            normed = (value * inverse * gain[:, at]).astype(bf16)
            return carry + plain_dot(normed, down[at, :])

        latent = lax.fori_loop(0, X, project, jnp.zeros((R, K), f32))
        active_ref[...] = (latent * sigmoid(latent)).astype(bf16)
        slope_ref[...] = silu_slope(latent)

    @pl.when(sec == 3)
    def _():
        load_head.wait()

        def project(index, carry):
            at = pl.ds(pl.multiple_of(index * chunk, chunk), chunk)
            return carry + plain_dot(tok[:, :, at].reshape(R, chunk), up[at, :])

        latent_ref[...] = lax.fori_loop(0, X, project, jnp.zeros((R, K), f32))

    for pz in ring(z, Z):
        arrive(planes.at[color0, :, y, pz], "z0", pz)
    near, far = planes.at[color0, 0:half_x, y], planes.at[color0, half_x:X, y]
    copies.append(start(near, near, "y0", 0, sec, place(x, other_y, z)))
    copies.append(start(far, far, "y0", 1, far_sec, place(x, other_y, z)))
    half = planes.at[color0, :, y]
    copies.append(start(half, half, "d0", 0, sibling, dp))

    arrive(planes.at[color1, x, other_y, 0:half_z], "y1", 0)
    arrive(planes.at[color1, x, other_y, half_z:Z], "y1", 1)
    slab = planes.at[color1, x]
    for px in ring(x, X):
        copies.append(start(slab, slab, "x1", x, sec, place(px, y, z)))
    copies.append(start(slab, slab, "d1", x, sibling, dp))

    arrive(planes.at[color0, 0:half_x, other_y], "y0", 0)
    arrive(planes.at[color0, half_x:X, other_y], "y0", 1)
    half = planes.at[color0, :, other_y]
    copies.append(start(half, half, "d0", 1, sibling, dp))
    for px in ring(x, X):
        slab = planes.at[color1, px]
        arrive(slab, "x1", px)
        copies.append(start(slab, slab, "d1", px, sibling, dp))

    their0, their1 = 2 - 2 * core, 3 - 2 * core
    arrive(planes.at[their0, :, y], "d0", 0)
    arrive(planes.at[their0, :, other_y], "d0", 1)
    arrive(planes.at[their1, x], "d1", x)
    for px in ring(x, X):
        arrive(planes.at[their1, px], "d1", px)

    wide_slot = sent[0]
    sent[0] += X - 1

    @pl.when(ends)
    def _():
        for off, px in enumerate(ring(x, X)):
            at = pl.ds(pl.multiple_of(px * chunk, chunk), chunk)
            start(
                tok.at[:, :, at], wide_in.at[x], "wide", x, sec, place(px, y, z), wide_slot + off
            )

    acc[...] = jnp.zeros_like(acc)

    @pl.when(ends)
    def _():
        tok_code[...] = jnp.zeros_like(tok_code)

    def products(index, carry):
        at = pl.ds(pl.multiple_of(index * chunk, chunk), chunk)
        for color in range(4):
            piece = planes[color, index].astype(f32).reshape(chunk, lanes).astype(bf16)
            flat[:, color * lanes : (color + 1) * lanes] = piece
        block = flat[...]

        @pl.when(sec != 3)
        def _():
            acc[:, K + C :] += left_dot(block, up[at, :])

        @pl.when(sec != 0)
        def _():
            acc[:, 0:K] += left_dot(block, gdown[at, :])
            acc[:, K : K + C] += left_dot(block, block)

        @pl.when(ends)
        def _():
            tok_code[...] += plain_dot(tok[:, :, at].reshape(R, chunk), block)

        return carry

    lax.fori_loop(0, X, products, 0)
    weights[...] = acc[...].astype(bf16)

    def forward():
        code = code_in[...]
        both = plain_dot(code, weights[:, 0 : K + C])
        grid = both[:, K:]
        square = jnp.sum(code.astype(f32) * grid, axis=-1, keepdims=True) * (ratio * ratio / D)
        inverse = lax.rsqrt(square + epsilon)
        latent = ratio * inverse * both[:, 0:K]
        active = (latent * sigmoid(latent)).astype(bf16)
        return code, grid, inverse, latent, active

    def backward(inner, grid, inverse, latent, d_latent):
        weight = jnp.sum(d_latent.astype(f32) * latent, axis=-1, keepdims=True)
        weight = weight * inverse * inverse * (ratio / D)
        through = right_dot(d_latent, weights[:, 0:K])
        return (ratio * (inner + inverse * through - weight * grid)).astype(bf16)

    hops = []

    @pl.when(sec == 0)
    def _():
        result = tok_code[...] + right_dot(active_ref[...], weights[:, K + C :])
        code_out[...] = result.astype(bf16)
        start(code_out, code_in, "code", 0, 1, dp).wait_send()

    @pl.when(middle)
    def _():
        arrive(code_in, "code", 0)
        code, grid, inverse, latent, active = forward()
        result = ratio * grid + right_dot(active, weights[:, K + C :])
        code_out[...] = result.astype(bf16)
        hop = start(code_out, code_in, "code", 0, sec + 1, dp)
        code_grid[...] = grid
        inv_ref[...] = inverse
        latent_ref[...] = latent
        active_ref[...] = active
        slope_ref[...] = silu_slope(latent)
        hop.wait_send()

    def send_factor():
        result = []
        for px in ring(x, X):
            result.append(start(factor, factor_in.at[x], "factor", x, sec, place(px, y, z)))
        return result

    @pl.when(sec == 3)
    def _():
        arrive(code_in, "code", 0)
        code, grid, inverse, latent, active = forward()
        factor[...] = active
        d_latent = (latent_ref[...] * silu_slope(latent)).astype(bf16)
        back_out[...] = backward(tok_code[...], grid, inverse, latent, d_latent)
        hop = start(back_out, back_in, "back", 0, 2, dp)
        scaled = (d_latent.astype(f32) * (ratio * inverse)).astype(bf16)
        part[:, 0:K] = left_dot(code, scaled)
        hop.wait_send()

    @pl.when(middle)
    def _():
        arrive(back_in, "back", 0)
        back = back_in[...]
        both = plain_dot(back, weights[:, K:])
        inverse = inv_ref[...]
        d_latent = (both[:, C:] * slope_ref[...]).astype(bf16)
        back_out[...] = backward(both[:, 0:C], code_grid[...], inverse, latent_ref[...], d_latent)
        hop = start(back_out, back_in, "back", 0, sec - 1, dp)
        scaled = (d_latent.astype(f32) * (ratio * inverse)).astype(bf16)
        part[:, 0:K] = left_dot(code_in[...], scaled)
        part[:, K:] = left_dot(back, active_ref[...])
        hop.wait_send()

    @pl.when(sec == 0)
    def _():
        arrive(back_in, "back", 0)
        back = back_in[...]
        d_latent = (plain_dot(back, weights[:, K + C :]) * slope_ref[...]).astype(bf16)
        factor[...] = (d_latent.astype(f32) * inv_ref[...]).astype(bf16)
        part[:, 0:K] = left_dot(back, active_ref[...])

    block_rows = C // (X * Y)

    def sum_scatter(width):
        sum_a_send[:, :, 0:width] = part[:, 0:width].astype(bf16).reshape(X * Y, block_rows, width)
        result = []
        for pxy in xy_ring:
            result.append(
                start(sum_a_send.at[pxy, :, 0:width], sum_a_in.at[xy, :, 0:width], "sum_a", xy, sec, pxy * Z + z)
            )
        return result

    def sum_line(width):
        value = sum_a_send[xy, :, 0:width].astype(f32)
        for pxy in xy_ring:
            arrive(sum_a_in.at[pxy, :, 0:width], "sum_a", pxy)
            value = value + sum_a_in[pxy, :, 0:width].astype(f32)
        sum_z_send[:, 0:width] = value.astype(bf16)
        result = []
        for pz in ring(z, Z):
            result.append(
                start(sum_z_send.at[:, 0:width], sum_z_in.at[z, :, 0:width], "sum_z", z, sec, place(x, y, pz))
            )
        return result, value

    def sum_gather(width, value):
        for pz in ring(z, Z):
            arrive(sum_z_in.at[pz, :, 0:width], "sum_z", pz)
            value = value + sum_z_in[pz, :, 0:width].astype(f32)
        sum_g[xy, :, 0:width] = value.astype(bf16)
        result = []
        mine = sum_g.at[xy, :, 0:width]
        for pxy in xy_ring:
            result.append(start(mine, mine, "sum_g", xy, sec, pxy * Z + z))
        return result

    def sum_end(width):
        for pxy in xy_ring:
            arrive(sum_g.at[pxy, :, 0:width], "sum_g", pxy)
        return sum_g[:, :, 0:width].reshape(C, width)

    own_rows = pl.ds(pl.multiple_of(dp * own, 8), own)

    def put_down(value):
        column = gain_col[own_rows, :]
        weighted = down32[own_rows, :] * value
        folded = weighted[:, 0 : min(step, K)]
        for k in range(step, K, step):
            folded = folded + weighted[:, k : k + step]
        if own < step:
            folded = jnp.concatenate([folded, jnp.zeros((step - own, folded.shape[1]), f32)], axis=0)
        out_gain[...] = jnp.sum(folded.T, axis=0, keepdims=True)[:, 0:own]
        for k in range(0, K, step):
            out_down[:, k : k + step] = value[:, k : k + step] * column[:, : min(step, K)]

    @pl.when(middle)
    def _():
        waits = sum_scatter(2 * K)
        more, value = sum_line(2 * K)
        waits += more
        waits += sum_gather(2 * K, value)
        result = plain_dot(codec[...], sum_end(2 * K))
        put_down(result[:, 0:K])
        out_up[...] = result[:, K:]
        for copy in waits:
            copy.wait_send()

    @pl.when(ends)
    def _():
        waits = send_factor()
        waits += sum_scatter(K)
        at = pl.ds(pl.multiple_of(x * chunk, chunk), chunk)
        big[...] = left_dot(tok[:, :, at].reshape(R, chunk), factor[...])
        for px in ring(x, X):
            arrive(wide_in.at[px], "wide", px)
            arrive(factor_in.at[px], "factor", px)
            big[...] += left_dot(wide_in[px].reshape(R, chunk), factor_in[px])
        y_rows = chunk // Y
        their_rows = pl.ds(pl.multiple_of(other_y * y_rows, 8), y_rows)
        my_rows = pl.ds(pl.multiple_of(y * y_rows, 8), y_rows)
        y_send[...] = big[their_rows, :].astype(bf16)
        waits.append(start(y_send, y_in, "big_y", 0, sec, place(x, other_y, z)))
        more, value = sum_line(K)
        waits += more
        arrive(y_in, "big_y", 0)
        line_sum = (big[my_rows, :] + y_in[...].astype(f32)).reshape(Z, own, K)
        z_send[...] = line_sum.astype(bf16)
        for pz in ring(z, Z):
            waits.append(start(z_send.at[pz], z_in.at[z], "big_z", z, sec, place(x, y, pz)))
        waits += sum_gather(K, value)
        wide_sum = z_send[z].astype(f32)
        for pz in ring(z, Z):
            arrive(z_in.at[pz], "big_z", pz)
            wide_sum = wide_sum + z_in[pz].astype(f32)
        result = plain_dot(codec[...], sum_end(K))

        @pl.when(sec == 0)
        def _():
            put_down(wide_sum)
            out_up[...] = result

        @pl.when(sec == 3)
        def _():
            put_down(result)
            out_up[...] = wide_sum

        for copy in waits:
            copy.wait_send()
        for off in range(X - 1):
            left(wide_in.at[x], wide_slot + off)

    for copy in copies:
        copy.wait_send()


def on_device(hidden_in, head_grad, down_w, up_w, norm_gain, codec):
    micro, rows, D = hidden_in.shape
    K, C, own = down_w.shape[3], codec.shape[1], codec.shape[0]
    Y, Z = y_size, z_size
    X = lax.axis_size("dp") // (Y * Z)
    R, chunk, lanes = micro * rows, D // X, C // 4
    block_rows = C // (X * Y)
    any_space = pl.BlockSpec(memory_space=pl.ANY)
    vmem = pl.BlockSpec(memory_space=pltpu.VMEM)
    recv_count = 4 * X + 4 * Z + 10 + 2 * X * Y + 8
    scratch = [
        ((micro, rows, D), bf16),
        ((D, K), bf16),
        ((D, K), bf16),
        ((D, K), f32),
        ((D, 128), f32),
        ((D, K), bf16),
        ((4, X, Y, Z, own, lanes), bf16),
        ((chunk, C), bf16),
        ((C, 2 * K + C), f32),
        ((C, 2 * K + C), bf16),
        ((R, C), f32),
        ((R, K), f32),
        ((R, K), bf16),
        ((R, 1), f32),
        ((R, K), f32),
        ((R, C), f32),
        ((R, C), bf16),
        ((R, C), bf16),
        ((R, C), bf16),
        ((R, C), bf16),
        ((X, micro, rows, chunk), bf16),
        ((R, K), bf16),
        ((X, R, K), bf16),
        ((chunk, K), f32),
        ((chunk // Y, K), bf16),
        ((chunk // Y, K), bf16),
        ((Z, own, K), bf16),
        ((Z, own, K), bf16),
        ((C, 2 * K), f32),
        ((X * Y, block_rows, 2 * K), bf16),
        ((X * Y, block_rows, 2 * K), bf16),
        ((block_rows, 2 * K), bf16),
        ((Z, block_rows, 2 * K), bf16),
        ((X * Y, block_rows, 2 * K), bf16),
    ]
    sum_down, sum_up, sum_gain = pl.pallas_call(
        functools.partial(kernel, (X, Y, Z)),
        out_shape=(
            jax.ShapeDtypeStruct((own, K), f32),
            jax.ShapeDtypeStruct((own, K), f32),
            jax.ShapeDtypeStruct((1, own), f32),
        ),
        in_specs=[any_space] * 4 + [vmem] * 2,
        out_specs=(vmem, vmem, vmem),
        scratch_shapes=[pltpu.VMEM(shape, kind) for shape, kind in scratch]
        + [
            pltpu.SemaphoreType.DMA((3,)),
            pltpu.SemaphoreType.DMA((160,)),
            pltpu.SemaphoreType.DMA((recv_count,)),
        ],
        compiler_params=pltpu.CompilerParams(
            collective_id=0, has_side_effects=True, vmem_limit_bytes=56 * 1024 * 1024
        ),
    )(hidden_in, head_grad, down_w[0, 0], up_w[0, 0], norm_gain[0], codec)
    return (sum_down[None, None], sum_up[None, None], sum_gain[None])


def solution(mesh):
    in_specs = (
        P(None, "dp", None),
        P(None, "dp", None),
        P("section", None, None, None),
        P("section", None, None, None),
        P("section", None, None),
        P("dp", None),
    )
    out_specs = (
        P("section", None, "dp", None),
        P("section", None, "dp", None),
        P("section", None, "dp"),
    )
    return jax.shard_map(
        on_device, mesh=mesh, in_specs=in_specs, out_specs=out_specs, check_vma=False
    )
```

```python
import functools

import jax
import jax.numpy as jnp
from jax import lax
from jax.experimental import pallas as pl
from jax.experimental.pallas import tpu as pltpu
from jax.sharding import PartitionSpec as P

epsilon = 1e-06
y_size, z_size = 2, 8
f32, bf16 = jnp.float32, jnp.bfloat16
mesh_ids = pl.DeviceIdType.MESH


def plain_dot(left, right):
    return lax.dot_general(left, right, (((1,), (0,)), ((), ())), preferred_element_type=f32)


def right_dot(left, right):
    return lax.dot_general(left, right, (((1,), (1,)), ((), ())), preferred_element_type=f32)


def left_dot(left, right):
    return lax.dot_general(left, right, (((0,), (0,)), ((), ())), preferred_element_type=f32)


def sigmoid(value):
    return 1.0 / (1.0 + jnp.exp(-value))


def silu_slope(latent):
    gate = sigmoid(latent)
    return gate * (1.0 + latent * (1.0 - gate))


def kernel(
    sizes,
    hidden,
    head,
    down_hbm,
    up_hbm,
    gain,
    codec,
    out_down,
    out_up,
    out_gain,
    tok,
    down,
    up,
    down32,
    gain_col,
    gdown,
    planes,
    flat,
    tok_half,
    acc,
    weights,
    tok_code,
    latent_ref,
    active_ref,
    inv_ref,
    slope_ref,
    code_grid,
    code_in,
    code_out,
    back_in,
    back_out,
    active_in,
    wide_in,
    factor,
    factor_in,
    wide_part,
    wide_parts,
    wide_sum,
    down_part,
    down_in,
    down_block,
    down_blocks,
    down_sum,
    up_part,
    up_parts,
    up_line,
    up_lines,
    up_sum,
    up_result,
    up_results,
    local_sem,
    send_sem,
    recv_sem,
):
    X, Y, Z = sizes
    micro, rows, D = hidden.shape
    R = micro * rows
    C, K = codec.shape[1], down.shape[1]
    own = codec.shape[0]
    lanes = C // 4
    chunk = D // X
    ratio = D / C
    sec = lax.axis_index("section")
    dp = lax.axis_index("dp")
    core = lax.rem(sec, 2)
    x = dp // (Y * Z)
    y = lax.rem(dp // Z, Y)
    z = lax.rem(dp, Z)
    xy = dp // Z
    other_y = 1 - y
    far_sec = lax.rem(sec + 2, 4)
    sibling = sec + 1 - 2 * core
    ends = jnp.logical_or(sec == 0, sec == 3)
    middle = jnp.logical_not(ends)

    def place(px, py, pz):
        return (px * Y + py) * Z + pz

    def ring(mine, count):
        return [lax.rem(mine + off, count) for off in range(1, count)]

    def near_first(mine, count):
        offsets = sorted(range(1, count), key=lambda off: (min(off, count - off), off))
        return [lax.rem(mine + off, count) for off in offsets]

    names = [
        ("x0", X), ("z0", Z), ("y0", Z), ("z1", Z), ("y1", 2), ("x1a", X), ("x1b", X),
        ("d0", 2), ("d1a", X), ("d1b", X), ("code", 1), ("back", 1), ("active", 1), ("up", 1),
        ("wide", X * Y), ("factor", X * Y), ("big", Z), ("down_a", Z), ("down_b", X * Y),
        ("down_c", Z), ("up_a", X * Y), ("up_b", Z), ("up_c", X * Y),
    ]
    base, total = {}, 0
    for name, count in names:
        base[name] = total
        total += count
    sent = [0]

    def start(src, dst, name, index, section, place_at, slot=None):
        if slot is None:
            slot = sent[0]
            sent[0] += 1
        copy = pltpu.make_async_remote_copy(
            src_ref=src, dst_ref=dst, send_sem=send_sem.at[slot],
            recv_sem=recv_sem.at[base[name] + index],
            device_id=(section, place_at), device_id_type=mesh_ids,
        )
        copy.start()
        return copy

    def left(src, slot):
        pltpu.make_async_remote_copy(
            src_ref=src, dst_ref=src, send_sem=send_sem.at[slot], recv_sem=recv_sem.at[0],
            device_id=(sec, dp), device_id_type=mesh_ids,
        ).wait_send()

    def arrive(dst, name, index):
        pltpu.make_async_remote_copy(
            src_ref=dst, dst_ref=dst, send_sem=send_sem.at[0],
            recv_sem=recv_sem.at[base[name] + index],
            device_id=(sec, dp), device_id_type=mesh_ids,
        ).wait_recv()

    load_down = pltpu.make_async_copy(down_hbm, down, local_sem.at[0])
    load_up = pltpu.make_async_copy(up_hbm, up, local_sem.at[1])
    load_hidden = pltpu.make_async_copy(hidden, tok, local_sem.at[2])
    load_head = pltpu.make_async_copy(head, tok, local_sem.at[2])
    load_down.start()
    load_up.start()
    pl.when(sec == 0)(load_hidden.start)
    pl.when(sec == 3)(load_head.start)

    color0, color1 = 2 * core, 2 * core + 1

    @pl.when(core == 0)
    def _():
        planes[0, x, y, z] = codec[:, 0:lanes]
        planes[1, x, y, z] = codec[:, lanes : 2 * lanes]

    @pl.when(core == 1)
    def _():
        planes[2, x, y, z] = codec[:, 2 * lanes : 3 * lanes]
        planes[3, x, y, z] = codec[:, 3 * lanes :]

    barrier = pltpu.get_barrier_semaphore()
    peers = [(sec, place(x, y, pz)) for pz in ring(z, Z)]
    xy_ring = ring(xy, X * Y)
    peers += [(sec, pxy * Z + z) for pxy in xy_ring]
    peers += [(sibling, dp), (far_sec, place(x, other_y, z)), (3 - sec, dp)]
    for peer in peers:
        pl.semaphore_signal(barrier, inc=1, device_id=peer, device_id_type=mesh_ids)
    pl.semaphore_wait(barrier, len(peers))

    half_z = Z // 2
    copies = []
    mine = planes.at[color0, x, y, z]
    for px in ring(x, X):
        copies.append(start(mine, mine, "x0", x, sec, place(px, y, z)))
    mine = planes.at[color1, x, y, z]
    for pz in near_first(z, Z):
        copies.append(start(mine, mine, "z1", z, sec, place(x, y, pz)))

    y_part = chunk // Y

    @pl.when(sec == 0)
    def _():
        load_hidden.wait()

    @pl.when(sec == 3)
    def _():
        load_head.wait()

    @pl.when(ends)
    def _():
        def split(index, carry):
            at = pl.ds(pl.multiple_of(index * chunk, chunk), chunk)
            value = tok[:, :, at].reshape(R, chunk)
            for py in range(Y):
                tok_half[py, index] = value[:, py * y_part : (py + 1) * y_part]
            return carry

        lax.fori_loop(0, X, split, 0)

    for px in ring(x, X):
        arrive(planes.at[color0, px, y, z], "x0", px)

    def line(pz):
        return planes.at[color0, :, y, pz]

    def pass_y(index, pz):
        block = line(pz)
        section = sec if index % 2 == 0 else far_sec
        copies.append(start(block, block, "y0", pz, section, place(x, other_y, z)))

    for pz in near_first(z, Z):
        copies.append(start(line(z), line(z), "z0", z, sec, place(x, y, pz)))
    pass_y(0, z)

    load_down.wait()
    load_up.wait()

    @pl.when(sec == 0)
    def _():
        def squares(index, carry):
            at = pl.ds(pl.multiple_of(index * chunk, chunk), chunk)
            value = tok[:, :, at].reshape(R, chunk).astype(f32)
            return carry + jnp.sum(value * value, axis=-1, keepdims=True)

        square = lax.fori_loop(0, X, squares, jnp.zeros((R, 1), f32))
        inverse = lax.rsqrt(square / D + epsilon)
        inv_ref[...] = inverse

        def project(index, carry):
            at = pl.ds(pl.multiple_of(index * chunk, chunk), chunk)
            value = tok[:, :, at].reshape(R, chunk).astype(f32)
            normed = (value * inverse * gain[:, at]).astype(bf16)
            return carry + plain_dot(normed, down[at, :])

        latent = lax.fori_loop(0, X, project, jnp.zeros((R, K), f32))
        active_ref[...] = (latent * sigmoid(latent)).astype(bf16)
        slope_ref[...] = silu_slope(latent)

    @pl.when(sec == 3)
    def _():
        def project(index, carry):
            at = pl.ds(pl.multiple_of(index * chunk, chunk), chunk)
            return carry + plain_dot(tok[:, :, at].reshape(R, chunk), up[at, :])

        latent_ref[...] = lax.fori_loop(0, X, project, jnp.zeros((R, K), f32))

    for pz in ring(z, Z):
        arrive(planes.at[color1, x, y, pz], "z1", pz)
    near, far = planes.at[color1, x, y, 0:half_z], planes.at[color1, x, y, half_z:Z]
    copies.append(start(near, near, "y1", 0, sec, place(x, other_y, z)))
    copies.append(start(far, far, "y1", 1, far_sec, place(x, other_y, z)))
    slab = planes.at[color1, x, y]
    for px in ring(x, X):
        copies.append(start(slab, slab, "x1a", x, sec, place(px, y, z)))
    copies.append(start(slab, slab, "d1a", x, sibling, dp))

    step = 128

    def scale_rows(index, carry):
        at = pl.ds(pl.multiple_of(index * step, step), step)
        column = jnp.broadcast_to(gain[:, at], (step, step)).T
        gain_col[at, :] = column
        wide = down[at, :].astype(f32)
        down32[at, :] = wide
        parts = [wide[:, k : k + step] * column[:, : min(step, K)] for k in range(0, K, step)]
        gdown[at, :] = jnp.concatenate(parts, axis=1).astype(bf16)
        return carry

    def scale():
        lax.fori_loop(0, D // step, scale_rows, 0)

    pl.when(sec != 0)(scale)

    order = near_first(z, Z)
    for index, pz in enumerate(order):
        if index == 2:
            arrive(planes.at[color1, x, other_y, 0:half_z], "y1", 0)
            arrive(planes.at[color1, x, other_y, half_z:Z], "y1", 1)
            slab = planes.at[color1, x, other_y]
            for px in ring(x, X):
                copies.append(start(slab, slab, "x1b", x, sec, place(px, y, z)))
            copies.append(start(slab, slab, "d1b", x, sibling, dp))
        arrive(line(pz), "z0", pz)
        pass_y(index + 1, pz)
    half = planes.at[color0, :, y]
    copies.append(start(half, half, "d0", 0, sibling, dp))
    for px in ring(x, X):
        slab = planes.at[color1, px, y]
        arrive(slab, "x1a", px)
        copies.append(start(slab, slab, "d1a", px, sibling, dp))

    their0, their1 = 2 - 2 * core, 3 - 2 * core
    acc[...] = jnp.zeros_like(acc)

    @pl.when(ends)
    def _():
        tok_code[...] = jnp.zeros_like(tok_code)

    def products(py):
        def body(index, carry):
            at = pl.ds(pl.multiple_of(index * chunk + py * y_part, y_part), y_part)
            for color in range(4):
                piece = planes[color, index, py].astype(f32).reshape(y_part, lanes).astype(bf16)
                flat[:, color * lanes : (color + 1) * lanes] = piece
            block = flat[...]

            @pl.when(sec != 3)
            def _():
                acc[:, K + C :] += left_dot(block, up[at, :])

            @pl.when(sec != 0)
            def _():
                acc[:, 0:K] += left_dot(block, gdown[at, :])
                acc[:, K : K + C] += left_dot(block, block)

            @pl.when(ends)
            def _():
                tok_code[...] += plain_dot(tok_half[py, index], block)

            return carry

        lax.fori_loop(0, X, body, 0)

    arrive(planes.at[their0, :, y], "d0", 0)
    arrive(planes.at[their1, x, y], "d1a", x)
    for px in ring(x, X):
        arrive(planes.at[their1, px, y], "d1a", px)
    products(y)

    for index, pz in enumerate([z] + order):
        arrive(planes.at[color0, :, other_y, pz], "y0", pz)
    half = planes.at[color0, :, other_y]
    copies.append(start(half, half, "d0", 1, sibling, dp))
    for px in ring(x, X):
        slab = planes.at[color1, px, other_y]
        arrive(slab, "x1b", px)
        copies.append(start(slab, slab, "d1b", px, sibling, dp))

    arrive(planes.at[their0, :, other_y], "d0", 1)
    arrive(planes.at[their1, x, other_y], "d1b", x)
    for px in ring(x, X):
        arrive(planes.at[their1, px, other_y], "d1b", px)

    wide_slot = sent[0]
    sent[0] += X * Y - 1

    @pl.when(ends)
    def _():
        for off, pxy in enumerate(xy_ring):
            start(
                tok_half.at[lax.rem(pxy, Y), pxy // Y], wide_in.at[xy], "wide", xy, sec,
                pxy * Z + z, wide_slot + off,
            )

    products(other_y)
    weights[...] = acc[...].astype(bf16)

    def forward():
        code = code_in[...]
        both = plain_dot(code, weights[:, 0 : K + C])
        grid = both[:, K:]
        square = jnp.sum(code.astype(f32) * grid, axis=-1, keepdims=True) * (ratio * ratio / D)
        inverse = lax.rsqrt(square + epsilon)
        latent = ratio * inverse * both[:, 0:K]
        active = (latent * sigmoid(latent)).astype(bf16)
        return code, grid, inverse, latent, active

    def backward(inner, grid, inverse, latent, d_latent):
        weight = jnp.sum(d_latent.astype(f32) * latent, axis=-1, keepdims=True)
        weight = weight * inverse * inverse * (ratio / D)
        through = right_dot(d_latent, weights[:, 0:K])
        return (ratio * (inner + inverse * through - weight * grid)).astype(bf16)

    def hop_active():
        return start(active_ref, active_in, "active", 0, sec + 1, dp)

    @pl.when(sec == 0)
    def _():
        result = tok_code[...] + right_dot(active_ref[...], weights[:, K + C :])
        code_out[...] = result.astype(bf16)
        hop = start(code_out, code_in, "code", 0, 1, dp)
        more = hop_active()
        hop.wait_send()
        more.wait_send()

    @pl.when(middle)
    def _():
        arrive(code_in, "code", 0)
        code, grid, inverse, latent, active = forward()
        result = ratio * grid + right_dot(active, weights[:, K + C :])
        code_out[...] = result.astype(bf16)
        hop = start(code_out, code_in, "code", 0, sec + 1, dp)
        active_ref[...] = active
        more = hop_active()
        code_grid[...] = grid
        inv_ref[...] = inverse
        latent_ref[...] = latent
        slope_ref[...] = silu_slope(latent)
        hop.wait_send()
        more.wait_send()

    def code_sums(code, inverse, d_latent):
        scaled = (d_latent.astype(f32) * (ratio * inverse)).astype(bf16)
        down_part[...] = left_dot(code, scaled).astype(bf16).reshape(down_part.shape)

    @pl.when(sec == 3)
    def _():
        arrive(code_in, "code", 0)
        code, grid, inverse, latent, active = forward()
        factor[...] = active
        d_latent = (latent_ref[...] * silu_slope(latent)).astype(bf16)
        back_out[...] = backward(tok_code[...], grid, inverse, latent, d_latent)
        hop = start(back_out, back_in, "back", 0, 2, dp)
        code_sums(code, inverse, d_latent)
        hop.wait_send()

    @pl.when(middle)
    def _():
        arrive(back_in, "back", 0)
        both = plain_dot(back_in[...], weights[:, K:])
        inverse = inv_ref[...]
        d_latent = (both[:, C:] * slope_ref[...]).astype(bf16)
        back_out[...] = backward(both[:, 0:C], code_grid[...], inverse, latent_ref[...], d_latent)
        hop = start(back_out, back_in, "back", 0, sec - 1, dp)
        code_sums(code_in[...], inverse, d_latent)
        hop.wait_send()

    @pl.when(sec == 0)
    def _():
        scale()
        arrive(back_in, "back", 0)
        d_latent = (plain_dot(back_in[...], weights[:, K + C :]) * slope_ref[...]).astype(bf16)
        factor[...] = (d_latent.astype(f32) * inv_ref[...]).astype(bf16)

    XY = X * Y
    xy_peers = [(pxy, pxy * Z + z) for pxy in xy_ring]
    z_peers = [(pz, place(x, y, pz)) for pz in near_first(z, Z)]
    pending_rest, pending_ends = [], []

    def spread(ref_of, landings, name, mine, peers, pending):
        for peer, peer_dp in peers:
            slot = sent[0]
            start(ref_of(peer), landings.at[mine], name, mine, sec, peer_dp)
            pending.append((landings, slot))

    def gathered(first, landing, name, peers):
        value = first.astype(f32)
        for peer, _ in peers:
            arrive(landing.at[peer], name, peer)
            value = value + landing[peer].astype(f32)
        return value

    rest = sec != 0

    @pl.when(rest)
    def _():
        spread(lambda peer: down_part.at[peer], down_in, "down_a", z, z_peers, pending_rest)
        arrive(active_in, "active", 0)
        up_part[...] = left_dot(back_out[...], active_in[...]).astype(bf16).reshape(up_part.shape)
        spread(lambda peer: up_part.at[peer], up_parts, "up_a", xy, xy_peers, pending_rest)

    @pl.when(ends)
    def _():
        spread(lambda peer: factor, factor_in, "factor", xy, xy_peers, pending_ends)

    @pl.when(rest)
    def _():
        up_line[...] = gathered(up_part[xy], up_parts, "up_a", xy_peers).astype(bf16)
        spread(lambda peer: up_line, up_lines, "up_b", z, z_peers, pending_rest)

    @pl.when(ends)
    def _():
        value = left_dot(tok_half[y, x], factor[...])
        for pxy, _ in xy_peers:
            arrive(wide_in.at[pxy], "wide", pxy)
            arrive(factor_in.at[pxy], "factor", pxy)
            value = value + left_dot(wide_in[pxy], factor_in[pxy])
        wide_part[...] = value.reshape(Z, own, K).astype(bf16)
        spread(lambda peer: wide_part.at[peer], wide_parts, "big", z, z_peers, pending_ends)

    @pl.when(rest)
    def _():
        down_block[...] = gathered(down_part[z], down_in, "down_a", z_peers).astype(bf16)
        spread(lambda peer: down_block, down_blocks, "down_b", xy, xy_peers, pending_rest)
        up_sum[xy] = gathered(up_line[...], up_lines, "up_b", z_peers).astype(bf16)
        spread(lambda peer: up_sum.at[xy], up_sum, "up_c", xy, xy_peers, pending_rest)
        down_sum[z] = gathered(down_block[...], down_blocks, "down_b", xy_peers).astype(bf16)
        spread(lambda peer: down_sum.at[z], down_sum, "down_c", z, z_peers, pending_rest)
        for pxy, _ in xy_peers:
            arrive(up_sum.at[pxy], "up_c", pxy)
        up_result[...] = plain_dot(codec[...], up_sum[...].reshape(C, K))
        hop = start(up_result, up_results, "up", 0, sec - 1, dp)
        hop.wait_send()

    own_rows = pl.ds(pl.multiple_of(dp * own, 8), own)

    def put_down(value):
        column = gain_col[own_rows, :]
        weighted = down32[own_rows, :] * value
        folded = weighted[:, 0 : min(step, K)]
        for k in range(step, K, step):
            folded = folded + weighted[:, k : k + step]
        if own < step:
            folded = jnp.concatenate([folded, jnp.zeros((step - own, folded.shape[1]), f32)], axis=0)
        out_gain[...] = jnp.sum(folded.T, axis=0, keepdims=True)[:, 0:own]
        for k in range(0, K, step):
            out_down[:, k : k + step] = value[:, k : k + step] * column[:, : min(step, K)]

    @pl.when(ends)
    def _():
        wide_sum[...] = gathered(wide_part[z], wide_parts, "big", z_peers)

    @pl.when(rest)
    def _():
        for pz, _ in z_peers:
            arrive(down_sum.at[pz], "down_c", pz)
        put_down(plain_dot(codec[...], down_sum[...].reshape(C, K)))

    @pl.when(sec == 0)
    def _():
        put_down(wide_sum[...])

    @pl.when(sec == 3)
    def _():
        out_up[...] = wide_sum[...]

    @pl.when(sec != 3)
    def _():
        arrive(up_results, "up", 0)
        out_up[...] = up_results[...]

    @pl.when(rest)
    def _():
        for landing, slot in pending_rest:
            left(landing.at[0], slot)

    @pl.when(ends)
    def _():
        for landing, slot in pending_ends:
            left(landing.at[0], slot)
        for off in range(XY - 1):
            left(wide_in.at[0], wide_slot + off)

    for copy in copies:
        copy.wait_send()


def hand_out(down, up, gain, out_down, out_up, out_gain):
    out_down[...] = down[...]
    out_up[...] = up[...]
    out_gain[...] = gain[...]


def on_device(hidden_in, head_grad, down_w, up_w, norm_gain, codec):
    micro, rows, D = hidden_in.shape
    K, C, own = down_w.shape[3], codec.shape[1], codec.shape[0]
    Y, Z = y_size, z_size
    X = lax.axis_size("dp") // (Y * Z)
    R, chunk, lanes = micro * rows, D // X, C // 4
    block_rows = C // (X * Y)
    any_space = pl.BlockSpec(memory_space=pl.ANY)
    vmem = pl.BlockSpec(memory_space=pltpu.VMEM)
    recv_count = 5 * X + 7 * Z + 8 + 5 * X * Y
    scratch = [
        ((micro, rows, D), bf16),
        ((D, K), bf16),
        ((D, K), bf16),
        ((D, K), f32),
        ((D, 128), f32),
        ((D, K), bf16),
        ((4, X, Y, Z, own, lanes), bf16),
        ((chunk // Y, C), bf16),
        ((Y, X, R, chunk // Y), bf16),
        ((C, 2 * K + C), f32),
        ((C, 2 * K + C), bf16),
        ((R, C), f32),
        ((R, K), f32),
        ((R, K), bf16),
        ((R, 1), f32),
        ((R, K), f32),
        ((R, C), f32),
        ((R, C), bf16),
        ((R, C), bf16),
        ((R, C), bf16),
        ((R, C), bf16),
        ((R, K), bf16),
        ((X * Y, R, chunk // Y), bf16),
        ((R, K), bf16),
        ((X * Y, R, K), bf16),
        ((Z, own, K), bf16),
        ((Z, own, K), bf16),
        ((own, K), f32),
        ((Z, C // Z, K), bf16),
        ((Z, C // Z, K), bf16),
        ((C // Z, K), bf16),
        ((X * Y, C // Z, K), bf16),
        ((Z, C // Z, K), bf16),
        ((X * Y, block_rows, K), bf16),
        ((X * Y, block_rows, K), bf16),
        ((block_rows, K), bf16),
        ((Z, block_rows, K), bf16),
        ((X * Y, block_rows, K), bf16),
        ((own, K), f32),
        ((own, K), f32),
    ]
    sum_down, sum_up, sum_gain = pl.pallas_call(
        functools.partial(kernel, (X, Y, Z)),
        out_shape=(
            jax.ShapeDtypeStruct((own, K), f32),
            jax.ShapeDtypeStruct((own, K), f32),
            jax.ShapeDtypeStruct((1, own), f32),
        ),
        in_specs=[any_space] * 4 + [vmem] * 2,
        out_specs=(vmem, vmem, vmem),
        scratch_shapes=[pltpu.VMEM(shape, kind) for shape, kind in scratch]
        + [
            pltpu.SemaphoreType.DMA((3,)),
            pltpu.SemaphoreType.DMA((160,)),
            pltpu.SemaphoreType.DMA((recv_count,)),
        ],
        compiler_params=pltpu.CompilerParams(
            collective_id=0, has_side_effects=True, vmem_limit_bytes=56 * 1024 * 1024
        ),
    )(hidden_in, head_grad, down_w[0, 0], up_w[0, 0], norm_gain[0], codec)
    sum_down, sum_up, sum_gain = pl.pallas_call(
        hand_out,
        out_shape=(
            jax.ShapeDtypeStruct((own, K), f32),
            jax.ShapeDtypeStruct((own, K), f32),
            jax.ShapeDtypeStruct((1, own), f32),
        ),
        in_specs=[vmem] * 3,
        out_specs=(vmem, vmem, vmem),
    )(sum_down, sum_up, sum_gain)
    return (sum_down[None, None], sum_up[None, None], sum_gain[None])


def solution(mesh):
    in_specs = (
        P(None, "dp", None),
        P(None, "dp", None),
        P("section", None, None, None),
        P("section", None, None, None),
        P("section", None, None),
        P("dp", None),
    )
    out_specs = (
        P("section", None, "dp", None),
        P("section", None, "dp", None),
        P("section", None, "dp"),
    )
    return jax.shard_map(
        on_device, mesh=mesh, in_specs=in_specs, out_specs=out_specs, check_vma=False
    )
```

```python
import functools

import jax
import jax.numpy as jnp
from jax import lax
from jax.experimental import pallas as pl
from jax.experimental.pallas import tpu as pltpu
from jax.sharding import PartitionSpec as P

epsilon = 1e-06
y_size, z_size = 2, 8
f32, bf16 = jnp.float32, jnp.bfloat16
mesh_ids = pl.DeviceIdType.MESH


def plain_dot(left, right):
    return lax.dot_general(left, right, (((1,), (0,)), ((), ())), preferred_element_type=f32)


def right_dot(left, right):
    return lax.dot_general(left, right, (((1,), (1,)), ((), ())), preferred_element_type=f32)


def left_dot(left, right):
    return lax.dot_general(left, right, (((0,), (0,)), ((), ())), preferred_element_type=f32)


def sigmoid(value):
    return 1.0 / (1.0 + jnp.exp(-value))


def silu_slope(latent):
    gate = sigmoid(latent)
    return gate * (1.0 + latent * (1.0 - gate))


def kernel(
    sizes,
    hidden,
    head,
    down_hbm,
    up_hbm,
    gain_hbm,
    codec_hbm,
    out_down,
    out_up,
    out_gain,
    tok,
    gain,
    codec,
    down,
    up_half,
    down32,
    gain_col,
    gdown_half,
    planes,
    flat,
    tok_half,
    acc,
    weights,
    tok_code,
    latent_ref,
    active_ref,
    inv_ref,
    slope_ref,
    code_grid,
    code_in,
    code_out,
    back_in,
    back_out,
    active_in,
    wide_in,
    factor,
    factor_in,
    wide_part,
    wide_parts,
    wide_sum,
    down_part,
    down_in,
    down_block,
    down_blocks,
    down_sum,
    up_part,
    up_parts,
    up_line,
    up_lines,
    up_sum,
    up_result,
    up_results,
    local_sem,
    send_sem,
    recv_sem,
):
    X, Y, Z = sizes
    micro, rows, D = hidden.shape
    R = micro * rows
    C, K = codec.shape[1], down.shape[1]
    own = codec.shape[0]
    y_part = D // (X * Y)
    lanes = C // 4
    chunk = D // X
    ratio = D / C
    sec = lax.axis_index("section")
    dp = lax.axis_index("dp")
    core = lax.rem(sec, 2)
    x = dp // (Y * Z)
    y = lax.rem(dp // Z, Y)
    z = lax.rem(dp, Z)
    xy = dp // Z
    other_y = 1 - y
    far_sec = lax.rem(sec + 2, 4)
    sibling = sec + 1 - 2 * core
    ends = jnp.logical_or(sec == 0, sec == 3)
    middle = jnp.logical_not(ends)

    def place(px, py, pz):
        return (px * Y + py) * Z + pz

    def ring(mine, count):
        return [lax.rem(mine + off, count) for off in range(1, count)]

    def near_first(mine, count):
        offsets = sorted(range(1, count), key=lambda off: (min(off, count - off), off))
        return [lax.rem(mine + off, count) for off in offsets]

    names = [
        ("x0", X), ("z0", Z), ("y0", Z), ("z1", Z), ("y1", 2), ("x1a", X), ("x1b", X),
        ("d0", 2), ("d1a", X), ("d1b", X), ("code", 1), ("back", 1), ("active", 1), ("up", 1),
        ("wide", X * Y), ("factor", X * Y), ("big", Z), ("down_a", Z), ("down_b", X * Y),
        ("down_c", Z), ("up_a", X * Y), ("up_b", Z), ("up_c", X * Y),
    ]
    base, total = {}, 0
    for name, count in names:
        base[name] = total
        total += count
    sent = [0]

    def start(src, dst, name, index, section, place_at, slot=None):
        if slot is None:
            slot = sent[0]
            sent[0] += 1
        copy = pltpu.make_async_remote_copy(
            src_ref=src, dst_ref=dst, send_sem=send_sem.at[slot],
            recv_sem=recv_sem.at[base[name] + index],
            device_id=(section, place_at), device_id_type=mesh_ids,
        )
        copy.start()
        return copy

    def left(src, slot):
        pltpu.make_async_remote_copy(
            src_ref=src, dst_ref=src, send_sem=send_sem.at[slot], recv_sem=recv_sem.at[0],
            device_id=(sec, dp), device_id_type=mesh_ids,
        ).wait_send()

    def arrive(dst, name, index):
        pltpu.make_async_remote_copy(
            src_ref=dst, dst_ref=dst, send_sem=send_sem.at[0],
            recv_sem=recv_sem.at[base[name] + index],
            device_id=(sec, dp), device_id_type=mesh_ids,
        ).wait_recv()

    barrier = pltpu.get_barrier_semaphore()
    peers = [(sec, place(x, y, pz)) for pz in ring(z, Z)]
    xy_ring = ring(xy, X * Y)
    peers += [(sec, pxy * Z + z) for pxy in xy_ring]
    peers += [(sibling, dp), (far_sec, place(x, other_y, z)), (3 - sec, dp)]
    for peer in peers:
        pl.semaphore_signal(barrier, inc=1, device_id=peer, device_id_type=mesh_ids)

    color0, color1 = 2 * core, 2 * core + 1
    loads = []

    def load(src, dst):
        copy = pltpu.make_async_copy(src, dst, local_sem.at[len(loads)])
        loads.append(copy)
        copy.start()
        return copy

    own_loads = []
    for color in (color0, color1):
        columns = pl.ds(pl.multiple_of(color * lanes, lanes), lanes)
        own_loads.append(load(codec_hbm.at[:, columns], planes.at[color, x, y, z]))
    load_tok = pltpu.make_async_copy(hidden, tok, local_sem.at[20])
    pl.when(sec == 0)(load_tok.start)
    pl.when(sec == 3)(pltpu.make_async_copy(head, tok, local_sem.at[20]).start)
    load_down = load(down_hbm, down)
    load_ups = [
        load(
            up_hbm.at[pl.ds(index * chunk + py * y_part, y_part)],
            up_half.at[py, pl.ds(index * y_part, y_part)],
        )
        for py in range(Y)
        for index in range(X)
    ]
    load_gain = load(gain_hbm, gain)
    load_codec = load(codec_hbm, codec)

    pl.semaphore_wait(barrier, len(peers))
    for copy in own_loads:
        copy.wait()

    half_z = Z // 2
    copies = []
    mine = planes.at[color0, x, y, z]
    for px in ring(x, X):
        copies.append(start(mine, mine, "x0", x, sec, place(px, y, z)))
    mine = planes.at[color1, x, y, z]
    for pz in near_first(z, Z):
        copies.append(start(mine, mine, "z1", z, sec, place(x, y, pz)))

    wide_slot = sent[0]
    sent[0] += X * Y - 1

    @pl.when(ends)
    def _():
        load_tok.wait()

        def split(index, carry):
            at = pl.ds(pl.multiple_of(index * chunk, chunk), chunk)
            value = tok[:, :, at].reshape(R, chunk)
            for py in range(Y):
                tok_half[py, index] = value[:, py * y_part : (py + 1) * y_part]
            return carry

        lax.fori_loop(0, X, split, 0)
        for off, pxy in enumerate(xy_ring):
            start(
                tok_half.at[lax.rem(pxy, Y), pxy // Y], wide_in.at[xy], "wide", xy, sec,
                pxy * Z + z, wide_slot + off,
            )

    for px in ring(x, X):
        arrive(planes.at[color0, px, y, z], "x0", px)

    def line(pz):
        return planes.at[color0, :, y, pz]

    def pass_y(index, pz):
        block = line(pz)
        section = sec if index % 2 == 0 else far_sec
        copies.append(start(block, block, "y0", pz, section, place(x, other_y, z)))

    for pz in near_first(z, Z):
        copies.append(start(line(z), line(z), "z0", z, sec, place(x, y, pz)))
    pass_y(0, z)

    load_down.wait()
    load_gain.wait()
    for copy in load_ups:
        copy.wait()

    @pl.when(sec == 0)
    def _():
        def squares(index, carry):
            at = pl.ds(pl.multiple_of(index * chunk, chunk), chunk)
            value = tok[:, :, at].reshape(R, chunk).astype(f32)
            return carry + jnp.sum(value * value, axis=-1, keepdims=True)

        square = lax.fori_loop(0, X, squares, jnp.zeros((R, 1), f32))
        inverse = lax.rsqrt(square / D + epsilon)
        inv_ref[...] = inverse

        def project(index, carry):
            at = pl.ds(pl.multiple_of(index * chunk, chunk), chunk)
            value = tok[:, :, at].reshape(R, chunk).astype(f32)
            normed = (value * inverse * gain[:, at]).astype(bf16)
            return carry + plain_dot(normed, down[at, :])

        latent = lax.fori_loop(0, X, project, jnp.zeros((R, K), f32))
        active_ref[...] = (latent * sigmoid(latent)).astype(bf16)
        slope_ref[...] = silu_slope(latent)

    @pl.when(sec == 3)
    def _():
        value = jnp.zeros((R, K), f32)
        for py in range(Y):
            for index in range(X):
                rows_at = pl.ds(index * y_part, y_part)
                value = value + plain_dot(tok_half[py, index], up_half[py, rows_at, :])
        latent_ref[...] = value

    for pz in ring(z, Z):
        arrive(planes.at[color1, x, y, pz], "z1", pz)
    near, far = planes.at[color1, x, y, 0:half_z], planes.at[color1, x, y, half_z:Z]
    copies.append(start(near, near, "y1", 0, sec, place(x, other_y, z)))
    copies.append(start(far, far, "y1", 1, far_sec, place(x, other_y, z)))
    slab = planes.at[color1, x, y]
    for px in ring(x, X):
        copies.append(start(slab, slab, "x1a", x, sec, place(px, y, z)))
    copies.append(start(slab, slab, "d1a", x, sibling, dp))

    step = 128

    def scale_rows(index, carry):
        at = pl.ds(pl.multiple_of(index * chunk, chunk), chunk)
        column = jnp.broadcast_to(gain[:, at], (step, chunk)).T
        gain_col[at, :] = column
        wide = down[at, :].astype(f32)
        down32[at, :] = wide
        parts = [wide[:, k : k + step] * column[:, : min(step, K)] for k in range(0, K, step)]
        scaled = jnp.concatenate(parts, axis=1).astype(bf16)
        rows_at = pl.ds(pl.multiple_of(index * y_part, y_part), y_part)
        for py in range(Y):
            gdown_half[py, rows_at, :] = scaled[py * y_part : (py + 1) * y_part]
        return carry

    def scale():
        lax.fori_loop(0, X, scale_rows, 0)

    pl.when(sec != 0)(scale)

    order = near_first(z, Z)
    for index, pz in enumerate(order):
        if index == 2:
            arrive(planes.at[color1, x, other_y, 0:half_z], "y1", 0)
            arrive(planes.at[color1, x, other_y, half_z:Z], "y1", 1)
            slab = planes.at[color1, x, other_y]
            for px in ring(x, X):
                copies.append(start(slab, slab, "x1b", x, sec, place(px, y, z)))
            copies.append(start(slab, slab, "d1b", x, sibling, dp))
        arrive(line(pz), "z0", pz)
        pass_y(index + 1, pz)
    half = planes.at[color0, :, y]
    copies.append(start(half, half, "d0", 0, sibling, dp))
    for px in ring(x, X):
        slab = planes.at[color1, px, y]
        arrive(slab, "x1a", px)
        copies.append(start(slab, slab, "d1a", px, sibling, dp))

    their0, their1 = 2 - 2 * core, 3 - 2 * core
    def products(py, add):
        for index in range(X):
            for color in range(4):
                piece = planes[color, index, py].astype(f32).reshape(y_part, lanes).astype(bf16)
                rows_at = slice(index * y_part, (index + 1) * y_part)
                flat[rows_at, color * lanes : (color + 1) * lanes] = piece

        @pl.when(sec != 3)
        def _():
            add(acc, slice(K + C, K + C + K), left_dot(flat[...], up_half[py]))

        @pl.when(ends)
        def _():
            value = jnp.zeros((R, C), f32)
            for index in range(X):
                rows_at = slice(index * y_part, (index + 1) * y_part)
                value = value + plain_dot(tok_half[py, index], flat[rows_at, :])
            add(tok_code, slice(0, C), value)

        @pl.when(sec != 0)
        def _():
            add(acc, slice(0, K), left_dot(flat[...], gdown_half[py]))
            add(acc, slice(K, K + C), left_dot(flat[...], flat[...]))

    def put(ref, columns, value):
        ref[:, columns] = value

    def add_to(ref, columns, value):
        ref[:, columns] += value

    arrive(planes.at[their0, :, y], "d0", 0)
    arrive(planes.at[their1, x, y], "d1a", x)
    for px in ring(x, X):
        arrive(planes.at[their1, px, y], "d1a", px)
    products(y, put)

    for index, pz in enumerate([z] + order):
        arrive(planes.at[color0, :, other_y, pz], "y0", pz)
    half = planes.at[color0, :, other_y]
    copies.append(start(half, half, "d0", 1, sibling, dp))
    for px in ring(x, X):
        slab = planes.at[color1, px, other_y]
        arrive(slab, "x1b", px)
        copies.append(start(slab, slab, "d1b", px, sibling, dp))

    arrive(planes.at[their0, :, other_y], "d0", 1)
    arrive(planes.at[their1, x, other_y], "d1b", x)
    for px in ring(x, X):
        arrive(planes.at[their1, px, other_y], "d1b", px)

    products(other_y, add_to)

    @pl.when(sec != 3)
    def _():
        weights[:, K + C :] = acc[:, K + C :].astype(bf16)

    @pl.when(sec != 0)
    def _():
        weights[:, 0 : K + C] = acc[:, 0 : K + C].astype(bf16)

    def forward():
        code = code_in[...]
        both = plain_dot(code, weights[:, 0 : K + C])
        grid = both[:, K:]
        square = jnp.sum(code.astype(f32) * grid, axis=-1, keepdims=True) * (ratio * ratio / D)
        inverse = lax.rsqrt(square + epsilon)
        latent = ratio * inverse * both[:, 0:K]
        active = (latent * sigmoid(latent)).astype(bf16)
        return code, grid, inverse, latent, active

    def backward(inner, grid, inverse, latent, d_latent):
        weight = jnp.sum(d_latent.astype(f32) * latent, axis=-1, keepdims=True)
        weight = weight * inverse * inverse * (ratio / D)
        through = right_dot(d_latent, weights[:, 0:K])
        return (ratio * (inner + inverse * through - weight * grid)).astype(bf16)

    late = []

    def hop(group, src, dst, name, section):
        late.append((group, src, sent[0]))
        start(src, dst, name, 0, section, dp)

    @pl.when(sec == 0)
    def _():
        result = tok_code[...] + right_dot(active_ref[...], weights[:, K + C :])
        code_out[...] = result.astype(bf16)
        hop("first", code_out, code_in, "code", 1)
        hop("first", active_ref, active_in, "active", 1)

    @pl.when(middle)
    def _():
        arrive(code_in, "code", 0)
        code, grid, inverse, latent, active = forward()
        result = ratio * grid + right_dot(active, weights[:, K + C :])
        code_out[...] = result.astype(bf16)
        hop("middle", code_out, code_in, "code", sec + 1)
        active_ref[...] = active
        hop("middle", active_ref, active_in, "active", sec + 1)
        code_grid[...] = grid
        inv_ref[...] = inverse
        latent_ref[...] = latent
        slope_ref[...] = silu_slope(latent)

    def code_sums(code, inverse, d_latent):
        scaled = (d_latent.astype(f32) * (ratio * inverse)).astype(bf16)
        down_part[...] = left_dot(code, scaled).astype(bf16).reshape(down_part.shape)

    @pl.when(sec == 3)
    def _():
        arrive(code_in, "code", 0)
        code, grid, inverse, latent, active = forward()
        factor[...] = active
        d_latent = (latent_ref[...] * silu_slope(latent)).astype(bf16)
        back_out[...] = backward(tok_code[...], grid, inverse, latent, d_latent)
        hop("last", back_out, back_in, "back", 2)
        code_sums(code, inverse, d_latent)

    @pl.when(middle)
    def _():
        arrive(back_in, "back", 0)
        both = plain_dot(back_in[...], weights[:, K:])
        inverse = inv_ref[...]
        d_latent = (both[:, C:] * slope_ref[...]).astype(bf16)
        back_out[...] = backward(both[:, 0:C], code_grid[...], inverse, latent_ref[...], d_latent)
        hop("middle", back_out, back_in, "back", sec - 1)
        code_sums(code_in[...], inverse, d_latent)

    @pl.when(sec == 0)
    def _():
        scale()
        arrive(back_in, "back", 0)
        d_latent = (plain_dot(back_in[...], weights[:, K + C :]) * slope_ref[...]).astype(bf16)
        factor[...] = (d_latent.astype(f32) * inv_ref[...]).astype(bf16)

    XY = X * Y
    xy_peers = [(pxy, pxy * Z + z) for pxy in xy_ring]
    z_peers = [(pz, place(x, y, pz)) for pz in near_first(z, Z)]
    pending_rest, pending_ends = [], []

    def spread(ref_of, landings, name, mine, peers, pending):
        for peer, peer_dp in peers:
            slot = sent[0]
            start(ref_of(peer), landings.at[mine], name, mine, sec, peer_dp)
            pending.append((landings, slot))

    def gathered(first, landing, name, peers):
        value = first.astype(f32)
        for peer, _ in peers:
            arrive(landing.at[peer], name, peer)
            value = value + landing[peer].astype(f32)
        return value

    rest = sec != 0
    load_codec.wait()

    @pl.when(rest)
    def _():
        spread(lambda peer: down_part.at[peer], down_in, "down_a", z, z_peers, pending_rest)
        arrive(active_in, "active", 0)
        up_part[...] = left_dot(back_out[...], active_in[...]).astype(bf16).reshape(up_part.shape)
        spread(lambda peer: up_part.at[peer], up_parts, "up_a", xy, xy_peers, pending_rest)

    @pl.when(ends)
    def _():
        spread(lambda peer: factor, factor_in, "factor", xy, xy_peers, pending_ends)

    @pl.when(rest)
    def _():
        up_line[...] = gathered(up_part[xy], up_parts, "up_a", xy_peers).astype(bf16)
        spread(lambda peer: up_line, up_lines, "up_b", z, z_peers, pending_rest)

    @pl.when(ends)
    def _():
        value = left_dot(tok_half[y, x], factor[...])
        for pxy, _ in xy_peers:
            arrive(wide_in.at[pxy], "wide", pxy)
            arrive(factor_in.at[pxy], "factor", pxy)
            value = value + left_dot(wide_in[pxy], factor_in[pxy])
        wide_part[...] = value.reshape(Z, own, K).astype(bf16)
        spread(lambda peer: wide_part.at[peer], wide_parts, "big", z, z_peers, pending_ends)

    @pl.when(rest)
    def _():
        down_block[...] = gathered(down_part[z], down_in, "down_a", z_peers).astype(bf16)
        spread(lambda peer: down_block, down_blocks, "down_b", xy, xy_peers, pending_rest)
        up_sum[xy] = gathered(up_line[...], up_lines, "up_b", z_peers).astype(bf16)
        spread(lambda peer: up_sum.at[xy], up_sum, "up_c", xy, xy_peers, pending_rest)
        down_sum[z] = gathered(down_block[...], down_blocks, "down_b", xy_peers).astype(bf16)
        spread(lambda peer: down_sum.at[z], down_sum, "down_c", z, z_peers, pending_rest)
        for pxy, _ in xy_peers:
            arrive(up_sum.at[pxy], "up_c", pxy)
        up_result[...] = plain_dot(codec[...], up_sum[...].reshape(C, K))
        hop("rest", up_result, up_results, "up", sec - 1)

    own_rows = pl.ds(pl.multiple_of(dp * own, 8), own)

    def put_down(value):
        column = gain_col[own_rows, :]
        weighted = down32[own_rows, :] * value
        folded = weighted[:, 0 : min(step, K)]
        for k in range(step, K, step):
            folded = folded + weighted[:, k : k + step]
        if own < step:
            folded = jnp.concatenate([folded, jnp.zeros((step - own, folded.shape[1]), f32)], axis=0)
        out_gain[...] = jnp.sum(folded.T, axis=0, keepdims=True)[:, 0:own]
        for k in range(0, K, step):
            out_down[:, k : k + step] = value[:, k : k + step] * column[:, : min(step, K)]

    @pl.when(ends)
    def _():
        wide_sum[...] = gathered(wide_part[z], wide_parts, "big", z_peers)

    @pl.when(rest)
    def _():
        for pz, _ in z_peers:
            arrive(down_sum.at[pz], "down_c", pz)
        put_down(plain_dot(codec[...], down_sum[...].reshape(C, K)))

    @pl.when(sec == 0)
    def _():
        put_down(wide_sum[...])

    @pl.when(sec == 3)
    def _():
        out_up[...] = wide_sum[...]

    @pl.when(sec != 3)
    def _():
        arrive(up_results, "up", 0)
        out_up[...] = up_results[...]

    @pl.when(rest)
    def _():
        for landing, slot in pending_rest:
            left(landing.at[0], slot)

    @pl.when(ends)
    def _():
        for landing, slot in pending_ends:
            left(landing.at[0], slot)
        for off in range(XY - 1):
            left(wide_in.at[0], wide_slot + off)

    for group, chosen in (("first", sec == 0), ("middle", middle), ("last", sec == 3), ("rest", rest)):
        @pl.when(chosen)
        def _():
            for which, src, slot in late:
                if which == group:
                    left(src, slot)

    for copy in copies:
        copy.wait_send()


def hand_out(down, up, gain, out_down, out_up, out_gain, sem):
    copies = [
        pltpu.make_async_copy(down, out_down, sem.at[0]),
        pltpu.make_async_copy(up, out_up, sem.at[1]),
        pltpu.make_async_copy(gain, out_gain, sem.at[2]),
    ]
    for copy in copies:
        copy.start()
    for copy in copies:
        copy.wait()


def on_device(hidden_in, head_grad, down_w, up_w, norm_gain, codec):
    micro, rows, D = hidden_in.shape
    K, C, own = down_w.shape[3], codec.shape[1], codec.shape[0]
    Y, Z = y_size, z_size
    X = lax.axis_size("dp") // (Y * Z)
    R, chunk, lanes = micro * rows, D // X, C // 4
    block_rows = C // (X * Y)
    any_space = pl.BlockSpec(memory_space=pl.ANY)
    vmem = pl.BlockSpec(memory_space=pltpu.VMEM)
    recv_count = 5 * X + 7 * Z + 8 + 5 * X * Y
    scratch = [
        ((micro, rows, D), bf16),
        ((1, D), f32),
        ((own, C), bf16),
        ((D, K), bf16),
        ((Y, D // Y, K), bf16),
        ((D, K), f32),
        ((D, 128), f32),
        ((Y, D // Y, K), bf16),
        ((4, X, Y, Z, own, lanes), bf16),
        ((D // Y, C), bf16),
        ((Y, X, R, chunk // Y), bf16),
        ((C, 2 * K + C), f32),
        ((C, 2 * K + C), bf16),
        ((R, C), f32),
        ((R, K), f32),
        ((R, K), bf16),
        ((R, 1), f32),
        ((R, K), f32),
        ((R, C), f32),
        ((R, C), bf16),
        ((R, C), bf16),
        ((R, C), bf16),
        ((R, C), bf16),
        ((R, K), bf16),
        ((X * Y, R, chunk // Y), bf16),
        ((R, K), bf16),
        ((X * Y, R, K), bf16),
        ((Z, own, K), bf16),
        ((Z, own, K), bf16),
        ((own, K), f32),
        ((Z, C // Z, K), bf16),
        ((Z, C // Z, K), bf16),
        ((C // Z, K), bf16),
        ((X * Y, C // Z, K), bf16),
        ((Z, C // Z, K), bf16),
        ((X * Y, block_rows, K), bf16),
        ((X * Y, block_rows, K), bf16),
        ((block_rows, K), bf16),
        ((Z, block_rows, K), bf16),
        ((X * Y, block_rows, K), bf16),
        ((own, K), f32),
        ((own, K), f32),
    ]
    sum_down, sum_up, sum_gain = pl.pallas_call(
        functools.partial(kernel, (X, Y, Z)),
        out_shape=(
            jax.ShapeDtypeStruct((own, K), f32),
            jax.ShapeDtypeStruct((own, K), f32),
            jax.ShapeDtypeStruct((1, own), f32),
        ),
        in_specs=[any_space] * 6,
        out_specs=(vmem, vmem, vmem),
        scratch_shapes=[pltpu.VMEM(shape, kind) for shape, kind in scratch]
        + [
            pltpu.SemaphoreType.DMA((21,)),
            pltpu.SemaphoreType.DMA((160,)),
            pltpu.SemaphoreType.DMA((recv_count,)),
        ],
        compiler_params=pltpu.CompilerParams(
            collective_id=0, has_side_effects=True, vmem_limit_bytes=56 * 1024 * 1024
        ),
    )(hidden_in, head_grad, down_w[0, 0], up_w[0, 0], norm_gain[0], codec)
    sum_down, sum_up, sum_gain = pl.pallas_call(
        hand_out,
        out_shape=(
            jax.ShapeDtypeStruct((own, K), f32),
            jax.ShapeDtypeStruct((own, K), f32),
            jax.ShapeDtypeStruct((1, own), f32),
        ),
        in_specs=[any_space] * 3,
        out_specs=(any_space,) * 3,
        scratch_shapes=[pltpu.SemaphoreType.DMA((3,))],
    )(sum_down, sum_up, sum_gain)
    return (sum_down[None, None], sum_up[None, None], sum_gain[None])


def solution(mesh):
    in_specs = (
        P(None, "dp", None),
        P(None, "dp", None),
        P("section", None, None, None),
        P("section", None, None, None),
        P("section", None, None),
        P("dp", None),
    )
    out_specs = (
        P("section", None, "dp", None),
        P("section", None, "dp", None),
        P("section", None, "dp"),
    )
    return jax.shard_map(
        on_device, mesh=mesh, in_specs=in_specs, out_specs=out_specs, check_vma=False
    )
```

```python
import functools

import jax
import jax.numpy as jnp
from jax import lax
from jax.experimental import pallas as pl
from jax.experimental.pallas import tpu as pltpu
from jax.sharding import PartitionSpec as P

epsilon = 1e-06
y_size, z_size = 2, 8
f32, bf16 = jnp.float32, jnp.bfloat16
mesh_ids = pl.DeviceIdType.MESH


def plain_dot(left, right):
    return lax.dot_general(left, right, (((1,), (0,)), ((), ())), preferred_element_type=f32)


def right_dot(left, right):
    return lax.dot_general(left, right, (((1,), (1,)), ((), ())), preferred_element_type=f32)


def left_dot(left, right):
    return lax.dot_general(left, right, (((0,), (0,)), ((), ())), preferred_element_type=f32)


def sigmoid(value):
    return 1.0 / (1.0 + jnp.exp(-value))


def silu_slope(latent):
    gate = sigmoid(latent)
    return gate * (1.0 + latent * (1.0 - gate))


def kernel(
    sizes,
    hidden,
    head,
    down_hbm,
    up_hbm,
    gain_hbm,
    codec_hbm,
    out_down,
    out_up,
    out_gain,
    tok,
    gain,
    codec,
    down,
    up_half,
    down32,
    gain_col,
    gdown_half,
    planes,
    flat,
    tok_half,
    out_half,
    acc,
    weights,
    tok_code,
    latent_ref,
    active_ref,
    inv_ref,
    slope_ref,
    code_in,
    code_out,
    back_in,
    back_out,
    turn_out,
    scaled_out,
    scaled,
    lead_weight,
    lead_slope,
    lead_code,
    active_in,
    wide_in,
    factor,
    factor_in,
    wide_part,
    wide_parts,
    wide_sum,
    down_part,
    down_in,
    down_block,
    down_blocks,
    down_sum,
    up_part,
    up_parts,
    up_line,
    up_lines,
    up_sum,
    up_result,
    up_results,
    local_sem,
    send_sem,
    recv_sem,
):
    X, Y, Z = sizes
    micro, rows, D = hidden.shape
    R = micro * rows
    C, K = codec.shape[1], down.shape[1]
    own = codec.shape[0]
    y_part = D // (X * Y)
    lanes = C // 4
    chunk = D // X
    ratio = D / C
    sec = lax.axis_index("section")
    dp = lax.axis_index("dp")
    core = lax.rem(sec, 2)
    x = dp // (Y * Z)
    y = lax.rem(dp // Z, Y)
    z = lax.rem(dp, Z)
    xy = dp // Z
    other_y = 1 - y
    far_sec = lax.rem(sec + 2, 4)
    sibling = sec + 1 - 2 * core
    ends = jnp.logical_or(sec == 0, sec == 3)

    def place(px, py, pz):
        return (px * Y + py) * Z + pz

    def ring(mine, count):
        return [lax.rem(mine + off, count) for off in range(1, count)]

    def near_first(mine, count):
        offsets = sorted(range(1, count), key=lambda off: (min(off, count - off), off))
        return [lax.rem(mine + off, count) for off in offsets]

    names = [
        ("x0", X), ("z0", Z), ("y0", Z), ("z1", Z), ("y1", 2), ("x1a", X), ("x1b", X),
        ("z4", 2), ("d0", 1), ("d0z", Z), ("d1a", X), ("d1b", X), ("code", 1), ("back", 1), ("active", 1), ("up", 1),
        ("scaled", 1), ("lead_weight", 1), ("lead_slope", 1), ("lead_code", 1),
        ("wide", X * Y), ("factor", X * Y), ("big", Z), ("down_a", Z), ("down_b", X * Y),
        ("down_c", Z), ("up_a", X * Y), ("up_b", Z), ("up_c", X * Y),
    ]
    base, total = {}, 0
    for name, count in names:
        base[name] = total
        total += count
    sent = [0]

    def start(src, dst, name, index, section, place_at, slot=None):
        if slot is None:
            slot = sent[0]
            sent[0] += 1
        copy = pltpu.make_async_remote_copy(
            src_ref=src, dst_ref=dst, send_sem=send_sem.at[slot],
            recv_sem=recv_sem.at[base[name] + index],
            device_id=(section, place_at), device_id_type=mesh_ids,
        )
        copy.start()
        return copy

    def left(src, slot):
        pltpu.make_async_remote_copy(
            src_ref=src, dst_ref=src, send_sem=send_sem.at[slot], recv_sem=recv_sem.at[0],
            device_id=(sec, dp), device_id_type=mesh_ids,
        ).wait_send()

    def arrive(dst, name, index):
        pltpu.make_async_remote_copy(
            src_ref=dst, dst_ref=dst, send_sem=send_sem.at[0],
            recv_sem=recv_sem.at[base[name] + index],
            device_id=(sec, dp), device_id_type=mesh_ids,
        ).wait_recv()

    barrier = pltpu.get_barrier_semaphore()
    peers = [(sec, place(x, y, pz)) for pz in ring(z, Z)]
    xy_ring = ring(xy, X * Y)
    peers += [(which, pxy * Z + z) for which in (sec, sibling) for pxy in xy_ring]
    peers += [(sibling, dp), (far_sec, place(x, other_y, z)), (3 - sec, dp)]
    for peer in peers:
        pl.semaphore_signal(barrier, inc=1, device_id=peer, device_id_type=mesh_ids)

    color0, color1 = 2 * core, 2 * core + 1
    loads = []

    def load(src, dst):
        copy = pltpu.make_async_copy(src, dst, local_sem.at[len(loads)])
        loads.append(copy)
        copy.start()
        return copy

    own_loads = []
    for color in (color0, color1):
        columns = pl.ds(pl.multiple_of(color * lanes, lanes), lanes)
        own_loads.append(load(codec_hbm.at[:, columns], planes.at[color, x, y, z]))
    load_tok = pltpu.make_async_copy(hidden, tok, local_sem.at[20])
    pl.when(sec == 0)(load_tok.start)
    pl.when(sec == 3)(pltpu.make_async_copy(head, tok, local_sem.at[20]).start)
    load_down = load(down_hbm, down)
    load_ups = [
        load(
            up_hbm.at[pl.ds(index * chunk + py * y_part, y_part)],
            up_half.at[py, pl.ds(index * y_part, y_part)],
        )
        for py in range(Y)
        for index in range(X)
    ]
    load_gain = load(gain_hbm, gain)
    load_codec = load(codec_hbm, codec)

    pl.semaphore_wait(barrier, len(peers))
    for copy in own_loads:
        copy.wait()

    half_z = Z // 2
    copies = []
    mine = planes.at[color0, x, y, z]
    for px in ring(x, X):
        copies.append(start(mine, mine, "x0", x, sec, place(px, y, z)))
    mine = planes.at[color1, x, y, z]
    for pz in near_first(z, Z):
        copies.append(start(mine, mine, "z1", z, sec, place(x, y, pz)))

    wide_slot = sent[0]
    sent[0] += X * Y - 1
    wide_peers = [(px, y) for px in ring(x, X)] + [(px, other_y) for px in [x] + ring(x, X)]

    @pl.when(ends)
    def _():
        load_tok.wait()

        def split(index, carry):
            at = pl.ds(pl.multiple_of(index * chunk, chunk), chunk)
            value = tok[:, :, at].reshape(R, chunk)
            for py in range(Y):
                tok_half[py, index] = value[:, py * y_part : (py + 1) * y_part]
            return carry

        lax.fori_loop(0, X, split, 0)
        for off, (px, py) in enumerate(wide_peers):
            start(
                tok_half.at[py, px], wide_in.at[xy], "wide", xy, sec, place(px, py, z),
                wide_slot + off,
            )

    for px in ring(x, X):
        arrive(planes.at[color0, px, y, z], "x0", px)

    def line(pz):
        return planes.at[color0, :, y, pz]

    def pass_y(index, pz):
        block = line(pz)
        section = sec if index % 2 == 0 else far_sec
        copies.append(start(block, block, "y0", pz, section, place(x, other_y, z)))

    def along(steps):
        return lax.rem(z + Z + steps, Z)

    def send_line(block, pz, steps):
        copies.append(start(block, block, "z0", pz, sec, place(x, y, along(steps))))

    for steps in (1, -1, 2, -2):
        send_line(line(z), z, steps)
    pass_y(0, z)

    load_down.wait()
    load_gain.wait()
    for copy in load_ups:
        copy.wait()

    @pl.when(sec == 0)
    def _():
        def squares(index, carry):
            at = pl.ds(pl.multiple_of(index * chunk, chunk), chunk)
            value = tok[:, :, at].reshape(R, chunk).astype(f32)
            return carry + jnp.sum(value * value, axis=-1, keepdims=True)

        square = lax.fori_loop(0, X, squares, jnp.zeros((R, 1), f32))
        inverse = lax.rsqrt(square / D + epsilon)
        inv_ref[...] = inverse

        def project(index, carry):
            at = pl.ds(pl.multiple_of(index * chunk, chunk), chunk)
            value = tok[:, :, at].reshape(R, chunk).astype(f32)
            normed = (value * inverse * gain[:, at]).astype(bf16)
            return carry + plain_dot(normed, down[at, :])

        latent = lax.fori_loop(0, X, project, jnp.zeros((R, K), f32))
        active_ref[...] = (latent * sigmoid(latent)).astype(bf16)
        slope_ref[...] = silu_slope(latent)
        for py in range(Y):
            for index in range(X):
                rows_at = pl.ds(index * y_part, y_part)
                value = right_dot(active_ref[...], up_half[py, rows_at, :])
                value = value + tok_half[py, index].astype(f32)
                out_half[py, index] = value.astype(bf16)

    @pl.when(sec == 3)
    def _():
        value = jnp.zeros((R, K), f32)
        for py in range(Y):
            for index in range(X):
                rows_at = pl.ds(index * y_part, y_part)
                value = value + plain_dot(tok_half[py, index], up_half[py, rows_at, :])
        latent_ref[...] = value

    for pz in ring(z, Z):
        arrive(planes.at[color1, x, y, pz], "z1", pz)
    near, far = planes.at[color1, x, y, 0:half_z], planes.at[color1, x, y, half_z:Z]
    copies.append(start(near, near, "y1", 0, sec, place(x, other_y, z)))
    copies.append(start(far, far, "y1", 1, far_sec, place(x, other_y, z)))
    slab = planes.at[color1, x, y]
    for px in ring(x, X):
        copies.append(start(slab, slab, "x1a", x, sec, place(px, y, z)))
    copies.append(start(slab, slab, "d1a", x, sibling, dp))

    step = 128

    def scale_rows(index, carry):
        at = pl.ds(pl.multiple_of(index * chunk, chunk), chunk)
        column = jnp.broadcast_to(gain[:, at], (step, chunk)).T
        gain_col[at, :] = column
        wide = down[at, :].astype(f32)
        down32[at, :] = wide
        parts = [wide[:, k : k + step] * column[:, : min(step, K)] for k in range(0, K, step)]
        scaled = jnp.concatenate(parts, axis=1).astype(bf16)
        rows_at = pl.ds(pl.multiple_of(index * y_part, y_part), y_part)
        for py in range(Y):
            gdown_half[py, rows_at, :] = scaled[py * y_part : (py + 1) * y_part]
        return carry

    def scale():
        lax.fori_loop(0, X, scale_rows, 0)

    order = [along(steps) for steps in (1, -1, 2, -2, 3, -3, 4)]
    half_x = X // 2
    for index, pz in enumerate(order[0:2]):
        arrive(line(pz), "z0", pz)
        pass_y(index + 1, pz)
    for index, way in enumerate((1, -1)):
        pz = along(2 * way)
        arrive(line(pz), "z0", pz)
        send_line(line(pz), pz, -way)
        part = planes.at[color0, 0:half_x, y, pz] if way > 0 else planes.at[color0, half_x:X, y, pz]
        copies.append(
            start(part, part, "z4", index, sec, place(x, y, along(-2 * way)))
        )
        pass_y(index + 3, pz)
    arrive(planes.at[color1, x, other_y, 0:half_z], "y1", 0)
    arrive(planes.at[color1, x, other_y, half_z:Z], "y1", 1)
    slab = planes.at[color1, x, other_y]
    for px in ring(x, X):
        copies.append(start(slab, slab, "x1b", x, sec, place(px, y, z)))
    copies.append(start(slab, slab, "d1b", x, sibling, dp))
    pl.when(sec != 0)(scale)
    for index, pz in enumerate(order[4:6]):
        arrive(line(pz), "z0", pz)
        pass_y(index + 5, pz)
    arrive(planes.at[color0, 0:half_x, y, order[6]], "z4", 0)
    arrive(planes.at[color0, half_x:X, y, order[6]], "z4", 1)
    pass_y(7, order[6])
    half = planes.at[color0, :, y]
    copies.append(start(half, half, "d0", 0, sibling, dp))
    for px in ring(x, X):
        slab = planes.at[color1, px, y]
        arrive(slab, "x1a", px)
        copies.append(start(slab, slab, "d1a", px, sibling, dp))

    late = []

    def hop(group, src, dst, name, section):
        late.append((group, src, sent[0]))
        start(src, dst, name, 0, section, dp)

    their0, their1 = 2 - 2 * core, 3 - 2 * core
    def products(py, add, last):
        for index in range(X):
            for color in range(4):
                piece = planes[color, index, py].astype(f32).reshape(y_part, lanes).astype(bf16)
                rows_at = slice(index * y_part, (index + 1) * y_part)
                flat[rows_at, color * lanes : (color + 1) * lanes] = piece

        def wide_code(rows):
            value = jnp.zeros((R, C), f32)
            for index in range(X):
                rows_at = slice(index * y_part, (index + 1) * y_part)
                value = value + plain_dot(rows[py, index], flat[rows_at, :])
            add(tok_code, slice(0, C), value)

        pl.when(sec == 0)(lambda: wide_code(out_half))
        if last:
            @pl.when(sec == 0)
            def _():
                code_out[...] = tok_code[...].astype(bf16)
                hop("first", code_out, code_in, "code", 1)
                hop("first", active_ref, active_in, "active", 1)

        @pl.when(sec != 3)
        def _():
            add(acc, slice(K + C, K + C + K), left_dot(flat[...], up_half[py]))

        pl.when(sec == 3)(lambda: wide_code(tok_half))

        @pl.when(sec != 0)
        def _():
            add(acc, slice(0, K), left_dot(flat[...], gdown_half[py]))
            add(acc, slice(K, K + C), left_dot(flat[...], flat[...]))

    def put(ref, columns, value):
        ref[:, columns] = value

    def add_to(ref, columns, value):
        ref[:, columns] += value

    arrive(planes.at[their0, :, y], "d0", 0)
    arrive(planes.at[their1, x, y], "d1a", x)
    for px in ring(x, X):
        arrive(planes.at[their1, px, y], "d1a", px)
    products(y, put, False)

    for pz in [z] + order:
        block = planes.at[color0, :, other_y, pz]
        arrive(block, "y0", pz)
        copies.append(start(block, block, "d0z", pz, sibling, dp))
    for px in ring(x, X):
        slab = planes.at[color1, px, other_y]
        arrive(slab, "x1b", px)
        copies.append(start(slab, slab, "d1b", px, sibling, dp))

    for pz in [z] + order:
        arrive(planes.at[their0, :, other_y, pz], "d0z", pz)
    arrive(planes.at[their1, x, other_y], "d1b", x)
    for px in ring(x, X):
        arrive(planes.at[their1, px, other_y], "d1b", px)

    products(other_y, add_to, True)

    @pl.when(sec != 3)
    def _():
        weights[:, K + C :] = acc[:, K + C :].astype(bf16)

    @pl.when(sec != 0)
    def _():
        weights[:, 0 : K + C] = acc[:, 0 : K + C].astype(bf16)

    XY = X * Y
    def forward(code, weight):
        grid = plain_dot(code, weights[:, K : K + C])
        square = jnp.sum(code.astype(f32) * grid, axis=-1, keepdims=True) * (ratio * ratio / D)
        inverse = lax.rsqrt(square + epsilon)
        latent = ratio * inverse * plain_dot(code, weight)
        active = (latent * sigmoid(latent)).astype(bf16)
        return grid, inverse, latent, active

    def backward(inner, grid, inverse, latent, d_latent, weight):
        share = jnp.sum(d_latent.astype(f32) * latent, axis=-1, keepdims=True)
        share = share * inverse * inverse * (ratio / D)
        through = right_dot(d_latent, weight)
        return (ratio * (inner + inverse * through - share * grid)).astype(bf16)

    def next_code(grid, active):
        return (ratio * grid + right_dot(active, weights[:, K + C :])).astype(bf16)

    def scale_latent(d_latent, inverse):
        return (d_latent.astype(f32) * (ratio * inverse)).astype(bf16)

    def send_factor(name):
        for pxy in [xy] + xy_ring:
            late.append((name, factor, sent[0]))
            start(factor, factor_in.at[xy], "factor", xy, sibling, pxy * Z + z)

    @pl.when(sec == 0)
    def _():
        latent_ref[...] = slope_ref[...] * inv_ref[...]
        hop("first", weights.at[:, K + C :], lead_weight, "lead_weight", 1)
        hop("first", latent_ref, lead_slope, "lead_slope", 1)
        scale()

    @pl.when(sec == 3)
    def _():
        hop("last", weights.at[:, 0:K], lead_weight, "lead_weight", 2)
        hop("last", latent_ref, lead_slope, "lead_slope", 2)
        hop("last", tok_code, lead_code, "lead_code", 2)
        arrive(code_in, "code", 0)
        arrive(scaled, "scaled", 0)
        down_part[...] = left_dot(code_in[...], scaled[...]).astype(bf16).reshape(down_part.shape)
        arrive(active_in, "active", 0)
        arrive(back_in, "back", 0)
        up_part[...] = left_dot(back_in[...], active_in[...]).astype(bf16).reshape(up_part.shape)

    @pl.when(sec == 1)
    def _():
        arrive(code_in, "code", 0)
        grid, inverse, latent, active = forward(code_in[...], weights[:, 0:K])
        code_out[...] = next_code(grid, active)
        hop("second", code_out, code_in, "code", 2)
        active_ref[...] = active
        hop("second", active_ref, active_in, "active", 2)
        slope = silu_slope(latent)
        arrive(lead_weight, "lead_weight", 0)
        arrive(lead_slope, "lead_slope", 0)
        arrive(active_in, "active", 0)
        arrive(back_in, "back", 0)
        both = plain_dot(back_in[...], weights[:, K:])
        d_latent = (both[:, C:] * slope).astype(bf16)
        back = backward(both[:, 0:C], grid, inverse, latent, d_latent, weights[:, 0:K])
        factor[...] = (plain_dot(back, lead_weight[...]) * lead_slope[...]).astype(bf16)
        down = left_dot(code_in[...], scale_latent(d_latent, inverse))
        down_part[...] = down.astype(bf16).reshape(down_part.shape)
        up_part[...] = left_dot(back, active_in[...]).astype(bf16).reshape(up_part.shape)

    @pl.when(sec == 2)
    def _():
        arrive(code_in, "code", 0)
        grid, inverse, latent, active = forward(code_in[...], weights[:, 0:K])
        code = next_code(grid, active)
        code_out[...] = code
        hop("third", code_out, code_in, "code", 3)
        active_ref[...] = active
        hop("third", active_ref, active_in, "active", 3)
        arrive(lead_weight, "lead_weight", 0)
        arrive(lead_slope, "lead_slope", 0)
        arrive(lead_code, "lead_code", 0)
        last_grid, last_inverse, last_latent, last_active = forward(code, lead_weight[...])
        last = (lead_slope[...] * silu_slope(last_latent)).astype(bf16)
        turn = backward(
            lead_code[...], last_grid, last_inverse, last_latent, last, lead_weight[...]
        )
        both = plain_dot(turn, weights[:, K:])
        d_latent = (both[:, C:] * silu_slope(latent)).astype(bf16)
        back = backward(both[:, 0:C], grid, inverse, latent, d_latent, weights[:, 0:K])
        back_out[...] = back
        hop("third", back_out, back_in, "back", 1)
        turn_out[...] = turn
        hop("third", turn_out, back_in, "back", 3)
        scaled_out[...] = scale_latent(last, last_inverse)
        hop("third", scaled_out, scaled, "scaled", 3)
        factor[...] = last_active
        down = left_dot(code_in[...], scale_latent(d_latent, inverse))
        down_part[...] = down.astype(bf16).reshape(down_part.shape)
        arrive(active_in, "active", 0)
        up_part[...] = left_dot(back, active_in[...]).astype(bf16).reshape(up_part.shape)

    xy_peers = [(pxy, pxy * Z + z) for pxy in xy_ring]
    z_peers = [(pz, place(x, y, pz)) for pz in near_first(z, Z)]
    pending_rest, pending_ends = [], []

    def spread(ref_of, landings, name, mine, peers, pending):
        for peer, peer_dp in peers:
            slot = sent[0]
            start(ref_of(peer), landings.at[mine], name, mine, sec, peer_dp)
            pending.append((landings, slot))

    def gathered(first, landing, name, peers):
        value = first.astype(f32)
        for peer, _ in peers:
            arrive(landing.at[peer], name, peer)
            value = value + landing[peer].astype(f32)
        return value

    rest = sec != 0
    load_codec.wait()

    @pl.when(rest)
    def _():
        spread(lambda peer: down_part.at[peer], down_in, "down_a", z, z_peers, pending_rest)
        spread(lambda peer: up_part.at[peer], up_parts, "up_a", xy, xy_peers, pending_rest)

    @pl.when(rest)
    def _():
        up_line[...] = gathered(up_part[xy], up_parts, "up_a", xy_peers).astype(bf16)
        spread(lambda peer: up_line, up_lines, "up_b", z, z_peers, pending_rest)

    @pl.when(jnp.logical_not(ends))
    def _():
        send_factor("lead")

    @pl.when(ends)
    def _():
        arrive(factor_in.at[xy], "factor", xy)
        value = left_dot(tok_half[y, x], factor_in[xy])
        for pxy, _ in xy_peers:
            arrive(wide_in.at[pxy], "wide", pxy)
            arrive(factor_in.at[pxy], "factor", pxy)
            value = value + left_dot(wide_in[pxy], factor_in[pxy])
        wide_part[...] = value.reshape(Z, own, K).astype(bf16)
        spread(lambda peer: wide_part.at[peer], wide_parts, "big", z, z_peers, pending_ends)

    @pl.when(rest)
    def _():
        down_block[...] = gathered(down_part[z], down_in, "down_a", z_peers).astype(bf16)
        spread(lambda peer: down_block, down_blocks, "down_b", xy, xy_peers, pending_rest)
        up_sum[xy] = gathered(up_line[...], up_lines, "up_b", z_peers).astype(bf16)
        spread(lambda peer: up_sum.at[xy], up_sum, "up_c", xy, xy_peers, pending_rest)
        down_sum[z] = gathered(down_block[...], down_blocks, "down_b", xy_peers).astype(bf16)
        spread(lambda peer: down_sum.at[z], down_sum, "down_c", z, z_peers, pending_rest)
        for pxy, _ in xy_peers:
            arrive(up_sum.at[pxy], "up_c", pxy)
        up_result[...] = plain_dot(codec[...], up_sum[...].reshape(C, K))
        hop("rest", up_result, up_results, "up", sec - 1)

    own_rows = pl.ds(pl.multiple_of(dp * own, 8), own)

    def put_down(value):
        column = gain_col[own_rows, :]
        weighted = down32[own_rows, :] * value
        folded = weighted[:, 0 : min(step, K)]
        for k in range(step, K, step):
            folded = folded + weighted[:, k : k + step]
        if own < step:
            folded = jnp.concatenate([folded, jnp.zeros((step - own, folded.shape[1]), f32)], axis=0)
        out_gain[...] = jnp.sum(folded.T, axis=0, keepdims=True)[:, 0:own]
        for k in range(0, K, step):
            out_down[:, k : k + step] = value[:, k : k + step] * column[:, : min(step, K)]

    @pl.when(ends)
    def _():
        wide_sum[...] = gathered(wide_part[z], wide_parts, "big", z_peers)

    @pl.when(rest)
    def _():
        for pz, _ in z_peers:
            arrive(down_sum.at[pz], "down_c", pz)
        put_down(plain_dot(codec[...], down_sum[...].reshape(C, K)))

    @pl.when(sec == 0)
    def _():
        put_down(wide_sum[...])

    @pl.when(sec == 3)
    def _():
        out_up[...] = wide_sum[...]

    @pl.when(sec != 3)
    def _():
        arrive(up_results, "up", 0)
        out_up[...] = up_results[...]

    @pl.when(rest)
    def _():
        for landing, slot in pending_rest:
            left(landing.at[0], slot)

    @pl.when(ends)
    def _():
        for landing, slot in pending_ends:
            left(landing.at[0], slot)
        for off in range(XY - 1):
            left(wide_in.at[0], wide_slot + off)

    groups = [("first", sec == 0), ("second", sec == 1), ("third", sec == 2), ("last", sec == 3)]
    groups += [("rest", rest), ("lead", jnp.logical_not(ends))]
    for group, chosen in groups:
        @pl.when(chosen)
        def _():
            for which, src, slot in late:
                if which == group:
                    left(src, slot)

    for copy in copies:
        copy.wait_send()


def hand_out(down, up, gain, out_down, out_up, out_gain, sem):
    copies = [
        pltpu.make_async_copy(down, out_down, sem.at[0]),
        pltpu.make_async_copy(up, out_up, sem.at[1]),
        pltpu.make_async_copy(gain, out_gain, sem.at[2]),
    ]
    for copy in copies:
        copy.start()
    for copy in copies:
        copy.wait()


def on_device(hidden_in, head_grad, down_w, up_w, norm_gain, codec):
    micro, rows, D = hidden_in.shape
    K, C, own = down_w.shape[3], codec.shape[1], codec.shape[0]
    Y, Z = y_size, z_size
    X = lax.axis_size("dp") // (Y * Z)
    R, chunk, lanes = micro * rows, D // X, C // 4
    block_rows = C // (X * Y)
    any_space = pl.BlockSpec(memory_space=pl.ANY)
    vmem = pl.BlockSpec(memory_space=pltpu.VMEM)
    recv_count = 5 * X + 8 * Z + 14 + 5 * X * Y
    scratch = [
        ((micro, rows, D), bf16),
        ((1, D), f32),
        ((own, C), bf16),
        ((D, K), bf16),
        ((Y, D // Y, K), bf16),
        ((D, K), f32),
        ((D, 128), f32),
        ((Y, D // Y, K), bf16),
        ((4, X, Y, Z, own, lanes), bf16),
        ((D // Y, C), bf16),
        ((Y, X, R, chunk // Y), bf16),
        ((Y, X, R, chunk // Y), bf16),
        ((C, 2 * K + C), f32),
        ((C, 2 * K + C), bf16),
        ((R, C), f32),
        ((R, K), f32),
        ((R, K), bf16),
        ((R, 1), f32),
        ((R, K), f32),
        ((R, C), bf16),
        ((R, C), bf16),
        ((R, C), bf16),
        ((R, C), bf16),
        ((R, C), bf16),
        ((R, K), bf16),
        ((R, K), bf16),
        ((C, K), bf16),
        ((R, K), f32),
        ((R, C), f32),
        ((R, K), bf16),
        ((X * Y, R, chunk // Y), bf16),
        ((R, K), bf16),
        ((X * Y, R, K), bf16),
        ((Z, own, K), bf16),
        ((Z, own, K), bf16),
        ((own, K), f32),
        ((Z, C // Z, K), bf16),
        ((Z, C // Z, K), bf16),
        ((C // Z, K), bf16),
        ((X * Y, C // Z, K), bf16),
        ((Z, C // Z, K), bf16),
        ((X * Y, block_rows, K), bf16),
        ((X * Y, block_rows, K), bf16),
        ((block_rows, K), bf16),
        ((Z, block_rows, K), bf16),
        ((X * Y, block_rows, K), bf16),
        ((own, K), f32),
        ((own, K), f32),
    ]
    sum_down, sum_up, sum_gain = pl.pallas_call(
        functools.partial(kernel, (X, Y, Z)),
        out_shape=(
            jax.ShapeDtypeStruct((own, K), f32),
            jax.ShapeDtypeStruct((own, K), f32),
            jax.ShapeDtypeStruct((1, own), f32),
        ),
        in_specs=[any_space] * 6,
        out_specs=(vmem, vmem, vmem),
        scratch_shapes=[pltpu.VMEM(shape, kind) for shape, kind in scratch]
        + [
            pltpu.SemaphoreType.DMA((21,)),
            pltpu.SemaphoreType.DMA((160,)),
            pltpu.SemaphoreType.DMA((recv_count,)),
        ],
        compiler_params=pltpu.CompilerParams(
            collective_id=0, has_side_effects=True, vmem_limit_bytes=56 * 1024 * 1024
        ),
    )(hidden_in, head_grad, down_w[0, 0], up_w[0, 0], norm_gain[0], codec)
    sum_down, sum_up, sum_gain = pl.pallas_call(
        hand_out,
        out_shape=(
            jax.ShapeDtypeStruct((own, K), f32),
            jax.ShapeDtypeStruct((own, K), f32),
            jax.ShapeDtypeStruct((1, own), f32),
        ),
        in_specs=[any_space] * 3,
        out_specs=(any_space,) * 3,
        scratch_shapes=[pltpu.SemaphoreType.DMA((3,))],
    )(sum_down, sum_up, sum_gain)
    return (sum_down[None, None], sum_up[None, None], sum_gain[None])


def solution(mesh):
    in_specs = (
        P(None, "dp", None),
        P(None, "dp", None),
        P("section", None, None, None),
        P("section", None, None, None),
        P("section", None, None),
        P("dp", None),
    )
    out_specs = (
        P("section", None, "dp", None),
        P("section", None, "dp", None),
        P("section", None, "dp"),
    )
    return jax.shard_map(
        on_device, mesh=mesh, in_specs=in_specs, out_specs=out_specs, check_vma=False
    )
```

```python
import functools

import jax
import jax.numpy as jnp
from jax import lax
from jax.experimental import pallas as pl
from jax.experimental.pallas import tpu as pltpu
from jax.sharding import PartitionSpec as P

epsilon = 1e-06
y_size, z_size = 2, 8
f32, bf16 = jnp.float32, jnp.bfloat16
mesh_ids = pl.DeviceIdType.MESH


def plain_dot(left, right):
    return lax.dot_general(left, right, (((1,), (0,)), ((), ())), preferred_element_type=f32)


def right_dot(left, right):
    return lax.dot_general(left, right, (((1,), (1,)), ((), ())), preferred_element_type=f32)


def left_dot(left, right):
    return lax.dot_general(left, right, (((0,), (0,)), ((), ())), preferred_element_type=f32)


def sigmoid(value):
    return 1.0 / (1.0 + jnp.exp(-value))


def silu_slope(latent):
    gate = sigmoid(latent)
    return gate * (1.0 + latent * (1.0 - gate))


def kernel(
    sizes,
    hidden,
    head,
    down_hbm,
    up_hbm,
    gain_hbm,
    codec_hbm,
    out_down,
    out_up,
    out_gain,
    tok,
    gain,
    codec,
    down,
    up_half,
    down32,
    gain_col,
    gdown_half,
    planes,
    flat,
    tok_half,
    out_half,
    acc,
    weights,
    tok_code,
    latent_ref,
    active_ref,
    inv_ref,
    slope_ref,
    code_in,
    code_out,
    back_in,
    back_out,
    turn_out,
    scaled_out,
    scaled,
    lead_weight,
    lead_slope,
    lead_code,
    active_in,
    wide_in,
    factor,
    factor_in,
    wide_part,
    wide_parts,
    wide_sum,
    down_part,
    down_in,
    down_block,
    down_blocks,
    down_sum,
    up_part,
    up_parts,
    up_line,
    up_lines,
    up_sum,
    up_result,
    up_results,
    local_sem,
    send_sem,
    recv_sem,
):
    X, Y, Z = sizes
    micro, rows, D = hidden.shape
    R = micro * rows
    C, K = codec.shape[1], down.shape[1]
    own = codec.shape[0]
    y_part = D // (X * Y)
    lanes = C // 4
    chunk = D // X
    ratio = D / C
    sec = lax.axis_index("section")
    dp = lax.axis_index("dp")
    core = lax.rem(sec, 2)
    x = dp // (Y * Z)
    y = lax.rem(dp // Z, Y)
    z = lax.rem(dp, Z)
    xy = dp // Z
    other_y = 1 - y
    far_sec = lax.rem(sec + 2, 4)
    sibling = sec + 1 - 2 * core
    ends = jnp.logical_or(sec == 0, sec == 3)

    def place(px, py, pz):
        return (px * Y + py) * Z + pz

    def ring(mine, count):
        return [lax.rem(mine + off, count) for off in range(1, count)]

    def near_first(mine, count):
        offsets = sorted(range(1, count), key=lambda off: (min(off, count - off), off))
        return [lax.rem(mine + off, count) for off in offsets]

    names = [
        ("x0", X), ("z0", Z), ("y0", Z), ("z1", Z), ("y1", 2), ("x1a", X), ("x1b", X),
        ("z4", 2), ("d0", 1), ("d0z", Z), ("d1a", X), ("d1b", X), ("code", 1), ("back", 1), ("active", 1), ("up", 1),
        ("scaled", 1), ("lead_weight", 1), ("lead_slope", 1), ("lead_code", 1),
        ("wide", X * Y), ("factor", X * Y), ("big", Z), ("down_a", Z), ("down_b", X * Y),
        ("down_c", Z), ("up_a", X * Y), ("up_b", Z), ("up_c", X * Y),
    ]
    base, total = {}, 0
    for name, count in names:
        base[name] = total
        total += count
    sent = [0]

    def start(src, dst, name, index, section, place_at, slot=None):
        if slot is None:
            slot = sent[0]
            sent[0] += 1
        copy = pltpu.make_async_remote_copy(
            src_ref=src, dst_ref=dst, send_sem=send_sem.at[slot],
            recv_sem=recv_sem.at[base[name] + index],
            device_id=(section, place_at), device_id_type=mesh_ids,
        )
        copy.start()
        return copy

    def left(src, slot):
        pltpu.make_async_remote_copy(
            src_ref=src, dst_ref=src, send_sem=send_sem.at[slot], recv_sem=recv_sem.at[0],
            device_id=(sec, dp), device_id_type=mesh_ids,
        ).wait_send()

    def arrive(dst, name, index):
        pltpu.make_async_remote_copy(
            src_ref=dst, dst_ref=dst, send_sem=send_sem.at[0],
            recv_sem=recv_sem.at[base[name] + index],
            device_id=(sec, dp), device_id_type=mesh_ids,
        ).wait_recv()

    barrier = pltpu.get_barrier_semaphore()
    peers = [(sec, place(x, y, pz)) for pz in ring(z, Z)]
    xy_ring = ring(xy, X * Y)
    peers += [(which, pxy * Z + z) for which in (sec, sibling) for pxy in xy_ring]
    peers += [(sibling, dp), (far_sec, place(x, other_y, z)), (3 - sec, dp)]
    for peer in peers:
        pl.semaphore_signal(barrier, inc=1, device_id=peer, device_id_type=mesh_ids)

    color0, color1 = 2 * core, 2 * core + 1
    loads = []

    def load(src, dst):
        copy = pltpu.make_async_copy(src, dst, local_sem.at[len(loads)])
        loads.append(copy)
        copy.start()
        return copy

    own_loads = []
    for color in (color0, color1):
        columns = pl.ds(pl.multiple_of(color * lanes, lanes), lanes)
        own_loads.append(load(codec_hbm.at[:, columns], planes.at[color, x, y, z]))
    load_tok = pltpu.make_async_copy(hidden, tok, local_sem.at[20])
    pl.when(sec == 0)(load_tok.start)
    pl.when(sec == 3)(pltpu.make_async_copy(head, tok, local_sem.at[20]).start)
    load_down = load(down_hbm, down)
    load_ups = [
        load(
            up_hbm.at[pl.ds(index * chunk + py * y_part, y_part)],
            up_half.at[py, pl.ds(index * y_part, y_part)],
        )
        for py in range(Y)
        for index in range(X)
    ]
    load_gain = load(gain_hbm, gain)
    load_codec = load(codec_hbm, codec)

    pl.semaphore_wait(barrier, len(peers))
    for copy in own_loads:
        copy.wait()

    half_z = Z // 2
    copies = []
    mine = planes.at[color0, x, y, z]
    for px in near_first(x, X)[::-1]:
        copies.append(start(mine, mine, "x0", x, sec, place(px, y, z)))
    mine = planes.at[color1, x, y, z]
    for pz in near_first(z, Z):
        copies.append(start(mine, mine, "z1", z, sec, place(x, y, pz)))

    wide_slot = sent[0]
    sent[0] += X * Y - 1
    wide_peers = [(px, y) for px in ring(x, X)] + [(px, other_y) for px in [x] + ring(x, X)]

    @pl.when(ends)
    def _():
        load_tok.wait()

        def split(index, carry):
            at = pl.ds(pl.multiple_of(index * chunk, chunk), chunk)
            value = tok[:, :, at].reshape(R, chunk)
            for py in range(Y):
                tok_half[py, index] = value[:, py * y_part : (py + 1) * y_part]
            return carry

        lax.fori_loop(0, X, split, 0)
        for off, (px, py) in enumerate(wide_peers):
            start(
                tok_half.at[py, px], wide_in.at[xy], "wide", xy, sec, place(px, py, z),
                wide_slot + off,
            )

    for px in ring(x, X):
        arrive(planes.at[color0, px, y, z], "x0", px)

    def line(pz):
        return planes.at[color0, :, y, pz]

    def pass_y(index, pz):
        block = line(pz)
        section = sec if index % 2 == 0 else far_sec
        copies.append(start(block, block, "y0", pz, section, place(x, other_y, z)))

    def along(steps):
        return lax.rem(z + Z + steps, Z)

    def send_line(block, pz, steps):
        copies.append(start(block, block, "z0", pz, sec, place(x, y, along(steps))))

    for steps in (1, -1, 2, -2):
        send_line(line(z), z, steps)
    pass_y(0, z)

    load_down.wait()
    load_gain.wait()
    for copy in load_ups:
        copy.wait()

    @pl.when(sec == 0)
    def _():
        def squares(index, carry):
            at = pl.ds(pl.multiple_of(index * chunk, chunk), chunk)
            value = tok[:, :, at].reshape(R, chunk).astype(f32)
            return carry + jnp.sum(value * value, axis=-1, keepdims=True)

        square = lax.fori_loop(0, X, squares, jnp.zeros((R, 1), f32))
        inverse = lax.rsqrt(square / D + epsilon)
        inv_ref[...] = inverse

        def project(index, carry):
            at = pl.ds(pl.multiple_of(index * chunk, chunk), chunk)
            value = tok[:, :, at].reshape(R, chunk).astype(f32)
            normed = (value * inverse * gain[:, at]).astype(bf16)
            return carry + plain_dot(normed, down[at, :])

        latent = lax.fori_loop(0, X, project, jnp.zeros((R, K), f32))
        active_ref[...] = (latent * sigmoid(latent)).astype(bf16)
        slope_ref[...] = silu_slope(latent)
        for py in range(Y):
            for index in range(X):
                rows_at = pl.ds(index * y_part, y_part)
                value = right_dot(active_ref[...], up_half[py, rows_at, :])
                value = value + tok_half[py, index].astype(f32)
                out_half[py, index] = value.astype(bf16)

    @pl.when(sec == 3)
    def _():
        value = jnp.zeros((R, K), f32)
        for py in range(Y):
            for index in range(X):
                rows_at = pl.ds(index * y_part, y_part)
                value = value + plain_dot(tok_half[py, index], up_half[py, rows_at, :])
        latent_ref[...] = value

    for pz in ring(z, Z):
        arrive(planes.at[color1, x, y, pz], "z1", pz)
    near, far = planes.at[color1, x, y, 0:half_z], planes.at[color1, x, y, half_z:Z]
    copies.append(start(near, near, "y1", 0, sec, place(x, other_y, z)))
    copies.append(start(far, far, "y1", 1, far_sec, place(x, other_y, z)))
    slab = planes.at[color1, x, y]
    for px in near_first(x, X)[::-1]:
        copies.append(start(slab, slab, "x1a", x, sec, place(px, y, z)))
    copies.append(start(slab, slab, "d1a", x, sibling, dp))

    step = 128

    def scale_rows(index, carry):
        at = pl.ds(pl.multiple_of(index * chunk, chunk), chunk)
        column = jnp.broadcast_to(gain[:, at], (step, chunk)).T
        gain_col[at, :] = column
        wide = down[at, :].astype(f32)
        down32[at, :] = wide
        parts = [wide[:, k : k + step] * column[:, : min(step, K)] for k in range(0, K, step)]
        scaled = jnp.concatenate(parts, axis=1).astype(bf16)
        rows_at = pl.ds(pl.multiple_of(index * y_part, y_part), y_part)
        for py in range(Y):
            gdown_half[py, rows_at, :] = scaled[py * y_part : (py + 1) * y_part]
        return carry

    def scale():
        lax.fori_loop(0, X, scale_rows, 0)

    order = [along(steps) for steps in (1, -1, 2, -2, 3, -3, 4)]
    half_x = X // 2
    for index, pz in enumerate(order[0:2]):
        arrive(line(pz), "z0", pz)
        pass_y(index + 1, pz)
    for index, way in enumerate((1, -1)):
        pz = along(2 * way)
        arrive(line(pz), "z0", pz)
        send_line(line(pz), pz, -way)
        part = planes.at[color0, 0:half_x, y, pz] if way > 0 else planes.at[color0, half_x:X, y, pz]
        copies.append(
            start(part, part, "z4", index, sec, place(x, y, along(-2 * way)))
        )
        pass_y(index + 3, pz)
    arrive(planes.at[color1, x, other_y, 0:half_z], "y1", 0)
    arrive(planes.at[color1, x, other_y, half_z:Z], "y1", 1)
    slab = planes.at[color1, x, other_y]
    for px in near_first(x, X)[::-1]:
        copies.append(start(slab, slab, "x1b", x, sec, place(px, y, z)))
    copies.append(start(slab, slab, "d1b", x, sibling, dp))
    pl.when(sec != 0)(scale)
    for index, pz in enumerate(order[4:6]):
        arrive(line(pz), "z0", pz)
        pass_y(index + 5, pz)
    arrive(planes.at[color0, 0:half_x, y, order[6]], "z4", 0)
    arrive(planes.at[color0, half_x:X, y, order[6]], "z4", 1)
    pass_y(7, order[6])
    half = planes.at[color0, :, y]
    copies.append(start(half, half, "d0", 0, sibling, dp))
    for px in ring(x, X):
        slab = planes.at[color1, px, y]
        arrive(slab, "x1a", px)
        copies.append(start(slab, slab, "d1a", px, sibling, dp))

    late = []

    def hop(group, src, dst, name, section):
        late.append((group, src, sent[0]))
        start(src, dst, name, 0, section, dp)

    their0, their1 = 2 - 2 * core, 3 - 2 * core
    def products(py, add, last):
        for index in range(X):
            for color in range(4):
                piece = planes[color, index, py].astype(f32).reshape(y_part, lanes).astype(bf16)
                rows_at = slice(index * y_part, (index + 1) * y_part)
                flat[rows_at, color * lanes : (color + 1) * lanes] = piece

        def wide_code(rows):
            value = jnp.zeros((R, C), f32)
            for index in range(X):
                rows_at = slice(index * y_part, (index + 1) * y_part)
                value = value + plain_dot(rows[py, index], flat[rows_at, :])
            add(tok_code, slice(0, C), value)

        pl.when(sec == 0)(lambda: wide_code(out_half))
        if last:
            @pl.when(sec == 0)
            def _():
                code_out[...] = tok_code[...].astype(bf16)
                hop("first", code_out, code_in, "code", 1)
                hop("first", active_ref, active_in, "active", 1)

        @pl.when(sec != 3)
        def _():
            add(acc, slice(K + C, K + C + K), left_dot(flat[...], up_half[py]))

        pl.when(sec == 3)(lambda: wide_code(tok_half))

        @pl.when(sec != 0)
        def _():
            add(acc, slice(0, K), left_dot(flat[...], gdown_half[py]))
            add(acc, slice(K, K + C), left_dot(flat[...], flat[...]))

    def put(ref, columns, value):
        ref[:, columns] = value

    def add_to(ref, columns, value):
        ref[:, columns] += value

    arrive(planes.at[their0, :, y], "d0", 0)
    arrive(planes.at[their1, x, y], "d1a", x)
    for px in ring(x, X):
        arrive(planes.at[their1, px, y], "d1a", px)
    products(y, put, False)

    for pz in [z] + order:
        block = planes.at[color0, :, other_y, pz]
        arrive(block, "y0", pz)
        copies.append(start(block, block, "d0z", pz, sibling, dp))
    for px in ring(x, X):
        slab = planes.at[color1, px, other_y]
        arrive(slab, "x1b", px)
        copies.append(start(slab, slab, "d1b", px, sibling, dp))

    for pz in [z] + order:
        arrive(planes.at[their0, :, other_y, pz], "d0z", pz)
    arrive(planes.at[their1, x, other_y], "d1b", x)
    for px in ring(x, X):
        arrive(planes.at[their1, px, other_y], "d1b", px)

    products(other_y, add_to, True)

    @pl.when(sec != 3)
    def _():
        weights[:, K + C :] = acc[:, K + C :].astype(bf16)

    @pl.when(sec != 0)
    def _():
        weights[:, 0 : K + C] = acc[:, 0 : K + C].astype(bf16)

    XY = X * Y
    def forward(code, weight):
        grid = plain_dot(code, weights[:, K : K + C])
        square = jnp.sum(code.astype(f32) * grid, axis=-1, keepdims=True) * (ratio * ratio / D)
        inverse = lax.rsqrt(square + epsilon)
        latent = ratio * inverse * plain_dot(code, weight)
        active = (latent * sigmoid(latent)).astype(bf16)
        return grid, inverse, latent, active

    def backward(inner, grid, inverse, latent, d_latent, weight):
        share = jnp.sum(d_latent.astype(f32) * latent, axis=-1, keepdims=True)
        share = share * inverse * inverse * (ratio / D)
        through = right_dot(d_latent, weight)
        return (ratio * (inner + inverse * through - share * grid)).astype(bf16)

    def next_code(grid, active):
        return (ratio * grid + right_dot(active, weights[:, K + C :])).astype(bf16)

    def scale_latent(d_latent, inverse):
        return (d_latent.astype(f32) * (ratio * inverse)).astype(bf16)

    def send_factor(name):
        for pxy in [xy] + xy_ring:
            late.append((name, factor, sent[0]))
            start(factor, factor_in.at[xy], "factor", xy, sibling, pxy * Z + z)

    far_x = sorted(range(X), key=lambda off: -min(off, X - off))
    xy_far = [(lax.rem(x + off, X), other_y) for off in far_x]
    xy_far += [(lax.rem(x + off, X), y) for off in far_x[:-1]]
    xy_peers = [(px * Y + py, place(px, py, z)) for px, py in xy_far]
    z_peers = [(pz, place(x, y, pz)) for pz in near_first(z, Z)[::-1]]
    pending_rest, pending_ends, pending_back, first_slot = [], [], [], {}

    def spread(ref_of, landings, name, mine, peers, pending):
        if name not in first_slot:
            first_slot[name] = sent[0]
            sent[0] += len(peers)
            pending.extend((landings, first_slot[name] + n) for n in range(len(peers)))
        for n, (peer, peer_dp) in enumerate(peers):
            start(
                ref_of(peer), landings.at[mine], name, mine, sec, peer_dp, first_slot[name] + n
            )

    def gathered(first, landing, name, peers):
        value = first.astype(f32)
        for peer, _ in peers:
            arrive(landing.at[peer], name, peer)
            value = value + landing[peer].astype(f32)
        return value

    @pl.when(sec == 0)
    def _():
        latent_ref[...] = slope_ref[...] * inv_ref[...]
        hop("first", weights.at[:, K + C :], lead_weight, "lead_weight", 1)
        hop("first", latent_ref, lead_slope, "lead_slope", 1)
        scale()

    @pl.when(sec == 3)
    def _():
        hop("last", weights.at[:, 0:K], lead_weight, "lead_weight", 2)
        hop("last", latent_ref, lead_slope, "lead_slope", 2)
        hop("last", tok_code, lead_code, "lead_code", 2)
        arrive(code_in, "code", 0)
        arrive(scaled, "scaled", 0)
        down_part[...] = left_dot(code_in[...], scaled[...]).astype(bf16).reshape(down_part.shape)
        spread(lambda peer: down_part.at[peer], down_in, "down_a", z, z_peers, pending_rest)
        arrive(active_in, "active", 0)
        arrive(back_in, "back", 0)
        up_part[...] = left_dot(back_in[...], active_in[...]).astype(bf16).reshape(up_part.shape)
        spread(lambda peer: up_part.at[peer], up_parts, "up_a", xy, xy_peers, pending_rest)

    @pl.when(sec == 1)
    def _():
        arrive(code_in, "code", 0)
        grid, inverse, latent, active = forward(code_in[...], weights[:, 0:K])
        code_out[...] = next_code(grid, active)
        hop("second", code_out, code_in, "code", 2)
        active_ref[...] = active
        hop("second", active_ref, active_in, "active", 2)
        slope = silu_slope(latent)
        arrive(lead_weight, "lead_weight", 0)
        arrive(lead_slope, "lead_slope", 0)
        arrive(active_in, "active", 0)
        arrive(back_in, "back", 0)
        both = plain_dot(back_in[...], weights[:, K:])
        d_latent = (both[:, C:] * slope).astype(bf16)
        back = backward(both[:, 0:C], grid, inverse, latent, d_latent, weights[:, 0:K])
        up_part[...] = left_dot(back, active_in[...]).astype(bf16).reshape(up_part.shape)
        spread(lambda peer: up_part.at[peer], up_parts, "up_a", xy, xy_peers, pending_rest)
        down = left_dot(code_in[...], scale_latent(d_latent, inverse))
        down_part[...] = down.astype(bf16).reshape(down_part.shape)
        spread(lambda peer: down_part.at[peer], down_in, "down_a", z, z_peers, pending_rest)
        factor[...] = (plain_dot(back, lead_weight[...]) * lead_slope[...]).astype(bf16)

    @pl.when(sec == 2)
    def _():
        arrive(code_in, "code", 0)
        grid, inverse, latent, active = forward(code_in[...], weights[:, 0:K])
        code = next_code(grid, active)
        code_out[...] = code
        hop("third", code_out, code_in, "code", 3)
        active_ref[...] = active
        hop("third", active_ref, active_in, "active", 3)
        arrive(lead_weight, "lead_weight", 0)
        arrive(lead_slope, "lead_slope", 0)
        arrive(lead_code, "lead_code", 0)
        last_grid, last_inverse, last_latent, last_active = forward(code, lead_weight[...])
        last = (lead_slope[...] * silu_slope(last_latent)).astype(bf16)
        scaled_out[...] = scale_latent(last, last_inverse)
        hop("third", scaled_out, scaled, "scaled", 3)
        turn = backward(
            lead_code[...], last_grid, last_inverse, last_latent, last, lead_weight[...]
        )
        both = plain_dot(turn, weights[:, K:])
        d_latent = (both[:, C:] * silu_slope(latent)).astype(bf16)
        back = backward(both[:, 0:C], grid, inverse, latent, d_latent, weights[:, 0:K])
        back_out[...] = back
        hop("third", back_out, back_in, "back", 1)
        turn_out[...] = turn
        hop("third", turn_out, back_in, "back", 3)
        factor[...] = last_active
        arrive(active_in, "active", 0)
        up_part[...] = left_dot(back, active_in[...]).astype(bf16).reshape(up_part.shape)
        spread(lambda peer: up_part.at[peer], up_parts, "up_a", xy, xy_peers, pending_rest)
        down = left_dot(code_in[...], scale_latent(d_latent, inverse))
        down_part[...] = down.astype(bf16).reshape(down_part.shape)
        spread(lambda peer: down_part.at[peer], down_in, "down_a", z, z_peers, pending_rest)

    rest = sec != 0
    back_half = sec >= 2
    load_codec.wait()

    @pl.when(rest)
    def _():
        up_line[...] = gathered(up_part[xy], up_parts, "up_a", xy_peers).astype(bf16)
        spread(lambda peer: up_line, up_lines, "up_b", z, z_peers, pending_rest)

    @pl.when(jnp.logical_not(ends))
    def _():
        send_factor("lead")

    @pl.when(ends)
    def _():
        arrive(factor_in.at[xy], "factor", xy)
        value = left_dot(tok_half[y, x], factor_in[xy])
        for pxy, _ in xy_peers:
            arrive(wide_in.at[pxy], "wide", pxy)
            arrive(factor_in.at[pxy], "factor", pxy)
            value = value + left_dot(wide_in[pxy], factor_in[pxy])
        wide_part[...] = value.reshape(Z, own, K).astype(bf16)
        spread(lambda peer: wide_part.at[peer], wide_parts, "big", z, z_peers, pending_ends)

    @pl.when(rest)
    def _():
        down_block[...] = gathered(down_part[z], down_in, "down_a", z_peers).astype(bf16)
        spread(lambda peer: down_block, down_blocks, "down_b", xy, xy_peers, pending_rest)
        up_sum[xy] = gathered(up_line[...], up_lines, "up_b", z_peers).astype(bf16)

        @pl.when(sec == 1)
        def _():
            for pxy in [xy] + xy_ring:
                late.append(("second", up_line, sent[0]))
                start(up_sum.at[xy], up_sum.at[xy], "up_c", xy, sibling, pxy * Z + z)

        @pl.when(back_half)
        def _():
            spread(lambda peer: up_sum.at[xy], up_sum, "up_c", xy, xy_peers, pending_back)

        down_sum[z] = gathered(down_block[...], down_blocks, "down_b", xy_peers).astype(bf16)
        spread(lambda peer: down_sum.at[z], down_sum, "down_c", z, z_peers, pending_rest)

    @pl.when(back_half)
    def _():
        for pxy, _ in xy_peers:
            arrive(up_sum.at[pxy], "up_c", pxy)
        up_result[...] = plain_dot(codec[...], up_sum[...].reshape(C, K))
        hop("back_half", up_result, up_results, "up", sec - 1)

    own_rows = pl.ds(pl.multiple_of(dp * own, 8), own)

    def put_down(value):
        column = gain_col[own_rows, :]
        weighted = down32[own_rows, :] * value
        folded = weighted[:, 0 : min(step, K)]
        for k in range(step, K, step):
            folded = folded + weighted[:, k : k + step]
        if own < step:
            folded = jnp.concatenate([folded, jnp.zeros((step - own, folded.shape[1]), f32)], axis=0)
        out_gain[...] = jnp.sum(folded.T, axis=0, keepdims=True)[:, 0:own]
        for k in range(0, K, step):
            out_down[:, k : k + step] = value[:, k : k + step] * column[:, : min(step, K)]

    @pl.when(ends)
    def _():
        wide_sum[...] = gathered(wide_part[z], wide_parts, "big", z_peers)

    @pl.when(rest)
    def _():
        for pz, _ in z_peers:
            arrive(down_sum.at[pz], "down_c", pz)
        put_down(plain_dot(codec[...], down_sum[...].reshape(C, K)))

    @pl.when(sec == 0)
    def _():
        put_down(wide_sum[...])

    @pl.when(sec == 3)
    def _():
        out_up[...] = wide_sum[...]

    @pl.when(sec == 0)
    def _():
        for pxy in [xy] + xy_ring:
            arrive(up_sum.at[pxy], "up_c", pxy)
        out_up[...] = plain_dot(codec[...], up_sum[...].reshape(C, K))

    @pl.when(jnp.logical_not(ends))
    def _():
        arrive(up_results, "up", 0)
        out_up[...] = up_results[...]

    @pl.when(rest)
    def _():
        for landing, slot in pending_rest:
            left(landing.at[0], slot)

    @pl.when(ends)
    def _():
        for landing, slot in pending_ends:
            left(landing.at[0], slot)
        for off in range(XY - 1):
            left(wide_in.at[0], wide_slot + off)

    @pl.when(back_half)
    def _():
        for landing, slot in pending_back:
            left(landing.at[0], slot)

    groups = [("back_half", back_half), ("first", sec == 0), ("second", sec == 1), ("third", sec == 2), ("last", sec == 3)]
    groups += [("rest", rest), ("lead", jnp.logical_not(ends))]
    for group, chosen in groups:
        @pl.when(chosen)
        def _():
            for which, src, slot in late:
                if which == group:
                    left(src, slot)

    for copy in copies:
        copy.wait_send()


def hand_out(down, up, gain, out_down, out_up, out_gain, sem):
    copies = [
        pltpu.make_async_copy(down, out_down, sem.at[0]),
        pltpu.make_async_copy(up, out_up, sem.at[1]),
        pltpu.make_async_copy(gain, out_gain, sem.at[2]),
    ]
    for copy in copies:
        copy.start()
    for copy in copies:
        copy.wait()


def on_device(hidden_in, head_grad, down_w, up_w, norm_gain, codec):
    micro, rows, D = hidden_in.shape
    K, C, own = down_w.shape[3], codec.shape[1], codec.shape[0]
    Y, Z = y_size, z_size
    X = lax.axis_size("dp") // (Y * Z)
    R, chunk, lanes = micro * rows, D // X, C // 4
    block_rows = C // (X * Y)
    any_space = pl.BlockSpec(memory_space=pl.ANY)
    vmem = pl.BlockSpec(memory_space=pltpu.VMEM)
    recv_count = 5 * X + 8 * Z + 14 + 5 * X * Y
    scratch = [
        ((micro, rows, D), bf16),
        ((1, D), f32),
        ((own, C), bf16),
        ((D, K), bf16),
        ((Y, D // Y, K), bf16),
        ((D, K), f32),
        ((D, 128), f32),
        ((Y, D // Y, K), bf16),
        ((4, X, Y, Z, own, lanes), bf16),
        ((D // Y, C), bf16),
        ((Y, X, R, chunk // Y), bf16),
        ((Y, X, R, chunk // Y), bf16),
        ((C, 2 * K + C), f32),
        ((C, 2 * K + C), bf16),
        ((R, C), f32),
        ((R, K), f32),
        ((R, K), bf16),
        ((R, 1), f32),
        ((R, K), f32),
        ((R, C), bf16),
        ((R, C), bf16),
        ((R, C), bf16),
        ((R, C), bf16),
        ((R, C), bf16),
        ((R, K), bf16),
        ((R, K), bf16),
        ((C, K), bf16),
        ((R, K), f32),
        ((R, C), f32),
        ((R, K), bf16),
        ((X * Y, R, chunk // Y), bf16),
        ((R, K), bf16),
        ((X * Y, R, K), bf16),
        ((Z, own, K), bf16),
        ((Z, own, K), bf16),
        ((own, K), f32),
        ((Z, C // Z, K), bf16),
        ((Z, C // Z, K), bf16),
        ((C // Z, K), bf16),
        ((X * Y, C // Z, K), bf16),
        ((Z, C // Z, K), bf16),
        ((X * Y, block_rows, K), bf16),
        ((X * Y, block_rows, K), bf16),
        ((block_rows, K), bf16),
        ((Z, block_rows, K), bf16),
        ((X * Y, block_rows, K), bf16),
        ((own, K), f32),
        ((own, K), f32),
    ]
    sum_down, sum_up, sum_gain = pl.pallas_call(
        functools.partial(kernel, (X, Y, Z)),
        out_shape=(
            jax.ShapeDtypeStruct((own, K), f32),
            jax.ShapeDtypeStruct((own, K), f32),
            jax.ShapeDtypeStruct((1, own), f32),
        ),
        in_specs=[any_space] * 6,
        out_specs=(vmem, vmem, vmem),
        scratch_shapes=[pltpu.VMEM(shape, kind) for shape, kind in scratch]
        + [
            pltpu.SemaphoreType.DMA((21,)),
            pltpu.SemaphoreType.DMA((160,)),
            pltpu.SemaphoreType.DMA((recv_count,)),
        ],
        compiler_params=pltpu.CompilerParams(
            collective_id=0, has_side_effects=True, vmem_limit_bytes=56 * 1024 * 1024
        ),
    )(hidden_in, head_grad, down_w[0, 0], up_w[0, 0], norm_gain[0], codec)
    sum_down, sum_up, sum_gain = pl.pallas_call(
        hand_out,
        out_shape=(
            jax.ShapeDtypeStruct((own, K), f32),
            jax.ShapeDtypeStruct((own, K), f32),
            jax.ShapeDtypeStruct((1, own), f32),
        ),
        in_specs=[any_space] * 3,
        out_specs=(any_space,) * 3,
        scratch_shapes=[pltpu.SemaphoreType.DMA((3,))],
    )(sum_down, sum_up, sum_gain)
    return (sum_down[None, None], sum_up[None, None], sum_gain[None])


def solution(mesh):
    in_specs = (
        P(None, "dp", None),
        P(None, "dp", None),
        P("section", None, None, None),
        P("section", None, None, None),
        P("section", None, None),
        P("dp", None),
    )
    out_specs = (
        P("section", None, "dp", None),
        P("section", None, "dp", None),
        P("section", None, "dp"),
    )
    return jax.shard_map(
        on_device, mesh=mesh, in_specs=in_specs, out_specs=out_specs, check_vma=False
    )
```

```python
import functools

import jax
import jax.numpy as jnp
from jax import lax
from jax.experimental import pallas as pl
from jax.experimental.pallas import tpu as pltpu
from jax.sharding import PartitionSpec as P

epsilon = 1e-06
y_size, z_size = 2, 8
f32, bf16 = jnp.float32, jnp.bfloat16
mesh_ids = pl.DeviceIdType.MESH


def plain_dot(left, right):
    return lax.dot_general(left, right, (((1,), (0,)), ((), ())), preferred_element_type=f32)


def right_dot(left, right):
    return lax.dot_general(left, right, (((1,), (1,)), ((), ())), preferred_element_type=f32)


def left_dot(left, right):
    return lax.dot_general(left, right, (((0,), (0,)), ((), ())), preferred_element_type=f32)


def sigmoid(value):
    return 1.0 / (1.0 + jnp.exp(-value))


def silu_slope(latent):
    gate = sigmoid(latent)
    return gate * (1.0 + latent * (1.0 - gate))


def kernel(
    sizes,
    hidden,
    head,
    down_hbm,
    up_hbm,
    gain_hbm,
    codec_hbm,
    out_down,
    out_up,
    out_gain,
    tok,
    gain,
    codec,
    down,
    up_half,
    down32,
    gain_col,
    gdown_half,
    planes,
    flat,
    tok_half,
    out_half,
    acc,
    weights,
    tok_code,
    latent_ref,
    active_ref,
    inv_ref,
    slope_ref,
    code_in,
    code_out,
    back_in,
    back_out,
    turn_out,
    scaled_out,
    scaled,
    lead_weight,
    lead_slope,
    lead_code,
    active_in,
    wide_in,
    factor,
    factor_in,
    wide_part,
    wide_parts,
    wide_sum,
    down_part,
    down_in,
    down_block,
    down_blocks,
    down_sum,
    up_part,
    up_parts,
    up_line,
    up_lines,
    up_sum,
    up_result,
    up_results,
    local_sem,
    send_sem,
    recv_sem,
):
    X, Y, Z = sizes
    micro, rows, D = hidden.shape
    R = micro * rows
    C, K = codec.shape[1], down.shape[1]
    own = codec.shape[0]
    y_part = D // (X * Y)
    lanes = C // 4
    chunk = D // X
    ratio = D / C
    sec = lax.axis_index("section")
    dp = lax.axis_index("dp")
    core = lax.rem(sec, 2)
    x = dp // (Y * Z)
    y = lax.rem(dp // Z, Y)
    z = lax.rem(dp, Z)
    xy = dp // Z
    other_y = 1 - y
    far_sec = lax.rem(sec + 2, 4)
    sibling = sec + 1 - 2 * core
    ends = jnp.logical_or(sec == 0, sec == 3)

    def place(px, py, pz):
        return (px * Y + py) * Z + pz

    def ring(mine, count):
        return [lax.rem(mine + off, count) for off in range(1, count)]

    def near_first(mine, count):
        offsets = sorted(range(1, count), key=lambda off: (min(off, count - off), off))
        return [lax.rem(mine + off, count) for off in offsets]

    names = [
        ("x0", X), ("z0", Z), ("y0", Z), ("z1", Z), ("y1", 2), ("x1a", X), ("x1b", X),
        ("z4", 2), ("d0", 1), ("d0z", Z), ("d1a", X), ("d1b", X), ("code", 1), ("back", 1), ("active", 1), ("up", 1),
        ("scaled", 1), ("lead_weight", 1), ("lead_slope", 1), ("lead_code", 1),
        ("wide", X * Y), ("factor", X * Y), ("big", Z), ("down_a", Z), ("down_b", X * Y),
        ("down_c", Z), ("up_a", X * Y), ("up_b", Z), ("up_c", X * Y),
    ]
    base, total = {}, 0
    for name, count in names:
        base[name] = total
        total += count
    sent = [0]

    def start(src, dst, name, index, section, place_at, slot=None):
        if slot is None:
            slot = sent[0]
            sent[0] += 1
        copy = pltpu.make_async_remote_copy(
            src_ref=src, dst_ref=dst, send_sem=send_sem.at[slot],
            recv_sem=recv_sem.at[base[name] + index],
            device_id=(section, place_at), device_id_type=mesh_ids,
        )
        copy.start()
        return copy

    def left(src, slot):
        pltpu.make_async_remote_copy(
            src_ref=src, dst_ref=src, send_sem=send_sem.at[slot], recv_sem=recv_sem.at[0],
            device_id=(sec, dp), device_id_type=mesh_ids,
        ).wait_send()

    def arrive(dst, name, index):
        pltpu.make_async_remote_copy(
            src_ref=dst, dst_ref=dst, send_sem=send_sem.at[0],
            recv_sem=recv_sem.at[base[name] + index],
            device_id=(sec, dp), device_id_type=mesh_ids,
        ).wait_recv()

    barrier = pltpu.get_barrier_semaphore()
    peers = [(sec, place(x, y, pz)) for pz in ring(z, Z)]
    xy_ring = ring(xy, X * Y)
    peers += [(which, pxy * Z + z) for which in (sec, sibling) for pxy in xy_ring]
    peers += [(sibling, dp), (far_sec, place(x, other_y, z)), (3 - sec, dp)]
    for peer in peers:
        pl.semaphore_signal(barrier, inc=1, device_id=peer, device_id_type=mesh_ids)

    color0, color1 = 2 * core, 2 * core + 1
    loads = []

    def load(src, dst):
        copy = pltpu.make_async_copy(src, dst, local_sem.at[len(loads)])
        loads.append(copy)
        copy.start()
        return copy

    own_loads = []
    for color in (color0, color1):
        columns = pl.ds(pl.multiple_of(color * lanes, lanes), lanes)
        own_loads.append(load(codec_hbm.at[:, columns], planes.at[color, x, y, z]))
    load_tok = pltpu.make_async_copy(hidden, tok, local_sem.at[20])
    pl.when(sec == 0)(load_tok.start)
    pl.when(sec == 3)(pltpu.make_async_copy(head, tok, local_sem.at[20]).start)
    load_down = load(down_hbm, down)
    load_ups = [
        load(
            up_hbm.at[pl.ds(index * chunk + py * y_part, y_part)],
            up_half.at[py, pl.ds(index * y_part, y_part)],
        )
        for py in range(Y)
        for index in range(X)
    ]
    load_gain = load(gain_hbm, gain)
    load_codec = load(codec_hbm, codec)

    pl.semaphore_wait(barrier, len(peers))
    for copy in own_loads:
        copy.wait()

    half_z = Z // 2
    copies = []
    mine = planes.at[color0, x, y, z]
    for px in near_first(x, X)[::-1]:
        copies.append(start(mine, mine, "x0", x, sec, place(px, y, z)))
    mine = planes.at[color1, x, y, z]
    for pz in near_first(z, Z):
        copies.append(start(mine, mine, "z1", z, sec, place(x, y, pz)))

    wide_slot = sent[0]
    sent[0] += X * Y - 1
    wide_peers = [(px, y) for px in ring(x, X)] + [(px, other_y) for px in [x] + ring(x, X)]

    @pl.when(ends)
    def _():
        load_tok.wait()

        def split(index, carry):
            at = pl.ds(pl.multiple_of(index * chunk, chunk), chunk)
            value = tok[:, :, at].reshape(R, chunk)
            for py in range(Y):
                tok_half[py, index] = value[:, py * y_part : (py + 1) * y_part]
            return carry

        lax.fori_loop(0, X, split, 0)
        for off, (px, py) in enumerate(wide_peers):
            start(
                tok_half.at[py, px], wide_in.at[xy], "wide", xy, sec, place(px, py, z),
                wide_slot + off,
            )

    for px in ring(x, X):
        arrive(planes.at[color0, px, y, z], "x0", px)

    def line(pz):
        return planes.at[color0, :, y, pz]

    def pass_y(index, pz):
        block = line(pz)
        section = sec if index % 2 == 0 else far_sec
        copies.append(start(block, block, "y0", pz, section, place(x, other_y, z)))

    def along(steps):
        return lax.rem(z + Z + steps, Z)

    def send_line(block, pz, steps):
        copies.append(start(block, block, "z0", pz, sec, place(x, y, along(steps))))

    for steps in (1, -1, 2, -2):
        send_line(line(z), z, steps)
    pass_y(0, z)

    load_down.wait()
    load_gain.wait()
    for copy in load_ups:
        copy.wait()

    @pl.when(sec == 0)
    def _():
        def squares(index, carry):
            at = pl.ds(pl.multiple_of(index * chunk, chunk), chunk)
            value = tok[:, :, at].reshape(R, chunk).astype(f32)
            return carry + jnp.sum(value * value, axis=-1, keepdims=True)

        square = lax.fori_loop(0, X, squares, jnp.zeros((R, 1), f32))
        inverse = lax.rsqrt(square / D + epsilon)
        inv_ref[...] = inverse

        def project(index, carry):
            at = pl.ds(pl.multiple_of(index * chunk, chunk), chunk)
            value = tok[:, :, at].reshape(R, chunk).astype(f32)
            normed = (value * inverse * gain[:, at]).astype(bf16)
            return carry + plain_dot(normed, down[at, :])

        latent = lax.fori_loop(0, X, project, jnp.zeros((R, K), f32))
        active_ref[...] = (latent * sigmoid(latent)).astype(bf16)
        slope_ref[...] = silu_slope(latent)
        for py in range(Y):
            for index in range(X):
                rows_at = pl.ds(index * y_part, y_part)
                value = right_dot(active_ref[...], up_half[py, rows_at, :])
                value = value + tok_half[py, index].astype(f32)
                out_half[py, index] = value.astype(bf16)

    @pl.when(sec == 3)
    def _():
        value = jnp.zeros((R, K), f32)
        for py in range(Y):
            for index in range(X):
                rows_at = pl.ds(index * y_part, y_part)
                value = value + plain_dot(tok_half[py, index], up_half[py, rows_at, :])
        latent_ref[...] = value

    for pz in ring(z, Z):
        arrive(planes.at[color1, x, y, pz], "z1", pz)
    near, far = planes.at[color1, x, y, 0:half_z], planes.at[color1, x, y, half_z:Z]
    copies.append(start(near, near, "y1", 0, sec, place(x, other_y, z)))
    copies.append(start(far, far, "y1", 1, far_sec, place(x, other_y, z)))
    slab = planes.at[color1, x, y]
    for px in near_first(x, X)[::-1]:
        copies.append(start(slab, slab, "x1a", x, sec, place(px, y, z)))
    copies.append(start(slab, slab, "d1a", x, sibling, dp))

    step = 128

    def scale_rows(index, carry):
        at = pl.ds(pl.multiple_of(index * chunk, chunk), chunk)
        column = jnp.broadcast_to(gain[:, at], (step, chunk)).T
        gain_col[at, :] = column
        wide = down[at, :].astype(f32)
        down32[at, :] = wide
        parts = [wide[:, k : k + step] * column[:, : min(step, K)] for k in range(0, K, step)]
        scaled = jnp.concatenate(parts, axis=1).astype(bf16)
        rows_at = pl.ds(pl.multiple_of(index * y_part, y_part), y_part)
        for py in range(Y):
            gdown_half[py, rows_at, :] = scaled[py * y_part : (py + 1) * y_part]
        return carry

    def scale():
        lax.fori_loop(0, X, scale_rows, 0)

    order = [along(steps) for steps in (1, -1, 2, -2, 3, -3, 4)]
    half_x = X // 2
    for index, pz in enumerate(order[0:2]):
        arrive(line(pz), "z0", pz)
        pass_y(index + 1, pz)
    for index, way in enumerate((1, -1)):
        pz = along(2 * way)
        arrive(line(pz), "z0", pz)
        send_line(line(pz), pz, -way)
        part = planes.at[color0, 0:half_x, y, pz] if way > 0 else planes.at[color0, half_x:X, y, pz]
        copies.append(
            start(part, part, "z4", index, sec, place(x, y, along(-2 * way)))
        )
        pass_y(index + 3, pz)
    arrive(planes.at[color1, x, other_y, 0:half_z], "y1", 0)
    arrive(planes.at[color1, x, other_y, half_z:Z], "y1", 1)
    slab = planes.at[color1, x, other_y]
    for px in near_first(x, X)[::-1]:
        copies.append(start(slab, slab, "x1b", x, sec, place(px, y, z)))
    copies.append(start(slab, slab, "d1b", x, sibling, dp))
    pl.when(sec != 0)(scale)
    for index, pz in enumerate(order[4:6]):
        arrive(line(pz), "z0", pz)
        pass_y(index + 5, pz)
    arrive(planes.at[color0, 0:half_x, y, order[6]], "z4", 0)
    arrive(planes.at[color0, half_x:X, y, order[6]], "z4", 1)
    pass_y(7, order[6])
    half = planes.at[color0, :, y]
    copies.append(start(half, half, "d0", 0, sibling, dp))
    for px in ring(x, X):
        slab = planes.at[color1, px, y]
        arrive(slab, "x1a", px)
        copies.append(start(slab, slab, "d1a", px, sibling, dp))

    late = []

    def hop(group, src, dst, name, section):
        late.append((group, src, sent[0]))
        start(src, dst, name, 0, section, dp)

    their0, their1 = 2 - 2 * core, 3 - 2 * core
    def products(py, add, last):
        for index in range(X):
            for color in range(4):
                piece = planes[color, index, py].astype(f32).reshape(y_part, lanes).astype(bf16)
                rows_at = slice(index * y_part, (index + 1) * y_part)
                flat[rows_at, color * lanes : (color + 1) * lanes] = piece

        def wide_code(rows):
            value = jnp.zeros((R, C), f32)
            for index in range(X):
                rows_at = slice(index * y_part, (index + 1) * y_part)
                value = value + plain_dot(rows[py, index], flat[rows_at, :])
            add(tok_code, slice(0, C), value)

        pl.when(sec == 0)(lambda: wide_code(out_half))
        if last:
            @pl.when(sec == 0)
            def _():
                code_out[...] = tok_code[...].astype(bf16)
                hop("first", code_out, code_in, "code", 1)
                hop("first", active_ref, active_in, "active", 1)

        @pl.when(sec != 3)
        def _():
            add(acc, slice(K + C, K + C + K), left_dot(flat[...], up_half[py]))

        pl.when(sec == 3)(lambda: wide_code(tok_half))

        @pl.when(sec != 0)
        def _():
            add(acc, slice(0, K), left_dot(flat[...], gdown_half[py]))
            add(acc, slice(K, K + C), left_dot(flat[...], flat[...]))

    def put(ref, columns, value):
        ref[:, columns] = value

    def add_to(ref, columns, value):
        ref[:, columns] += value

    arrive(planes.at[their0, :, y], "d0", 0)
    arrive(planes.at[their1, x, y], "d1a", x)
    for px in ring(x, X):
        arrive(planes.at[their1, px, y], "d1a", px)
    products(y, put, False)

    for pz in [z] + order:
        block = planes.at[color0, :, other_y, pz]
        arrive(block, "y0", pz)
        copies.append(start(block, block, "d0z", pz, sibling, dp))
    for px in ring(x, X):
        slab = planes.at[color1, px, other_y]
        arrive(slab, "x1b", px)
        copies.append(start(slab, slab, "d1b", px, sibling, dp))

    for pz in [z] + order:
        arrive(planes.at[their0, :, other_y, pz], "d0z", pz)
    arrive(planes.at[their1, x, other_y], "d1b", x)
    for px in ring(x, X):
        arrive(planes.at[their1, px, other_y], "d1b", px)

    products(other_y, add_to, True)

    @pl.when(sec != 3)
    def _():
        weights[:, K + C :] = acc[:, K + C :].astype(bf16)

    @pl.when(sec != 0)
    def _():
        weights[:, 0 : K + C] = acc[:, 0 : K + C].astype(bf16)

    XY = X * Y
    def forward(code, weight):
        grid = plain_dot(code, weights[:, K : K + C])
        square = jnp.sum(code.astype(f32) * grid, axis=-1, keepdims=True) * (ratio * ratio / D)
        inverse = lax.rsqrt(jnp.maximum(square, 0.0) + epsilon)
        latent = ratio * inverse * plain_dot(code, weight)
        active = (latent * sigmoid(latent)).astype(bf16)
        return grid, inverse, latent, active

    def backward(inner, grid, inverse, latent, d_latent, weight):
        share = jnp.sum(d_latent.astype(f32) * latent, axis=-1, keepdims=True)
        share = share * inverse * inverse * (ratio / D)
        through = right_dot(d_latent, weight)
        return (ratio * (inner + inverse * through - share * grid)).astype(bf16)

    def next_code(grid, active):
        return (ratio * grid + right_dot(active, weights[:, K + C :])).astype(bf16)

    def scale_latent(d_latent, inverse):
        return (d_latent.astype(f32) * (ratio * inverse)).astype(bf16)

    def send_factor(name):
        for pxy in [xy] + xy_ring:
            late.append((name, factor, sent[0]))
            start(factor, factor_in.at[xy], "factor", xy, sibling, pxy * Z + z)

    far_x = sorted(range(X), key=lambda off: -min(off, X - off))
    xy_far = [(lax.rem(x + off, X), other_y) for off in far_x]
    xy_far += [(lax.rem(x + off, X), y) for off in far_x[:-1]]
    xy_peers = [(px * Y + py, place(px, py, z)) for px, py in xy_far]
    z_peers = [(pz, place(x, y, pz)) for pz in near_first(z, Z)[::-1]]
    pending_rest, pending_ends, pending_back, first_slot = [], [], [], {}

    def spread(ref_of, landings, name, mine, peers, pending):
        if name not in first_slot:
            first_slot[name] = sent[0]
            sent[0] += len(peers)
            pending.extend((landings, first_slot[name] + n) for n in range(len(peers)))
        for n, (peer, peer_dp) in enumerate(peers):
            start(
                ref_of(peer), landings.at[mine], name, mine, sec, peer_dp, first_slot[name] + n
            )

    def gathered(first, landing, name, peers):
        value = first.astype(f32)
        for peer, _ in peers:
            arrive(landing.at[peer], name, peer)
            value = value + landing[peer].astype(f32)
        return value

    @pl.when(sec == 0)
    def _():
        latent_ref[...] = slope_ref[...] * inv_ref[...]
        hop("first", weights.at[:, K + C :], lead_weight, "lead_weight", 1)
        hop("first", latent_ref, lead_slope, "lead_slope", 1)
        scale()

    @pl.when(sec == 3)
    def _():
        hop("last", weights.at[:, 0:K], lead_weight, "lead_weight", 2)
        hop("last", latent_ref, lead_slope, "lead_slope", 2)
        hop("last", tok_code, lead_code, "lead_code", 2)
        arrive(code_in, "code", 0)
        arrive(scaled, "scaled", 0)
        down_part[...] = left_dot(code_in[...], scaled[...]).astype(bf16).reshape(down_part.shape)
        spread(lambda peer: down_part.at[peer], down_in, "down_a", z, z_peers, pending_rest)
        arrive(active_in, "active", 0)
        arrive(back_in, "back", 0)
        up_part[...] = left_dot(back_in[...], active_in[...]).astype(bf16).reshape(up_part.shape)
        spread(lambda peer: up_part.at[peer], up_parts, "up_a", xy, xy_peers, pending_rest)

    @pl.when(sec == 1)
    def _():
        arrive(code_in, "code", 0)
        grid, inverse, latent, active = forward(code_in[...], weights[:, 0:K])
        code_out[...] = next_code(grid, active)
        hop("second", code_out, code_in, "code", 2)
        active_ref[...] = active
        hop("second", active_ref, active_in, "active", 2)
        slope = silu_slope(latent)
        arrive(lead_weight, "lead_weight", 0)
        arrive(lead_slope, "lead_slope", 0)
        arrive(active_in, "active", 0)
        arrive(back_in, "back", 0)
        both = plain_dot(back_in[...], weights[:, K:])
        d_latent = (both[:, C:] * slope).astype(bf16)
        back = backward(both[:, 0:C], grid, inverse, latent, d_latent, weights[:, 0:K])
        up_part[...] = left_dot(back, active_in[...]).astype(bf16).reshape(up_part.shape)
        spread(lambda peer: up_part.at[peer], up_parts, "up_a", xy, xy_peers, pending_rest)
        down = left_dot(code_in[...], scale_latent(d_latent, inverse))
        down_part[...] = down.astype(bf16).reshape(down_part.shape)
        spread(lambda peer: down_part.at[peer], down_in, "down_a", z, z_peers, pending_rest)
        factor[...] = (plain_dot(back, lead_weight[...]) * lead_slope[...]).astype(bf16)

    @pl.when(sec == 2)
    def _():
        arrive(code_in, "code", 0)
        grid, inverse, latent, active = forward(code_in[...], weights[:, 0:K])
        code = next_code(grid, active)
        code_out[...] = code
        hop("third", code_out, code_in, "code", 3)
        active_ref[...] = active
        hop("third", active_ref, active_in, "active", 3)
        arrive(lead_weight, "lead_weight", 0)
        arrive(lead_slope, "lead_slope", 0)
        arrive(lead_code, "lead_code", 0)
        last_grid, last_inverse, last_latent, last_active = forward(code, lead_weight[...])
        last = (lead_slope[...] * silu_slope(last_latent)).astype(bf16)
        scaled_out[...] = scale_latent(last, last_inverse)
        hop("third", scaled_out, scaled, "scaled", 3)
        turn = backward(
            lead_code[...], last_grid, last_inverse, last_latent, last, lead_weight[...]
        )
        both = plain_dot(turn, weights[:, K:])
        d_latent = (both[:, C:] * silu_slope(latent)).astype(bf16)
        back = backward(both[:, 0:C], grid, inverse, latent, d_latent, weights[:, 0:K])
        back_out[...] = back
        hop("third", back_out, back_in, "back", 1)
        turn_out[...] = turn
        hop("third", turn_out, back_in, "back", 3)
        factor[...] = last_active
        arrive(active_in, "active", 0)
        up_part[...] = left_dot(back, active_in[...]).astype(bf16).reshape(up_part.shape)
        spread(lambda peer: up_part.at[peer], up_parts, "up_a", xy, xy_peers, pending_rest)
        down = left_dot(code_in[...], scale_latent(d_latent, inverse))
        down_part[...] = down.astype(bf16).reshape(down_part.shape)
        spread(lambda peer: down_part.at[peer], down_in, "down_a", z, z_peers, pending_rest)

    rest = sec != 0
    back_half = sec >= 2
    load_codec.wait()

    @pl.when(rest)
    def _():
        up_line[...] = gathered(up_part[xy], up_parts, "up_a", xy_peers).astype(bf16)
        spread(lambda peer: up_line, up_lines, "up_b", z, z_peers, pending_rest)

    @pl.when(jnp.logical_not(ends))
    def _():
        send_factor("lead")

    @pl.when(ends)
    def _():
        arrive(factor_in.at[xy], "factor", xy)
        value = left_dot(tok_half[y, x], factor_in[xy])
        for pxy, _ in xy_peers:
            arrive(wide_in.at[pxy], "wide", pxy)
            arrive(factor_in.at[pxy], "factor", pxy)
            value = value + left_dot(wide_in[pxy], factor_in[pxy])
        wide_part[...] = value.reshape(Z, own, K).astype(bf16)
        spread(lambda peer: wide_part.at[peer], wide_parts, "big", z, z_peers, pending_ends)

    @pl.when(rest)
    def _():
        down_block[...] = gathered(down_part[z], down_in, "down_a", z_peers).astype(bf16)
        spread(lambda peer: down_block, down_blocks, "down_b", xy, xy_peers, pending_rest)
        up_sum[xy] = gathered(up_line[...], up_lines, "up_b", z_peers).astype(bf16)

        @pl.when(sec == 1)
        def _():
            for pxy in [xy] + xy_ring:
                late.append(("second", up_line, sent[0]))
                start(up_sum.at[xy], up_sum.at[xy], "up_c", xy, sibling, pxy * Z + z)

        @pl.when(back_half)
        def _():
            spread(lambda peer: up_sum.at[xy], up_sum, "up_c", xy, xy_peers, pending_back)

        down_sum[z] = gathered(down_block[...], down_blocks, "down_b", xy_peers).astype(bf16)
        spread(lambda peer: down_sum.at[z], down_sum, "down_c", z, z_peers, pending_rest)

    @pl.when(back_half)
    def _():
        for pxy, _ in xy_peers:
            arrive(up_sum.at[pxy], "up_c", pxy)
        up_result[...] = plain_dot(codec[...], up_sum[...].reshape(C, K))
        hop("back_half", up_result, up_results, "up", sec - 1)

    own_rows = pl.ds(pl.multiple_of(dp * own, 8), own)

    def put_down(value):
        column = gain_col[own_rows, :]
        weighted = down32[own_rows, :] * value
        folded = weighted[:, 0 : min(step, K)]
        for k in range(step, K, step):
            folded = folded + weighted[:, k : k + step]
        if own < step:
            folded = jnp.concatenate([folded, jnp.zeros((step - own, folded.shape[1]), f32)], axis=0)
        out_gain[...] = jnp.sum(folded.T, axis=0, keepdims=True)[:, 0:own]
        for k in range(0, K, step):
            out_down[:, k : k + step] = value[:, k : k + step] * column[:, : min(step, K)]

    @pl.when(ends)
    def _():
        wide_sum[...] = gathered(wide_part[z], wide_parts, "big", z_peers)

    @pl.when(rest)
    def _():
        for pz, _ in z_peers:
            arrive(down_sum.at[pz], "down_c", pz)
        put_down(plain_dot(codec[...], down_sum[...].reshape(C, K)))

    @pl.when(sec == 0)
    def _():
        put_down(wide_sum[...])

    @pl.when(sec == 3)
    def _():
        out_up[...] = wide_sum[...]

    @pl.when(sec == 0)
    def _():
        for pxy in [xy] + xy_ring:
            arrive(up_sum.at[pxy], "up_c", pxy)
        out_up[...] = plain_dot(codec[...], up_sum[...].reshape(C, K))

    @pl.when(jnp.logical_not(ends))
    def _():
        arrive(up_results, "up", 0)
        out_up[...] = up_results[...]

    @pl.when(rest)
    def _():
        for landing, slot in pending_rest:
            left(landing.at[0], slot)

    @pl.when(ends)
    def _():
        for landing, slot in pending_ends:
            left(landing.at[0], slot)
        for off in range(XY - 1):
            left(wide_in.at[0], wide_slot + off)

    @pl.when(back_half)
    def _():
        for landing, slot in pending_back:
            left(landing.at[0], slot)

    groups = [("back_half", back_half), ("first", sec == 0), ("second", sec == 1), ("third", sec == 2), ("last", sec == 3)]
    groups += [("rest", rest), ("lead", jnp.logical_not(ends))]
    for group, chosen in groups:
        @pl.when(chosen)
        def _():
            for which, src, slot in late:
                if which == group:
                    left(src, slot)

    for copy in copies:
        copy.wait_send()


def hand_out(down, up, gain, out_down, out_up, out_gain, sem):
    copies = [
        pltpu.make_async_copy(down, out_down, sem.at[0]),
        pltpu.make_async_copy(up, out_up, sem.at[1]),
        pltpu.make_async_copy(gain, out_gain, sem.at[2]),
    ]
    for copy in copies:
        copy.start()
    for copy in copies:
        copy.wait()


def on_device(hidden_in, head_grad, down_w, up_w, norm_gain, codec):
    micro, rows, D = hidden_in.shape
    K, C, own = down_w.shape[3], codec.shape[1], codec.shape[0]
    Y, Z = y_size, z_size
    X = lax.axis_size("dp") // (Y * Z)
    R, chunk, lanes = micro * rows, D // X, C // 4
    block_rows = C // (X * Y)
    any_space = pl.BlockSpec(memory_space=pl.ANY)
    vmem = pl.BlockSpec(memory_space=pltpu.VMEM)
    recv_count = 5 * X + 8 * Z + 14 + 5 * X * Y
    scratch = [
        ((micro, rows, D), bf16),
        ((1, D), f32),
        ((own, C), bf16),
        ((D, K), bf16),
        ((Y, D // Y, K), bf16),
        ((D, K), f32),
        ((D, 128), f32),
        ((Y, D // Y, K), bf16),
        ((4, X, Y, Z, own, lanes), bf16),
        ((D // Y, C), bf16),
        ((Y, X, R, chunk // Y), bf16),
        ((Y, X, R, chunk // Y), bf16),
        ((C, 2 * K + C), f32),
        ((C, 2 * K + C), bf16),
        ((R, C), f32),
        ((R, K), f32),
        ((R, K), bf16),
        ((R, 1), f32),
        ((R, K), f32),
        ((R, C), bf16),
        ((R, C), bf16),
        ((R, C), bf16),
        ((R, C), bf16),
        ((R, C), bf16),
        ((R, K), bf16),
        ((R, K), bf16),
        ((C, K), bf16),
        ((R, K), f32),
        ((R, C), f32),
        ((R, K), bf16),
        ((X * Y, R, chunk // Y), bf16),
        ((R, K), bf16),
        ((X * Y, R, K), bf16),
        ((Z, own, K), bf16),
        ((Z, own, K), bf16),
        ((own, K), f32),
        ((Z, C // Z, K), bf16),
        ((Z, C // Z, K), bf16),
        ((C // Z, K), bf16),
        ((X * Y, C // Z, K), bf16),
        ((Z, C // Z, K), bf16),
        ((X * Y, block_rows, K), bf16),
        ((X * Y, block_rows, K), bf16),
        ((block_rows, K), bf16),
        ((Z, block_rows, K), bf16),
        ((X * Y, block_rows, K), bf16),
        ((own, K), f32),
        ((own, K), f32),
    ]
    sum_down, sum_up, sum_gain = pl.pallas_call(
        functools.partial(kernel, (X, Y, Z)),
        out_shape=(
            jax.ShapeDtypeStruct((own, K), f32),
            jax.ShapeDtypeStruct((own, K), f32),
            jax.ShapeDtypeStruct((1, own), f32),
        ),
        in_specs=[any_space] * 6,
        out_specs=(vmem, vmem, vmem),
        scratch_shapes=[pltpu.VMEM(shape, kind) for shape, kind in scratch]
        + [
            pltpu.SemaphoreType.DMA((21,)),
            pltpu.SemaphoreType.DMA((160,)),
            pltpu.SemaphoreType.DMA((recv_count,)),
        ],
        compiler_params=pltpu.CompilerParams(
            collective_id=0, has_side_effects=True, vmem_limit_bytes=56 * 1024 * 1024
        ),
    )(hidden_in, head_grad, down_w[0, 0], up_w[0, 0], norm_gain[0], codec)
    sum_down, sum_up, sum_gain = pl.pallas_call(
        hand_out,
        out_shape=(
            jax.ShapeDtypeStruct((own, K), f32),
            jax.ShapeDtypeStruct((own, K), f32),
            jax.ShapeDtypeStruct((1, own), f32),
        ),
        in_specs=[any_space] * 3,
        out_specs=(any_space,) * 3,
        scratch_shapes=[pltpu.SemaphoreType.DMA((3,))],
    )(sum_down, sum_up, sum_gain)
    return (sum_down[None, None], sum_up[None, None], sum_gain[None])


def solution(mesh):
    in_specs = (
        P(None, "dp", None),
        P(None, "dp", None),
        P("section", None, None, None),
        P("section", None, None, None),
        P("section", None, None),
        P("dp", None),
    )
    out_specs = (
        P("section", None, "dp", None),
        P("section", None, "dp", None),
        P("section", None, "dp"),
    )
    return jax.shard_map(
        on_device, mesh=mesh, in_specs=in_specs, out_specs=out_specs, check_vma=False
    )
```

```python
import functools

import jax
import jax.numpy as jnp
from jax import lax
from jax.experimental import pallas as pl
from jax.experimental.pallas import tpu as pltpu
from jax.sharding import PartitionSpec as P

epsilon = 1e-06
y_size, z_size = 2, 8
f32, bf16 = jnp.float32, jnp.bfloat16
mesh_ids = pl.DeviceIdType.MESH


def plain_dot(left, right):
    return lax.dot_general(left, right, (((1,), (0,)), ((), ())), preferred_element_type=f32)


def right_dot(left, right):
    return lax.dot_general(left, right, (((1,), (1,)), ((), ())), preferred_element_type=f32)


def left_dot(left, right):
    return lax.dot_general(left, right, (((0,), (0,)), ((), ())), preferred_element_type=f32)


def sigmoid(value):
    return 1.0 / (1.0 + jnp.exp(-value))


def silu_slope(latent):
    gate = sigmoid(latent)
    return gate * (1.0 + latent * (1.0 - gate))


def kernel(
    sizes,
    hidden,
    head,
    down_hbm,
    up_hbm,
    gain_hbm,
    codec_hbm,
    out_down,
    out_up,
    out_gain,
    tok,
    gain,
    codec,
    down,
    up_half,
    down32,
    gain_col,
    gdown_half,
    planes,
    flat,
    tok_half,
    out_half,
    acc,
    weights,
    tok_code,
    latent_ref,
    active_ref,
    inv_ref,
    slope_ref,
    code_in,
    code_out,
    back_in,
    back_out,
    turn_out,
    scaled_out,
    scaled,
    lead_weight,
    lead_slope,
    lead_code,
    active_in,
    wide_in,
    factor,
    factor_in,
    wide_part,
    wide_parts,
    wide_sum,
    down_part,
    down_in,
    down_block,
    down_blocks,
    down_sum,
    up_part,
    up_parts,
    up_line,
    up_lines,
    up_sum,
    up_result,
    up_results,
    local_sem,
    send_sem,
    recv_sem,
):
    X, Y, Z = sizes
    micro, rows, D = hidden.shape
    R = micro * rows
    C, K = codec.shape[1], down.shape[1]
    own = codec.shape[0]
    y_part = D // (X * Y)
    lanes = C // 4
    chunk = D // X
    ratio = D / C
    sec = lax.axis_index("section")
    dp = lax.axis_index("dp")
    core = lax.rem(sec, 2)
    x = dp // (Y * Z)
    y = lax.rem(dp // Z, Y)
    z = lax.rem(dp, Z)
    xy = dp // Z
    other_y = 1 - y
    far_sec = lax.rem(sec + 2, 4)
    sibling = sec + 1 - 2 * core
    ends = jnp.logical_or(sec == 0, sec == 3)

    def place(px, py, pz):
        return (px * Y + py) * Z + pz

    def ring(mine, count):
        return [lax.rem(mine + off, count) for off in range(1, count)]

    def near_first(mine, count):
        offsets = sorted(range(1, count), key=lambda off: (min(off, count - off), off))
        return [lax.rem(mine + off, count) for off in offsets]

    names = [
        ("x0", X), ("z0", Z), ("y0", Z), ("z1", Z), ("y1", 2), ("x1a", X), ("x1b", X),
        ("z4", 2), ("d0", Z), ("d0z", Z), ("d1a", X), ("d1b", X), ("code", 1), ("back", 1), ("active", 1), ("up", 1),
        ("scaled", 1), ("lead_weight", 1), ("lead_slope", 1), ("lead_code", 1),
        ("wide", X * Y), ("factor", X * Y), ("big", Z), ("down_a", Z), ("down_b", X * Y),
        ("down_c", Z), ("up_a", X * Y), ("up_b", Z), ("up_c", X * Y),
    ]
    base, total = {}, 0
    for name, count in names:
        base[name] = total
        total += count
    sent = [0]

    def start(src, dst, name, index, section, place_at, slot=None):
        if slot is None:
            slot = sent[0]
            sent[0] += 1
        copy = pltpu.make_async_remote_copy(
            src_ref=src, dst_ref=dst, send_sem=send_sem.at[slot],
            recv_sem=recv_sem.at[base[name] + index],
            device_id=(section, place_at), device_id_type=mesh_ids,
        )
        copy.start()
        return copy

    def left(src, slot):
        pltpu.make_async_remote_copy(
            src_ref=src, dst_ref=src, send_sem=send_sem.at[slot], recv_sem=recv_sem.at[0],
            device_id=(sec, dp), device_id_type=mesh_ids,
        ).wait_send()

    def arrive(dst, name, index):
        pltpu.make_async_remote_copy(
            src_ref=dst, dst_ref=dst, send_sem=send_sem.at[0],
            recv_sem=recv_sem.at[base[name] + index],
            device_id=(sec, dp), device_id_type=mesh_ids,
        ).wait_recv()

    barrier = pltpu.get_barrier_semaphore()
    peers = [(sec, place(x, y, pz)) for pz in ring(z, Z)]
    xy_ring = ring(xy, X * Y)
    peers += [(which, pxy * Z + z) for which in (sec, sibling) for pxy in xy_ring]
    peers += [(sibling, dp), (far_sec, place(x, other_y, z)), (3 - sec, dp)]
    for peer in peers:
        pl.semaphore_signal(barrier, inc=1, device_id=peer, device_id_type=mesh_ids)

    color0, color1 = 2 * core, 2 * core + 1
    loads = []

    def load(src, dst):
        copy = pltpu.make_async_copy(src, dst, local_sem.at[len(loads)])
        loads.append(copy)
        copy.start()
        return copy

    own_loads = []
    for color in (color0, color1):
        columns = pl.ds(pl.multiple_of(color * lanes, lanes), lanes)
        own_loads.append(load(codec_hbm.at[:, columns], planes.at[color, x, y, z]))
    load_tok = pltpu.make_async_copy(hidden, tok, local_sem.at[20])
    pl.when(sec == 0)(load_tok.start)
    pl.when(sec == 3)(pltpu.make_async_copy(head, tok, local_sem.at[20]).start)
    load_down = load(down_hbm, down)
    load_ups = [
        load(
            up_hbm.at[pl.ds(index * chunk + py * y_part, y_part)],
            up_half.at[py, pl.ds(index * y_part, y_part)],
        )
        for py in range(Y)
        for index in range(X)
    ]
    load_gain = load(gain_hbm, gain)
    load_codec = load(codec_hbm, codec)

    pl.semaphore_wait(barrier, len(peers))
    for copy in own_loads:
        copy.wait()

    half_z = Z // 2
    copies = []
    mine = planes.at[color0, x, y, z]
    for px in near_first(x, X)[::-1]:
        copies.append(start(mine, mine, "x0", x, sec, place(px, y, z)))
    mine = planes.at[color1, x, y, z]
    for pz in near_first(z, Z):
        copies.append(start(mine, mine, "z1", z, sec, place(x, y, pz)))

    wide_slot = sent[0]
    sent[0] += X * Y - 1
    wide_peers = [(px, y) for px in ring(x, X)] + [(px, other_y) for px in [x] + ring(x, X)]

    @pl.when(ends)
    def _():
        load_tok.wait()

        def split(index, carry):
            at = pl.ds(pl.multiple_of(index * chunk, chunk), chunk)
            value = tok[:, :, at].reshape(R, chunk)
            for py in range(Y):
                tok_half[py, index] = value[:, py * y_part : (py + 1) * y_part]
            return carry

        lax.fori_loop(0, X, split, 0)
        for off, (px, py) in enumerate(wide_peers):
            start(
                tok_half.at[py, px], wide_in.at[xy], "wide", xy, sec, place(px, py, z),
                wide_slot + off,
            )

    for px in ring(x, X):
        arrive(planes.at[color0, px, y, z], "x0", px)

    def line(pz):
        return planes.at[color0, :, y, pz]

    def pass_y(index, pz):
        block = line(pz)
        section = sec if index % 2 == 0 else far_sec
        copies.append(start(block, block, "y0", pz, section, place(x, other_y, z)))
        copies.append(start(block, block, "d0", pz, sibling, dp))

    def along(steps):
        return lax.rem(z + Z + steps, Z)

    def send_line(block, pz, steps):
        copies.append(start(block, block, "z0", pz, sec, place(x, y, along(steps))))

    for steps in (1, -1, 2, -2):
        send_line(line(z), z, steps)
    pass_y(0, z)

    load_down.wait()
    load_gain.wait()
    for copy in load_ups:
        copy.wait()

    @pl.when(sec == 0)
    def _():
        def squares(index, carry):
            at = pl.ds(pl.multiple_of(index * chunk, chunk), chunk)
            value = tok[:, :, at].reshape(R, chunk).astype(f32)
            return carry + jnp.sum(value * value, axis=-1, keepdims=True)

        square = lax.fori_loop(0, X, squares, jnp.zeros((R, 1), f32))
        inverse = lax.rsqrt(square / D + epsilon)
        inv_ref[...] = inverse

        def project(index, carry):
            at = pl.ds(pl.multiple_of(index * chunk, chunk), chunk)
            value = tok[:, :, at].reshape(R, chunk).astype(f32)
            normed = (value * inverse * gain[:, at]).astype(bf16)
            return carry + plain_dot(normed, down[at, :])

        latent = lax.fori_loop(0, X, project, jnp.zeros((R, K), f32))
        active_ref[...] = (latent * sigmoid(latent)).astype(bf16)
        slope_ref[...] = silu_slope(latent)
        for py in range(Y):
            for index in range(X):
                rows_at = pl.ds(index * y_part, y_part)
                value = right_dot(active_ref[...], up_half[py, rows_at, :])
                value = value + tok_half[py, index].astype(f32)
                out_half[py, index] = value.astype(bf16)

    @pl.when(sec == 3)
    def _():
        value = jnp.zeros((R, K), f32)
        for py in range(Y):
            for index in range(X):
                rows_at = pl.ds(index * y_part, y_part)
                value = value + plain_dot(tok_half[py, index], up_half[py, rows_at, :])
        latent_ref[...] = value

    for pz in ring(z, Z):
        arrive(planes.at[color1, x, y, pz], "z1", pz)
    near, far = planes.at[color1, x, y, 0:half_z], planes.at[color1, x, y, half_z:Z]
    copies.append(start(near, near, "y1", 0, sec, place(x, other_y, z)))
    copies.append(start(far, far, "y1", 1, far_sec, place(x, other_y, z)))
    slab = planes.at[color1, x, y]
    for px in near_first(x, X)[::-1]:
        copies.append(start(slab, slab, "x1a", x, sec, place(px, y, z)))
    copies.append(start(slab, slab, "d1a", x, sibling, dp))

    step = 128

    def scale_rows(index, carry):
        at = pl.ds(pl.multiple_of(index * chunk, chunk), chunk)
        column = jnp.broadcast_to(gain[:, at], (step, chunk)).T
        gain_col[at, :] = column
        wide = down[at, :].astype(f32)
        down32[at, :] = wide
        parts = [wide[:, k : k + step] * column[:, : min(step, K)] for k in range(0, K, step)]
        scaled = jnp.concatenate(parts, axis=1).astype(bf16)
        rows_at = pl.ds(pl.multiple_of(index * y_part, y_part), y_part)
        for py in range(Y):
            gdown_half[py, rows_at, :] = scaled[py * y_part : (py + 1) * y_part]
        return carry

    def scale():
        lax.fori_loop(0, X, scale_rows, 0)

    order = [along(steps) for steps in (1, -1, 2, -2, 3, -3, 4)]
    half_x = X // 2
    for index, pz in enumerate(order[0:2]):
        arrive(line(pz), "z0", pz)
        pass_y(index + 1, pz)
    for index, way in enumerate((1, -1)):
        pz = along(2 * way)
        arrive(line(pz), "z0", pz)
        send_line(line(pz), pz, -way)
        part = planes.at[color0, 0:half_x, y, pz] if way > 0 else planes.at[color0, half_x:X, y, pz]
        copies.append(
            start(part, part, "z4", index, sec, place(x, y, along(-2 * way)))
        )
        pass_y(index + 3, pz)
    arrive(planes.at[color1, x, other_y, 0:half_z], "y1", 0)
    arrive(planes.at[color1, x, other_y, half_z:Z], "y1", 1)
    slab = planes.at[color1, x, other_y]
    for px in near_first(x, X)[::-1]:
        copies.append(start(slab, slab, "x1b", x, sec, place(px, y, z)))
    copies.append(start(slab, slab, "d1b", x, sibling, dp))
    pl.when(sec != 0)(scale)
    for index, pz in enumerate(order[4:6]):
        arrive(line(pz), "z0", pz)
        pass_y(index + 5, pz)
    arrive(planes.at[color0, 0:half_x, y, order[6]], "z4", 0)
    arrive(planes.at[color0, half_x:X, y, order[6]], "z4", 1)
    pass_y(7, order[6])
    for px in ring(x, X):
        slab = planes.at[color1, px, y]
        arrive(slab, "x1a", px)
        copies.append(start(slab, slab, "d1a", px, sibling, dp))

    late = []

    def hop(group, src, dst, name, section):
        late.append((group, src, sent[0]))
        start(src, dst, name, 0, section, dp)

    their0, their1 = 2 - 2 * core, 3 - 2 * core
    def products(py, add, last):
        for index in range(X):
            for color in range(4):
                piece = planes[color, index, py].astype(f32).reshape(y_part, lanes).astype(bf16)
                rows_at = slice(index * y_part, (index + 1) * y_part)
                flat[rows_at, color * lanes : (color + 1) * lanes] = piece

        def wide_code(rows):
            value = jnp.zeros((R, C), f32)
            for index in range(X):
                rows_at = slice(index * y_part, (index + 1) * y_part)
                value = value + plain_dot(rows[py, index], flat[rows_at, :])
            add(tok_code, slice(0, C), value)

        pl.when(sec == 0)(lambda: wide_code(out_half))
        if last:
            @pl.when(sec == 0)
            def _():
                code_out[...] = tok_code[...].astype(bf16)
                hop("first", code_out, code_in, "code", 1)
                hop("first", active_ref, active_in, "active", 1)

        @pl.when(sec != 3)
        def _():
            add(acc, slice(K + C, K + C + K), left_dot(flat[...], up_half[py]))

        pl.when(sec == 3)(lambda: wide_code(tok_half))

        @pl.when(sec != 0)
        def _():
            add(acc, slice(0, K), left_dot(flat[...], gdown_half[py]))
            add(acc, slice(K, K + C), left_dot(flat[...], flat[...]))

    def put(ref, columns, value):
        ref[:, columns] = value

    def add_to(ref, columns, value):
        ref[:, columns] += value

    for pz in [z] + order:
        arrive(planes.at[their0, :, y, pz], "d0", pz)
    arrive(planes.at[their1, x, y], "d1a", x)
    for px in ring(x, X):
        arrive(planes.at[their1, px, y], "d1a", px)
    products(y, put, False)

    for pz in [z] + order:
        block = planes.at[color0, :, other_y, pz]
        arrive(block, "y0", pz)
        copies.append(start(block, block, "d0z", pz, sibling, dp))
    for px in ring(x, X):
        slab = planes.at[color1, px, other_y]
        arrive(slab, "x1b", px)
        copies.append(start(slab, slab, "d1b", px, sibling, dp))

    for pz in [z] + order:
        arrive(planes.at[their0, :, other_y, pz], "d0z", pz)
    arrive(planes.at[their1, x, other_y], "d1b", x)
    for px in ring(x, X):
        arrive(planes.at[their1, px, other_y], "d1b", px)

    products(other_y, add_to, True)

    @pl.when(sec != 3)
    def _():
        weights[:, K + C :] = acc[:, K + C :].astype(bf16)

    @pl.when(sec != 0)
    def _():
        weights[:, 0 : K + C] = acc[:, 0 : K + C].astype(bf16)

    XY = X * Y
    def forward(code, weight):
        grid = plain_dot(code, weights[:, K : K + C])
        square = jnp.sum(code.astype(f32) * grid, axis=-1, keepdims=True) * (ratio * ratio / D)
        inverse = lax.rsqrt(jnp.maximum(square, 0.0) + epsilon)
        latent = ratio * inverse * plain_dot(code, weight)
        active = (latent * sigmoid(latent)).astype(bf16)
        return grid, inverse, latent, active

    def backward(inner, grid, inverse, latent, d_latent, weight):
        share = jnp.sum(d_latent.astype(f32) * latent, axis=-1, keepdims=True)
        share = share * inverse * inverse * (ratio / D)
        through = right_dot(d_latent, weight)
        return (ratio * (inner + inverse * through - share * grid)).astype(bf16)

    def next_code(grid, active):
        return (ratio * grid + right_dot(active, weights[:, K + C :])).astype(bf16)

    def scale_latent(d_latent, inverse):
        return (d_latent.astype(f32) * (ratio * inverse)).astype(bf16)

    def send_factor(name):
        for pxy in [xy] + xy_ring:
            late.append((name, factor, sent[0]))
            start(factor, factor_in.at[xy], "factor", xy, sibling, pxy * Z + z)

    far_x = sorted(range(X), key=lambda off: -min(off, X - off))
    xy_far = [(lax.rem(x + off, X), other_y) for off in far_x]
    xy_far += [(lax.rem(x + off, X), y) for off in far_x[:-1]]
    xy_peers = [(px * Y + py, place(px, py, z)) for px, py in xy_far]
    z_peers = [(pz, place(x, y, pz)) for pz in near_first(z, Z)[::-1]]
    pending_rest, pending_ends, pending_back, first_slot = [], [], [], {}

    def spread(ref_of, landings, name, mine, peers, pending):
        if name not in first_slot:
            first_slot[name] = sent[0]
            sent[0] += len(peers)
            pending.extend((landings, first_slot[name] + n) for n in range(len(peers)))
        for n, (peer, peer_dp) in enumerate(peers):
            start(
                ref_of(peer), landings.at[mine], name, mine, sec, peer_dp, first_slot[name] + n
            )

    def gathered(first, landing, name, peers):
        value = first.astype(f32)
        for peer, _ in peers:
            arrive(landing.at[peer], name, peer)
            value = value + landing[peer].astype(f32)
        return value

    @pl.when(sec == 0)
    def _():
        latent_ref[...] = slope_ref[...] * inv_ref[...]
        hop("first", weights.at[:, K + C :], lead_weight, "lead_weight", 1)
        hop("first", latent_ref, lead_slope, "lead_slope", 1)
        scale()

    @pl.when(sec == 3)
    def _():
        hop("last", weights.at[:, 0:K], lead_weight, "lead_weight", 2)
        hop("last", latent_ref, lead_slope, "lead_slope", 2)
        hop("last", tok_code, lead_code, "lead_code", 2)
        arrive(code_in, "code", 0)
        arrive(scaled, "scaled", 0)
        down_part[...] = left_dot(code_in[...], scaled[...]).astype(bf16).reshape(down_part.shape)
        spread(lambda peer: down_part.at[peer], down_in, "down_a", z, z_peers, pending_rest)
        arrive(active_in, "active", 0)
        arrive(back_in, "back", 0)
        up_part[...] = left_dot(back_in[...], active_in[...]).astype(bf16).reshape(up_part.shape)
        spread(lambda peer: up_part.at[peer], up_parts, "up_a", xy, xy_peers, pending_rest)

    @pl.when(sec == 1)
    def _():
        arrive(code_in, "code", 0)
        grid, inverse, latent, active = forward(code_in[...], weights[:, 0:K])
        code_out[...] = next_code(grid, active)
        hop("second", code_out, code_in, "code", 2)
        active_ref[...] = active
        hop("second", active_ref, active_in, "active", 2)
        slope = silu_slope(latent)
        arrive(lead_weight, "lead_weight", 0)
        arrive(lead_slope, "lead_slope", 0)
        arrive(active_in, "active", 0)
        arrive(back_in, "back", 0)
        both = plain_dot(back_in[...], weights[:, K:])
        d_latent = (both[:, C:] * slope).astype(bf16)
        back = backward(both[:, 0:C], grid, inverse, latent, d_latent, weights[:, 0:K])
        up_part[...] = left_dot(back, active_in[...]).astype(bf16).reshape(up_part.shape)
        spread(lambda peer: up_part.at[peer], up_parts, "up_a", xy, xy_peers, pending_rest)
        down = left_dot(code_in[...], scale_latent(d_latent, inverse))
        down_part[...] = down.astype(bf16).reshape(down_part.shape)
        spread(lambda peer: down_part.at[peer], down_in, "down_a", z, z_peers, pending_rest)
        factor[...] = (plain_dot(back, lead_weight[...]) * lead_slope[...]).astype(bf16)

    @pl.when(sec == 2)
    def _():
        arrive(code_in, "code", 0)
        grid, inverse, latent, active = forward(code_in[...], weights[:, 0:K])
        code = next_code(grid, active)
        code_out[...] = code
        hop("third", code_out, code_in, "code", 3)
        active_ref[...] = active
        hop("third", active_ref, active_in, "active", 3)
        arrive(lead_weight, "lead_weight", 0)
        arrive(lead_slope, "lead_slope", 0)
        arrive(lead_code, "lead_code", 0)
        last_grid, last_inverse, last_latent, last_active = forward(code, lead_weight[...])
        last = (lead_slope[...] * silu_slope(last_latent)).astype(bf16)
        scaled_out[...] = scale_latent(last, last_inverse)
        hop("third", scaled_out, scaled, "scaled", 3)
        turn = backward(
            lead_code[...], last_grid, last_inverse, last_latent, last, lead_weight[...]
        )
        both = plain_dot(turn, weights[:, K:])
        d_latent = (both[:, C:] * silu_slope(latent)).astype(bf16)
        back = backward(both[:, 0:C], grid, inverse, latent, d_latent, weights[:, 0:K])
        back_out[...] = back
        hop("third", back_out, back_in, "back", 1)
        turn_out[...] = turn
        hop("third", turn_out, back_in, "back", 3)
        factor[...] = last_active
        arrive(active_in, "active", 0)
        up_part[...] = left_dot(back, active_in[...]).astype(bf16).reshape(up_part.shape)
        spread(lambda peer: up_part.at[peer], up_parts, "up_a", xy, xy_peers, pending_rest)
        down = left_dot(code_in[...], scale_latent(d_latent, inverse))
        down_part[...] = down.astype(bf16).reshape(down_part.shape)
        spread(lambda peer: down_part.at[peer], down_in, "down_a", z, z_peers, pending_rest)

    rest = sec != 0
    back_half = sec >= 2
    load_codec.wait()

    @pl.when(rest)
    def _():
        up_line[...] = gathered(up_part[xy], up_parts, "up_a", xy_peers).astype(bf16)
        spread(lambda peer: up_line, up_lines, "up_b", z, z_peers, pending_rest)

    @pl.when(jnp.logical_not(ends))
    def _():
        send_factor("lead")

    @pl.when(ends)
    def _():
        arrive(factor_in.at[xy], "factor", xy)
        value = left_dot(tok_half[y, x], factor_in[xy])
        for pxy, _ in xy_peers:
            arrive(wide_in.at[pxy], "wide", pxy)
            arrive(factor_in.at[pxy], "factor", pxy)
            value = value + left_dot(wide_in[pxy], factor_in[pxy])
        wide_part[...] = value.reshape(Z, own, K).astype(bf16)
        spread(lambda peer: wide_part.at[peer], wide_parts, "big", z, z_peers, pending_ends)

    @pl.when(rest)
    def _():
        down_block[...] = gathered(down_part[z], down_in, "down_a", z_peers).astype(bf16)
        spread(lambda peer: down_block, down_blocks, "down_b", xy, xy_peers, pending_rest)
        up_sum[xy] = gathered(up_line[...], up_lines, "up_b", z_peers).astype(bf16)

        @pl.when(sec == 1)
        def _():
            for pxy in [xy] + xy_ring:
                late.append(("second", up_line, sent[0]))
                start(up_sum.at[xy], up_sum.at[xy], "up_c", xy, sibling, pxy * Z + z)

        @pl.when(back_half)
        def _():
            spread(lambda peer: up_sum.at[xy], up_sum, "up_c", xy, xy_peers, pending_back)

        down_sum[z] = gathered(down_block[...], down_blocks, "down_b", xy_peers).astype(bf16)
        spread(lambda peer: down_sum.at[z], down_sum, "down_c", z, z_peers, pending_rest)

    @pl.when(back_half)
    def _():
        for pxy, _ in xy_peers:
            arrive(up_sum.at[pxy], "up_c", pxy)
        up_result[...] = plain_dot(codec[...], up_sum[...].reshape(C, K))
        hop("back_half", up_result, up_results, "up", sec - 1)

    own_rows = pl.ds(pl.multiple_of(dp * own, 8), own)

    def put_down(value):
        column = gain_col[own_rows, :]
        weighted = down32[own_rows, :] * value
        folded = weighted[:, 0 : min(step, K)]
        for k in range(step, K, step):
            folded = folded + weighted[:, k : k + step]
        if own < step:
            folded = jnp.concatenate([folded, jnp.zeros((step - own, folded.shape[1]), f32)], axis=0)
        out_gain[...] = jnp.sum(folded.T, axis=0, keepdims=True)[:, 0:own]
        for k in range(0, K, step):
            out_down[:, k : k + step] = value[:, k : k + step] * column[:, : min(step, K)]

    @pl.when(ends)
    def _():
        wide_sum[...] = gathered(wide_part[z], wide_parts, "big", z_peers)

    @pl.when(rest)
    def _():
        for pz, _ in z_peers:
            arrive(down_sum.at[pz], "down_c", pz)
        put_down(plain_dot(codec[...], down_sum[...].reshape(C, K)))

    @pl.when(sec == 0)
    def _():
        put_down(wide_sum[...])

    @pl.when(sec == 3)
    def _():
        out_up[...] = wide_sum[...]

    @pl.when(sec == 0)
    def _():
        for pxy in [xy] + xy_ring:
            arrive(up_sum.at[pxy], "up_c", pxy)
        out_up[...] = plain_dot(codec[...], up_sum[...].reshape(C, K))

    @pl.when(jnp.logical_not(ends))
    def _():
        arrive(up_results, "up", 0)
        out_up[...] = up_results[...]

    @pl.when(rest)
    def _():
        for landing, slot in pending_rest:
            left(landing.at[0], slot)

    @pl.when(ends)
    def _():
        for landing, slot in pending_ends:
            left(landing.at[0], slot)
        for off in range(XY - 1):
            left(wide_in.at[0], wide_slot + off)

    @pl.when(back_half)
    def _():
        for landing, slot in pending_back:
            left(landing.at[0], slot)

    groups = [("back_half", back_half), ("first", sec == 0), ("second", sec == 1), ("third", sec == 2), ("last", sec == 3)]
    groups += [("rest", rest), ("lead", jnp.logical_not(ends))]
    for group, chosen in groups:
        @pl.when(chosen)
        def _():
            for which, src, slot in late:
                if which == group:
                    left(src, slot)

    for copy in copies:
        copy.wait_send()


def hand_out(down, up, gain, out_down, out_up, out_gain, sem):
    copies = [
        pltpu.make_async_copy(down, out_down, sem.at[0]),
        pltpu.make_async_copy(up, out_up, sem.at[1]),
        pltpu.make_async_copy(gain, out_gain, sem.at[2]),
    ]
    for copy in copies:
        copy.start()
    for copy in copies:
        copy.wait()


def on_device(hidden_in, head_grad, down_w, up_w, norm_gain, codec):
    micro, rows, D = hidden_in.shape
    K, C, own = down_w.shape[3], codec.shape[1], codec.shape[0]
    Y, Z = y_size, z_size
    X = lax.axis_size("dp") // (Y * Z)
    R, chunk, lanes = micro * rows, D // X, C // 4
    block_rows = C // (X * Y)
    any_space = pl.BlockSpec(memory_space=pl.ANY)
    vmem = pl.BlockSpec(memory_space=pltpu.VMEM)
    recv_count = 5 * X + 9 * Z + 13 + 5 * X * Y
    scratch = [
        ((micro, rows, D), bf16),
        ((1, D), f32),
        ((own, C), bf16),
        ((D, K), bf16),
        ((Y, D // Y, K), bf16),
        ((D, K), f32),
        ((D, 128), f32),
        ((Y, D // Y, K), bf16),
        ((4, X, Y, Z, own, lanes), bf16),
        ((D // Y, C), bf16),
        ((Y, X, R, chunk // Y), bf16),
        ((Y, X, R, chunk // Y), bf16),
        ((C, 2 * K + C), f32),
        ((C, 2 * K + C), bf16),
        ((R, C), f32),
        ((R, K), f32),
        ((R, K), bf16),
        ((R, 1), f32),
        ((R, K), f32),
        ((R, C), bf16),
        ((R, C), bf16),
        ((R, C), bf16),
        ((R, C), bf16),
        ((R, C), bf16),
        ((R, K), bf16),
        ((R, K), bf16),
        ((C, K), bf16),
        ((R, K), f32),
        ((R, C), f32),
        ((R, K), bf16),
        ((X * Y, R, chunk // Y), bf16),
        ((R, K), bf16),
        ((X * Y, R, K), bf16),
        ((Z, own, K), bf16),
        ((Z, own, K), bf16),
        ((own, K), f32),
        ((Z, C // Z, K), bf16),
        ((Z, C // Z, K), bf16),
        ((C // Z, K), bf16),
        ((X * Y, C // Z, K), bf16),
        ((Z, C // Z, K), bf16),
        ((X * Y, block_rows, K), bf16),
        ((X * Y, block_rows, K), bf16),
        ((block_rows, K), bf16),
        ((Z, block_rows, K), bf16),
        ((X * Y, block_rows, K), bf16),
        ((own, K), f32),
        ((own, K), f32),
    ]
    sum_down, sum_up, sum_gain = pl.pallas_call(
        functools.partial(kernel, (X, Y, Z)),
        out_shape=(
            jax.ShapeDtypeStruct((own, K), f32),
            jax.ShapeDtypeStruct((own, K), f32),
            jax.ShapeDtypeStruct((1, own), f32),
        ),
        in_specs=[any_space] * 6,
        out_specs=(vmem, vmem, vmem),
        scratch_shapes=[pltpu.VMEM(shape, kind) for shape, kind in scratch]
        + [
            pltpu.SemaphoreType.DMA((21,)),
            pltpu.SemaphoreType.DMA((160,)),
            pltpu.SemaphoreType.DMA((recv_count,)),
        ],
        compiler_params=pltpu.CompilerParams(
            collective_id=0, has_side_effects=True, vmem_limit_bytes=56 * 1024 * 1024
        ),
    )(hidden_in, head_grad, down_w[0, 0], up_w[0, 0], norm_gain[0], codec)
    sum_down, sum_up, sum_gain = pl.pallas_call(
        hand_out,
        out_shape=(
            jax.ShapeDtypeStruct((own, K), f32),
            jax.ShapeDtypeStruct((own, K), f32),
            jax.ShapeDtypeStruct((1, own), f32),
        ),
        in_specs=[any_space] * 3,
        out_specs=(any_space,) * 3,
        scratch_shapes=[pltpu.SemaphoreType.DMA((3,))],
    )(sum_down, sum_up, sum_gain)
    return (sum_down[None, None], sum_up[None, None], sum_gain[None])


def solution(mesh):
    in_specs = (
        P(None, "dp", None),
        P(None, "dp", None),
        P("section", None, None, None),
        P("section", None, None, None),
        P("section", None, None),
        P("dp", None),
    )
    out_specs = (
        P("section", None, "dp", None),
        P("section", None, "dp", None),
        P("section", None, "dp"),
    )
    return jax.shard_map(
        on_device, mesh=mesh, in_specs=in_specs, out_specs=out_specs, check_vma=False
    )
```
